128 devices in a mesh: ctx: 16 (over x, y), fsdp: 8 (over z, core).
Axes of the slice: x: 4, y: 4, z: 4, core: 2. Of those that a mesh axis runs over, the one named last changes fastest.
Arguments:
- inputs: bfloat16 [16, 1024, 1024], P('fsdp', 'ctx'), may hold values from -6 to 6
- gain_attn: bfloat16 [1024], P('fsdp'), may hold values from 0.5 to 1.5
- w_query: bfloat16 [1024, 1024], P('fsdp'), may hold values from -0.1875 to 0.1875
- w_key: bfloat16 [1024, 1024], P('fsdp'), may hold values from -0.1875 to 0.1875
- w_value: bfloat16 [1024, 1024], P('fsdp'), may hold values from -0.1875 to 0.1875
- w_out: bfloat16 [1024, 1024], P('fsdp'), may hold values from -1.5 to 1.5
- persist_key: bfloat16 [16, 1024], P(None, 'fsdp'), may hold values from -6 to 6
- persist_value: bfloat16 [16, 1024], P(None, 'fsdp'), may hold values from -6 to 6
- gain_ffn: bfloat16 [1024], P('fsdp'), may hold values from 0.5 to 1.5
- w_gate: bfloat16 [1024, 2816], P('fsdp'), may hold values from -0.1875 to 0.1875
- w_up: bfloat16 [1024, 2816], P('fsdp'), may hold values from -0.1875 to 0.1875
- w_down: bfloat16 [2816, 1024], P('fsdp'), may hold values from -0.109375 to 0.109375
- decay_table: bfloat16 [16, 8], P('fsdp'), may hold values from -1 to 7
- momentum_table: bfloat16 [16, 8], P('fsdp'), may hold values from -2 to 3
- lengths: int32 [16], P('fsdp'), may hold values from 256 to 1024, as said below
- decay_index: int32 [16, 16], P('fsdp', 'ctx'), may hold values from 0 to 15
- momentum_index: int32 [16, 16], P('fsdp', 'ctx'), may hold values from 0 to 15
- cotangent: bfloat16 [16, 1024, 1024], P('fsdp', 'ctx'), may hold values from -6 to 6
Outputs:
- output: bfloat16 [16, 1024, 1024], P('fsdp', 'ctx')
- input_grad: float32 [16, 1024, 1024], P('fsdp', 'ctx')
- grad_gain_attn: float32 [1024], P('fsdp')
- grad_query: float32 [1024, 1024], P('fsdp')
- grad_key: float32 [1024, 1024], P('fsdp')
- grad_value: float32 [1024, 1024], P('fsdp')
- grad_out: float32 [1024, 1024], P('fsdp')
- grad_persist_key: float32 [16, 1024], P(None, 'fsdp')
- grad_persist_value: float32 [16, 1024], P(None, 'fsdp')
- grad_gain_ffn: float32 [1024], P('fsdp')
- grad_gate: float32 [1024, 2816], P('fsdp')
- grad_up: float32 [1024, 2816], P('fsdp')
- grad_down: float32 [2816, 1024], P('fsdp')
- grad_decay_table: float32 [16, 8], P('fsdp')
- grad_momentum_table: float32 [16, 8], P('fsdp')
The draws below stay inside these ranges and needn't reach their ends.
Inputs may be any that keep to these rules, and one draw needn't show every extreme that they name: `lengths`: among the 2 sequences of each index of fsdp, one has exactly 1024 live positions.
All inputs are finite; a program needn't handle non-finite values.
Results may differ from the reference program's by a relative error of at most 0.025.
Values may be sent and summed in bfloat16 or wider, within the bound.
A program may use at most 192 MiB of HBM per device.

```python
import jax
import jax.numpy as jnp
from jax import lax

D = 1024
H = 8
DH = 128
FF = 2816
PERS = 16
SEG = 1024
BLOCK = 64
LEVELS = 16
SEQ_DEV = 2
LENGTH = 1024
BATCH = 16
NBLOCK = 16


def draw_lengths(key, part):
    key = jax.random.fold_in(key, 7)
    pick_key, length_key = jax.random.split(key)
    groups = BATCH // SEQ_DEV
    drawn = jax.random.randint(length_key, (groups, SEQ_DEV), LENGTH // 4, LENGTH + 1)
    chosen = jax.random.randint(pick_key, (groups, 1), 0, SEQ_DEV)
    places = jnp.arange(SEQ_DEV)[None, :]
    return jnp.where(places == chosen, LENGTH, drawn).reshape(BATCH).astype(jnp.int32)


def place_ends(entries, key, least, high):
    dims = entries.shape
    place = [jax.random.randint(jax.random.fold_in(key, axis), (), 0, dims[axis]) for axis in range(len(dims))]
    entries = entries.at[tuple(place)].set(least)
    longest = dims.index(max(dims))
    place[longest] = (place[longest] + 1) % dims[longest]
    return entries.at[tuple(place)].set(high)


def block_scale(stream_key, dims, pieces, least, largest):
    loudness = 1.0
    for axis_at, blocks in pieces:
        draws = jax.random.uniform(jax.random.fold_in(jax.random.fold_in(stream_key, 6), axis_at), (blocks,), jnp.float32, least / len(pieces), largest / len(pieces))
        loudness = loudness * jnp.repeat(jnp.exp(draws), dims[axis_at] // blocks).reshape((-1,) + (1,) * (len(dims) - 1 - axis_at))
    return loudness


def noise(stream_key, extent, spread, bound, cuts=(), kind=jnp.bfloat16):
    entries = spread * jax.random.normal(stream_key, extent, jnp.float32)
    if cuts:
        entries = entries * block_scale(stream_key, extent, cuts, -0.22, 0.18)
    return jnp.clip(entries, -bound, bound).astype(kind)


def setup_inputs(seed: int = 0) -> dict:
    streams_of = jax.random.split(jax.random.key(seed), 19)
    return {
        "inputs": noise(streams_of[0], (BATCH, LENGTH, D), 1.0, 6.0, ((0, 8), (1, 16))),
        "gain_attn": jnp.clip(1.0 + 0.1 * jax.random.normal(streams_of[1], (D,), jnp.float32), 0.5, 1.5).astype(jnp.bfloat16),
        "w_query": noise(streams_of[2], (D, D), D ** -0.5, 0.1875, ((0, 8),)),
        "w_key": noise(streams_of[3], (D, D), D ** -0.5, 0.1875, ((0, 8),)),
        "w_value": noise(streams_of[4], (D, D), D ** -0.5, 0.1875, ((0, 8),)),
        "w_out": noise(streams_of[5], (D, D), (D // 64) ** -0.5, 1.5, ((0, 8),)),
        "persist_key": noise(streams_of[6], (PERS, D), 1.0, 6.0, ((1, 8),)),
        "persist_value": noise(streams_of[7], (PERS, D), 1.0, 6.0, ((1, 8),)),
        "gain_ffn": jnp.clip(1.0 + 0.1 * jax.random.normal(streams_of[8], (D,), jnp.float32), 0.5, 1.5).astype(jnp.bfloat16),
        "w_gate": noise(streams_of[9], (D, FF), D ** -0.5, 0.1875, ((0, 8),)),
        "w_up": noise(streams_of[10], (D, FF), D ** -0.5, 0.1875, ((0, 8),)),
        "w_down": noise(streams_of[11], (FF, D), FF ** -0.5, 0.109375, ((0, 8),)),
        "decay_table": jnp.clip(-1.0 + 8.0 * jax.random.uniform(streams_of[12], (LEVELS, H), jnp.float32) ** block_scale(streams_of[12], (LEVELS, H), ((0, 8),), -0.2, 0.2), -1.0, 7.0).astype(jnp.bfloat16),
        "momentum_table": jnp.clip(-2.0 + 5.0 * jax.random.uniform(streams_of[13], (LEVELS, H), jnp.float32) ** block_scale(streams_of[13], (LEVELS, H), ((0, 8),), -0.2, 0.2), -2.0, 3.0).astype(jnp.bfloat16),
        "lengths": draw_lengths(jax.random.fold_in(streams_of[18], 71), 0),
        "decay_index": place_ends(jax.random.randint(streams_of[15], (BATCH, NBLOCK), 0, LEVELS), jax.random.fold_in(streams_of[15], 1), 0, LEVELS - 1).astype(jnp.int32),
        "momentum_index": place_ends(jax.random.randint(streams_of[16], (BATCH, NBLOCK), 0, LEVELS), jax.random.fold_in(streams_of[16], 1), 0, LEVELS - 1).astype(jnp.int32),
        "cotangent": noise(streams_of[17], (BATCH, LENGTH, D), 1.0, 6.0, ((0, 8), (1, 16))),
    }


@jax.custom_vjp
def low(v):
    return lax.optimization_barrier(v.astype(jnp.bfloat16)).astype(jnp.float32)

@jax.custom_vjp
def low_back(v):
    return v

def low_keep(v):
    return (low(v), None)

def low_pass(kept, grad):
    return (grad,)

def back_keep(v):
    return (v, None)

def back_low(kept, grad):
    return (low(grad),)
low.defvjp(low_keep, low_pass)
low_back.defvjp(back_keep, back_low)
step_rate = 0.1

def product(left_side, right_side):
    return jnp.dot(left_side, right_side, precision=lax.Precision.HIGHEST, preferred_element_type=jnp.float32)

def scaled_rows(values, gain_row):
    return values * lax.rsqrt(lax.optimization_barrier(jnp.mean(values * values, axis=-1, keepdims=True)) + 1e-06) * gain_row

def unit_heads(values):
    return values * lax.rsqrt(lax.optimization_barrier(jnp.mean(values * values, axis=-1, keepdims=True)) + 1e-06) * values.shape[-1] ** (-0.5)

def segment_attention(queries, key_rows, values, persist_keys, persist_values, live_rows):
    all_keys = jnp.concatenate([persist_keys, key_rows], axis=0)
    all_values = jnp.concatenate([persist_values, values], axis=0)
    scores = jnp.einsum('qhd,khd->hqk', queries, all_keys, precision=lax.Precision.HIGHEST) * DH ** (-0.5)
    scores = low_back(scores)
    places = jnp.arange(SEG)
    allowed = (places[None, :] <= places[:, None]) & (live_rows[None, :] > 0.5)
    allowed = jnp.concatenate([jnp.ones((SEG, PERS), dtype=jnp.bool_), allowed], axis=1)
    scores = jnp.where(allowed[None], scores, -1e+30)
    attn_probs = low(jax.nn.softmax(scores, axis=-1))
    return jnp.einsum('hqk,khd->qhd', attn_probs, all_values, precision=lax.Precision.HIGHEST)

def memory_reads(query_units, key_units, values, retention, momentum):

    def block_step(state_pair, block_rows):
        memory, velocity = state_pair
        block_query, block_key, block_value, block_retention, block_momentum = block_rows
        read_rows = jnp.einsum('thk,hkl->thl', block_query, memory, precision=lax.Precision.HIGHEST)
        outer_keys = jnp.einsum('thk,thl->hkl', block_key, block_key, precision=lax.Precision.HIGHEST)
        outer_values = jnp.einsum('thk,thl->hkl', block_key, block_value, precision=lax.Precision.HIGHEST)
        surprise = jnp.einsum('hkj,hjl->hkl', outer_keys, memory, precision=lax.Precision.HIGHEST) - outer_values
        velocity = block_momentum[:, None, None] * velocity - step_rate * surprise
        memory = block_retention[:, None, None] * memory + velocity
        return ((memory, velocity), read_rows)
    zero_state = jnp.zeros((H, DH, DH), jnp.float32)
    _, read_rows = lax.scan(jax.checkpoint(block_step), (zero_state, zero_state), (query_units, key_units, values, retention, momentum))
    return read_rows

def layer(seq_in, weights, live_rows, decay_slots, momentum_slots):
    gain_attn, w_query, w_key, w_value, w_out, persist_key, persist_value, gain_ffn, w_gate, w_up, w_down, decay_table, momentum_table = weights
    normed = low(scaled_rows(seq_in, gain_attn))
    queries = low_back(low(product(normed, w_query))).reshape(LENGTH, H, DH)
    key_rows = low_back(low(product(normed, w_key))).reshape(LENGTH, H, DH)
    values = low_back(low(product(normed, w_value))).reshape(LENGTH, H, DH)
    segments = LENGTH // SEG
    persist_keys = persist_key.reshape(PERS, H, DH)
    persist_values = persist_value.reshape(PERS, H, DH)

    def one_segment(segment_rows):
        return segment_attention(segment_rows[0], segment_rows[1], segment_rows[2], persist_keys, persist_values, segment_rows[3])
    attended = lax.map(jax.checkpoint(one_segment), (queries.reshape(segments, SEG, H, DH), key_rows.reshape(segments, SEG, H, DH), values.reshape(segments, SEG, H, DH), live_rows.reshape(segments, SEG)))
    attended = low_back(attended.reshape(LENGTH, H, DH))
    retention = jax.nn.sigmoid(decay_table[decay_slots])
    momentum = jax.nn.sigmoid(momentum_table[momentum_slots])
    block_count = LENGTH // BLOCK
    query_units = unit_heads(queries).reshape(block_count, BLOCK, H, DH)
    key_units = (unit_heads(key_rows) * live_rows[:, None, None]).reshape(block_count, BLOCK, H, DH)
    read_rows = memory_reads(query_units, key_units, values.reshape(block_count, BLOCK, H, DH), retention, momentum)
    mixed = low((attended + read_rows.reshape(LENGTH, H, DH)).reshape(LENGTH, D))
    resid = seq_in + low_back(product(mixed, w_out))
    normed_ffn = low(scaled_rows(resid, gain_ffn))
    gate_proj = low_back(product(normed_ffn, w_gate))
    up_proj = low_back(product(normed_ffn, w_up))
    hidden = low(jax.nn.silu(gate_proj) * up_proj)
    return resid + low_back(product(hidden, w_down))

def reference(inputs, gain_attn, w_query, w_key, w_value, w_out, persist_key, persist_value, gain_ffn, w_gate, w_up, w_down, decay_table, momentum_table, lengths, decay_index, momentum_index, cotangent):
    weights = tuple((w.astype(jnp.float32) for w in (gain_attn, w_query, w_key, w_value, w_out, persist_key, persist_value, gain_ffn, w_gate, w_up, w_down, decay_table, momentum_table)))

    def per_sequence(totals, sequence_item):
        seq_in, seq_cot, seq_len, decay_slots, momentum_slots = sequence_item
        live_rows = (jnp.arange(LENGTH) < seq_len).astype(jnp.float32)

        def forward(seq_rows, weight_set):
            return layer(seq_rows, weight_set, live_rows, decay_slots, momentum_slots)
        result, pullback = jax.vjp(forward, seq_in.astype(jnp.float32), weights)
        grad_in, grad_weights = pullback(seq_cot.astype(jnp.float32) * live_rows[:, None])
        totals = tuple((first + second for first, second in zip(totals, grad_weights)))
        return (totals, (result.astype(jnp.bfloat16), grad_in))
    zero_grads = tuple((jnp.zeros_like(w) for w in weights))
    totals, (outputs, grads_in) = lax.scan(per_sequence, zero_grads, (inputs, cotangent, lengths, decay_index, momentum_index))
    return (outputs, grads_in, totals[0], totals[1], totals[2], totals[3], totals[4], totals[5], totals[6], totals[7], totals[8], totals[9], totals[10], totals[11], totals[12])
```

```python
import functools

import jax
import jax.numpy as jnp
from jax import lax
from jax.experimental import pallas as pl
from jax.experimental.pallas import tpu as pltpu
from jax.sharding import PartitionSpec as P

MESH = pl.DeviceIdType.MESH
HIGHEST = lax.Precision.HIGHEST
bf16, f32 = jnp.bfloat16, jnp.float32
EPS = 1e-06
RATE = 0.1
SCALE = 128**-0.5
VMEM_LIMIT = 60 << 20


def coords():
    c, f = lax.axis_index("ctx"), lax.axis_index("fsdp")
    return c, lax.div(f, 2), lax.rem(f, 2)


def pair_of(c):
    return lax.div(c, 8), lax.rem(lax.div(c, 2), 4), lax.rem(c, 2)


def at_ctx(c, dx, dy):
    x, y = lax.div(c, 4), lax.rem(c, 4)
    return lax.rem(x + dx, 4) * 4 + lax.rem(y + dy, 4)


CTX_STEPS = [(dx, dy) for dx in range(4) for dy in range(4) if dx or dy]
CTX_STEPS.sort(key=lambda s: -(min(s[0], 4 - s[0]) + min(s[1], 4 - s[1])))


def device(c, z, k):
    return (c, 2 * z + k)


def nn(a, b, precision=None):
    return jnp.dot(a, b, preferred_element_type=f32, precision=precision)


def nt(a, b, precision=None):
    return lax.dot_general(
        a, b, (((1,), (1,)), ((), ())), preferred_element_type=f32, precision=precision
    )


def tn(a, b, precision=None):
    return lax.dot_general(
        a, b, (((0,), (0,)), ((), ())), preferred_element_type=f32, precision=precision
    )


def meet(peers):
    barrier = pltpu.get_barrier_semaphore()
    for peer in peers:
        pl.semaphore_signal(barrier, inc=1, device_id=peer, device_id_type=MESH)
    pl.semaphore_wait(barrier, len(peers))


def z_peers(c, z, k):
    return [device(c, lax.rem(z + d, 4), k) for d in range(1, 4)]


def remote(src, dst, ssem, rsem, peer):
    return pltpu.make_async_remote_copy(
        src_ref=src, dst_ref=dst, send_sem=ssem, recv_sem=rsem, device_id=peer, device_id_type=MESH
    )


def comm_call(body, name, cid, out_shapes, sems, *operands):
    return pl.pallas_call(
        body,
        out_shape=out_shapes,
        in_specs=[pl.BlockSpec(memory_space=pl.ANY)] * len(operands),
        out_specs=jax.tree.map(lambda _: pl.BlockSpec(memory_space=pl.ANY), out_shapes),
        scratch_shapes=[
            pltpu.SemaphoreType.DMA((sems,)),
            pltpu.SemaphoreType.DMA((sems,)),
            pltpu.SemaphoreType.DMA((sems,)),
        ],
        compiler_params=pltpu.CompilerParams(collective_id=cid, has_side_effects=True),
        name=name,
    )(*operands)


def like(*shapes, dtype=bf16):
    return [jax.ShapeDtypeStruct(s, dtype) for s in shapes]


def front_kernel(
    x, cot, meta, wq, wk, wv, wo, wg, wu, wd, pers,
    x_all, cot_all, meta_all, wq_all, wk_all, wv_all, wo_all, wg_all, wu_all, wd_all, pers_all,
    ssem, rsem, lsem,
):
    c, z, k = coords()
    f = 2 * z + k
    sibling = device(c, z, 1 - k)
    meet(z_peers(c, z, k) + [sibling])

    def quarter(ref):
        return lambda zz: ref.at[:, pl.ds(pl.multiple_of(zz * 256, 256), 256)]

    spread = [
        (lambda zz: meta, meta_all),
        (quarter(wq), wq_all), (quarter(wk), wk_all), (quarter(wv), wv_all),
        (lambda zz: wo, wo_all),
        (lambda zz: wg.at[zz], wg_all), (lambda zz: wu.at[zz], wu_all),
    ]
    gather = [(x, x_all), (cot, cot_all)]
    sends, local = [], []

    def start(copy):
        copy.start()
        sends.append(copy)

    base = 0
    for i, (src, dst) in enumerate(gather):
        mine = pltpu.make_async_copy(src, dst.at[z], lsem.at[i])
        mine.start()
        local.append(mine)
        for d in range(1, 4):
            n = base + d - 1
            start(remote(src, dst.at[z], ssem.at[n], rsem.at[n], device(c, lax.rem(z + d, 4), k)))
        base += 3
    first = base
    for i, (src, dst) in enumerate(spread):
        mine = pltpu.make_async_copy(src(z), dst.at[f], lsem.at[2 + i])
        mine.start()
        local.append(mine)
        for d in range(1, 4):
            n = base + d - 1
            zz = lax.rem(z + d, 4)
            start(remote(src(zz), dst.at[f], ssem.at[n], rsem.at[n], device(c, zz, k)))
        start(remote(src(z), dst.at[f], ssem.at[base + 3], rsem.at[base + 3], sibling))
        base += 7
    for i, (src, dst) in enumerate([(wd, wd_all), (pers, pers_all)]):
        mine = pltpu.make_async_copy(src, dst.at[k], lsem.at[9 + i])
        mine.start()
        local.append(mine)
        start(remote(src, dst.at[k], ssem.at[base], rsem.at[base], sibling))
        base += 1
    landed = []
    for i, (src, dst) in enumerate(spread):
        b = first + 7 * i
        for d in range(1, 4):
            n = b + 3 + d
            slot = dst.at[2 * lax.rem(z - d + 4, 4) + k]
            remote(slot, slot, ssem.at[b + d - 1], rsem.at[b + d - 1], sibling).wait_recv()
            start(remote(slot, slot, ssem.at[n], rsem.at[n], sibling))
            landed.append((slot, n))
        landed.append((dst.at[f], b + 3))
    for i, (src, dst) in enumerate(gather):
        for d in range(1, 4):
            landed.append((dst.at[z], 3 * i + d - 1))
    landed += [(wd_all.at[k], base - 2), (pers_all.at[k], base - 1)]
    for slot, n in landed:
        remote(slot, slot, ssem.at[n], rsem.at[n], sibling).wait_recv()
    for copy in sends:
        copy.wait_send()
    for copy in local:
        copy.wait()


def ctx_swap_kernel(n, *refs):
    srcs, dsts = refs[:n], refs[n : 2 * n]
    ssem, rsem, lsem = refs[2 * n :]
    c, z, k = coords()
    steps = [(at_ctx(c, dx, dy)) for dx, dy in CTX_STEPS]
    meet([device(cc, z, k) for cc in steps])
    sends, local = [], []
    for i, (src, dst) in enumerate(zip(srcs, dsts)):
        mine = pltpu.make_async_copy(src.at[c], dst.at[c], lsem.at[i])
        mine.start()
        local.append(mine)
    for j, cc in enumerate(steps):
        for i, (src, dst) in enumerate(zip(srcs, dsts)):
            s = j * n + i
            copy = remote(src.at[cc], dst.at[c], ssem.at[s], rsem.at[s], device(cc, z, k))
            copy.start()
            sends.append(copy)
    for copy in sends:
        copy.wait()
    for copy in local:
        copy.wait()


def ctx_swap(cid, name, *operands):
    n = len(operands)
    return comm_call(
        functools.partial(ctx_swap_kernel, n), name, cid, like(*[o.shape for o in operands]), 15 * n, *operands
    )


def z_swap_kernel(n, gather, *refs):
    srcs, dsts = refs[:n], refs[n : 2 * n]
    ssem, rsem, lsem = refs[2 * n :]
    c, z, k = coords()
    meet(z_peers(c, z, k))
    sends, local = [], []
    for i, (src, dst) in enumerate(zip(srcs, dsts)):
        mine = pltpu.make_async_copy(src if gather else src.at[z], dst.at[z], lsem.at[i])
        mine.start()
        local.append(mine)
        for d in range(1, 4):
            s = 3 * i + d - 1
            zz = lax.rem(z + d, 4)
            copy = remote(
                src if gather else src.at[zz], dst.at[z], ssem.at[s], rsem.at[s], device(c, zz, k)
            )
            copy.start()
            sends.append(copy)
    for copy in sends:
        copy.wait()
    for copy in local:
        copy.wait()


def z_swap(cid, name, *operands, gather=False):
    n = len(operands)
    return comm_call(
        functools.partial(z_swap_kernel, n, gather),
        name,
        cid,
        like(*[(4, *o.shape) if gather else o.shape for o in operands]),
        3 * n,
        *operands,
    )


def mixed_home_kernel(mixed, tok, quart, ssem, rsem, lsem):
    c, z, k = coords()
    hb, zs, sb = pair_of(c)
    head = 2 * z + hb
    spots = [c] + [at_ctx(c, dx, dy) for dx, dy in CTX_STEPS]
    senders = [device(hb2 * 8 + z * 2 + sb2, zz, k) for zz in range(4) for hb2 in range(2) for sb2 in range(2)]
    here = zs == z
    barrier = pltpu.get_barrier_semaphore()

    for zz in range(4):
        for hb2 in range(2):
            for sb2 in range(2):
                cc = hb2 * 8 + z * 2 + sb2

                @pl.when(jnp.logical_not((cc == c) & (zz == z)))
                def _():
                    pl.semaphore_signal(barrier, inc=1, device_id=device(cc, zz, k), device_id_type=MESH)

    for cc in spots[1:]:
        pl.semaphore_signal(barrier, inc=1, device_id=device(cc, z, k), device_id_type=MESH)
    pl.semaphore_wait(barrier, jnp.where(here, 30, 31))
    slot = head * 2 + sb

    def home(j):
        return remote(
            mixed.at[spots[j]], tok.at[slot], ssem.at[j], rsem.at[slot], device(spots[j], zs, k)
        )

    @pl.when(here)
    def _():
        pltpu.make_async_copy(mixed.at[c], tok.at[slot], rsem.at[slot]).start()

    @pl.when(jnp.logical_not(here))
    def _():
        home(0).start()

    mine = pltpu.make_async_copy(mixed.at[c], quart.at[c], lsem.at[0])
    mine.start()
    others = []
    for j in range(1, 16):
        home(j).start()
    for j in range(1, 16):
        copy = remote(
            mixed.at[spots[j]], quart.at[c], ssem.at[15 + j], rsem.at[15 + j], device(spots[j], z, k)
        )
        copy.start()
        others.append(copy)
    for n in range(16):
        remote(tok.at[n], tok.at[n], ssem.at[0], rsem.at[n], device(c, z, k)).wait_recv()
    for copy in others:
        copy.wait()

    @pl.when(jnp.logical_not(here))
    def _():
        home(0).wait_send()

    for j in range(1, 16):
        home(j).wait_send()
    mine.wait()


def mixed_home(cid, mixed):
    return comm_call(mixed_home_kernel, "mixed_home", cid, like((16, 64, 128), (16, 64, 128)), 32, mixed)


def grads_out_kernel(dmix, branch, blocks, branch_all, ssem, rsem, lsem):
    c, z, k = coords()
    hb, zs, sb = pair_of(c)
    here = zs == z
    barrier = pltpu.get_barrier_semaphore()
    spots = [c] + [at_ctx(c, dx, dy) for dx, dy in CTX_STEPS]
    for cc in spots[1:]:
        pl.semaphore_signal(barrier, inc=1, device_id=device(cc, zs, k), device_id_type=MESH)

    @pl.when(jnp.logical_not(here))
    def _():
        pl.semaphore_signal(barrier, inc=1, device_id=device(c, zs, k), device_id_type=MESH)

    for peer in z_peers(c, z, k):
        pl.semaphore_signal(barrier, inc=1, device_id=peer, device_id_type=MESH)
    pl.semaphore_wait(barrier, jnp.where(here, 18, 19))
    mine_is = [((hb2 * 8 + z * 2 + sb2) == c) for hb2 in range(2) for sb2 in range(2)]
    mine = pltpu.make_async_copy(branch, branch_all.at[z], lsem.at[0])
    mine.start()
    sends = []
    for d in range(4):
        zz = lax.rem(z + d, 4)
        for i in range(4):
            hb2, sb2 = i // 2, i % 2
            n = 4 * d + i
            src = dmix.at[(2 * zz + hb2) * 2 + sb2]
            copy = remote(
                src, blocks.at[c], ssem.at[n], rsem.at[c], device(hb2 * 8 + z * 2 + sb2, zz, k)
            )
            if d:
                copy.start()
                sends.append((None, copy))
            else:

                @pl.when(mine_is[i])
                def _():
                    pltpu.make_async_copy(src, blocks.at[c], rsem.at[c]).start()

                @pl.when(jnp.logical_not(mine_is[i]))
                def _():
                    copy.start()

                sends.append((mine_is[i], copy))
    for d in range(1, 4):
        copy = remote(
            branch, branch_all.at[z], ssem.at[15 + d], rsem.at[15 + d], device(c, lax.rem(z + d, 4), k)
        )
        copy.start()
        sends.append((None, copy))
    for n in range(16):
        remote(blocks.at[n], blocks.at[n], ssem.at[0], rsem.at[n], device(c, z, k)).wait_recv()
    for d in range(1, 4):
        remote(branch, branch_all.at[z], ssem.at[0], rsem.at[15 + d], device(c, z, k)).wait_recv()
    for local, copy in sends:
        if local is None:
            copy.wait_send()
        else:

            @pl.when(jnp.logical_not(local))
            def _():
                copy.wait_send()

    mine.wait()


def grads_out(cid, dmix, branch):
    return comm_call(
        grads_out_kernel, "grads_out", cid, like((16, 64, 128), (4, 128, 1024)), 32, dmix, branch
    )


def core_swap_kernel(n, *refs):
    srcs, dsts = refs[:n], refs[n : 2 * n]
    ssem, rsem, lsem = refs[2 * n :]
    c, z, k = coords()
    sibling = device(c, z, 1 - k)
    meet([sibling])
    sends = []
    for i, (src, dst) in enumerate(zip(srcs, dsts)):
        part = src.at[1 - k] if len(src.shape) == 3 else src.at[:, 1 - k]
        copy = remote(part, dst, ssem.at[i], rsem.at[i], sibling)
        copy.start()
        sends.append(copy)
    for copy in sends:
        copy.wait()


def core_swap(cid, name, *operands):
    n = len(operands)
    shapes = [o.shape[1:] if o.ndim == 3 else (o.shape[0], *o.shape[2:]) for o in operands]
    return comm_call(functools.partial(core_swap_kernel, n), name, cid, like(*shapes), n, *operands)


def reduce_kernel(gu, qkv, down, out, gu_in, qkv_in, down_in, out_in, ssem, rsem, lsem):
    c, z, k = coords()
    steps = [(at_ctx(c, dx, dy)) for dx, dy in CTX_STEPS]
    meet([device(cc, z, k) for cc in steps])

    def pieces(cc):
        rg, h = lax.div(cc, 2), lax.rem(cc, 2)
        rows = pl.ds(pl.multiple_of(rg * 16, 16), 16)
        return [
            (gu.at[h, :, rows, :], gu_in.at[c]),
            (qkv.at[:, rows, pl.ds(pl.multiple_of(h * 384, 384), 384)], qkv_in.at[c]),
            (
                down.at[pl.ds(pl.multiple_of(h * 176, 16), 176), pl.ds(pl.multiple_of(rg * 128, 128), 128)],
                down_in.at[c],
            ),
            (out.at[rows, pl.ds(pl.multiple_of(h * 512, 512), 512)], out_in.at[c]),
        ]

    sends, local = [], []
    for i, (src, dst) in enumerate(pieces(c)):
        mine = pltpu.make_async_copy(src, dst, lsem.at[i])
        mine.start()
        local.append(mine)
    for j, cc in enumerate(steps):
        for i, (src, dst) in enumerate(pieces(cc)):
            n = 4 * j + i
            copy = remote(src, dst, ssem.at[n], rsem.at[n], device(cc, z, k))
            copy.start()
            sends.append(copy)
    for copy in sends:
        copy.wait()
    for copy in local:
        copy.wait()


def reduce_ctx(cid, gu, qkv, down, out):
    return comm_call(
        reduce_kernel,
        "reduce_ctx",
        cid,
        like((16, 4, 16, 768), (16, 4, 16, 384), (16, 176, 128), (16, 16, 512)),
        60,
        gu, qkv, down, out,
    )


def ctx_gather_kernel(n, *refs):
    srcs, dsts = refs[:n], refs[n : 2 * n]
    ssem, rsem, lsem = refs[2 * n :]
    c, z, k = coords()
    steps = [(at_ctx(c, dx, dy)) for dx, dy in CTX_STEPS]
    meet([device(cc, z, k) for cc in steps])
    sends, local = [], []
    for i, (src, dst) in enumerate(zip(srcs, dsts)):
        mine = pltpu.make_async_copy(src, dst.at[c], lsem.at[i])
        mine.start()
        local.append(mine)
    for j, cc in enumerate(steps):
        for i, (src, dst) in enumerate(zip(srcs, dsts)):
            s = j * n + i
            copy = remote(src, dst.at[c], ssem.at[s], rsem.at[s], device(cc, z, k))
            copy.start()
            sends.append(copy)
    for copy in sends:
        copy.wait()
    for copy in local:
        copy.wait()


def ctx_gather(cid, name, *operands):
    n = len(operands)
    return comm_call(
        functools.partial(ctx_gather_kernel, n),
        name,
        cid,
        like(*[(16, *o.shape) for o in operands]),
        15 * n,
        *operands,
    )


def unit_rows(rows):
    r = lax.rsqrt(jnp.mean(rows * rows, axis=-1, keepdims=True) + EPS)
    return rows * r * SCALE, r


def unit_back(rows, r, grad):
    return SCALE * (r * grad - rows * (r * r * r) * jnp.mean(rows * grad, axis=-1, keepdims=True))


def plan_rows(c, z, k, meta, qkv):
    hb, zs, sb = pair_of(c)
    head = 2 * z + hb
    length = meta[2 * zs + k, pl.ds(2 + sb, 1), :][:, :1]
    decay = meta[0, pl.ds(8 + head, 1), :]
    moment = meta[0, pl.ds(16 + head, 1), :]
    for f in range(1, 8):
        decay += meta[f, pl.ds(8 + head, 1), :]
        moment += meta[f, pl.ds(16 + head, 1), :]
    plan = qkv[:, 192:208, :].astype(f32)
    lanes = lax.broadcasted_iota(jnp.int32, (16, 128), 1).astype(f32)
    decay_pick = jnp.where(plan[:, 0, :] == lanes, 1.0, 0.0)
    moment_pick = jnp.where(plan[:, 1, :] == lanes, 1.0, 0.0)
    retention = jax.nn.sigmoid(jnp.sum(decay_pick * decay, axis=1, keepdims=True))
    momentum = jax.nn.sigmoid(jnp.sum(moment_pick * moment, axis=1, keepdims=True))
    return length, decay_pick, moment_pick, retention, momentum


def live_rows(length):
    places = lax.broadcasted_iota(jnp.int32, (1024, 1), 0).astype(f32)
    return jnp.where(places < length, 1.0, 0.0)


def pair_forward_kernel(
    qkv, pers, meta, mixed, probs, own, m0, s0, outer, q_u, k_u, vals, both, rate_f, rate_m, reads
):
    c, z, k = coords()
    hb = pair_of(c)[0]
    length, _, _, retention, momentum = plan_rows(c, z, k, meta, qkv)
    rate_f[...] = jnp.broadcast_to(retention, (16, 128))
    rate_m[...] = jnp.broadcast_to(momentum, (16, 128))
    q = qkv[:, 0:64, :].reshape(1024, 128)
    kk = qkv[:, 64:128, :].reshape(1024, 128)
    v = qkv[:, 128:192, :].reshape(1024, 128)
    live = live_rows(length)
    q_u[...] = unit_rows(q.astype(f32))[0]
    k_u[...] = unit_rows(kk.astype(f32))[0] * live
    vals[...] = v.astype(f32)
    for b in range(16):
        rows = slice(64 * b, 64 * b + 64)
        ku = k_u[rows, :]
        both[b] = tn(ku, jnp.concatenate([ku, vals[rows, :]], axis=1), HIGHEST)
        outer[b] = both[b, :, :128]
    memory = jnp.zeros((128, 128), f32)
    velocity = jnp.zeros((128, 128), f32)
    for b in range(16):
        m0[b] = memory
        s0[b] = velocity
        rows = slice(64 * b, 64 * b + 64)
        stacked = jnp.concatenate([q_u[rows, :], both[b, :, :128]], axis=0)
        got = nn(stacked, memory, HIGHEST)
        reads[rows, :] = got[:64]
        surprise = got[64:] - both[b, :, 128:]
        velocity = rate_m[b : b + 1, :] * velocity - RATE * surprise
        memory = rate_f[b : b + 1, :] * memory + velocity
    pk = pers[hb, 0]
    pv = pers[hb, 1]
    for i in range(4):
        span = 256 * (i + 1)
        qs = slice(256 * i, span)
        scores = nt(kk[:span], q[qs]) * SCALE
        own_scores = nt(pk, q[qs]) * SCALE
        key_at = lax.broadcasted_iota(jnp.int32, (span, 256), 0)
        query_at = lax.broadcasted_iota(jnp.int32, (span, 256), 1) + 256 * i
        allowed = (key_at <= query_at) & (key_at.astype(f32) < length)
        scores = jnp.where(allowed, scores, -1e30)
        top = jnp.maximum(
            jnp.max(scores, axis=0, keepdims=True), jnp.max(own_scores, axis=0, keepdims=True)
        )
        e = jnp.exp(scores - top)
        own_e = jnp.exp(own_scores - top)
        total = jnp.sum(e, axis=0, keepdims=True) + jnp.sum(own_e, axis=0, keepdims=True)
        p = (e / total).astype(bf16)
        own_p = (own_e / total).astype(bf16)
        probs[:span, qs] = p
        own[:, qs] = own_p
        att = tn(v[:span], p) + tn(pv, own_p)
        mixed[4 * i : 4 * i + 4] = (att.T + reads[qs, :]).astype(bf16).reshape(4, 64, 128)


def vmem_call(body, name, out_shapes, scratch, *operands):
    return pl.pallas_call(
        body,
        out_shape=out_shapes,
        in_specs=[pl.BlockSpec(memory_space=pltpu.VMEM)] * len(operands),
        out_specs=jax.tree.map(lambda _: pl.BlockSpec(memory_space=pltpu.VMEM), out_shapes),
        scratch_shapes=scratch,
        compiler_params=pltpu.CompilerParams(vmem_limit_bytes=VMEM_LIMIT),
        name=name,
    )(*operands)


def pair_forward(qkv, pers, meta):
    return vmem_call(
        pair_forward_kernel,
        "pair_forward",
        like((16, 64, 128), (1024, 1024), (16, 1024))
        + like((16, 128, 128), (16, 128, 128), (16, 128, 128), dtype=f32),
        [
            pltpu.VMEM((1024, 128), f32),
            pltpu.VMEM((1024, 128), f32),
            pltpu.VMEM((1024, 128), f32),
            pltpu.VMEM((16, 128, 256), f32),
            pltpu.VMEM((16, 128), f32),
            pltpu.VMEM((16, 128), f32),
            pltpu.VMEM((1024, 128), f32),
        ],
        qkv, pers, meta,
    )


def pair_backward_kernel(
    qkv, dmix, pers, meta, probs, own, m0, s0, outer,
    dqkv, d_own, d_plan,
    dq_s, dk_s, dv_s, adj, rate_f, rate_m,
):
    c, z, k = coords()
    hb = pair_of(c)[0]
    length, decay_pick, moment_pick, retention, momentum = plan_rows(c, z, k, meta, qkv)
    rate_f[...] = jnp.broadcast_to(retention, (16, 128))
    rate_m[...] = jnp.broadcast_to(momentum, (16, 128))
    q = qkv[:, 0:64, :].reshape(1024, 128)
    kk = qkv[:, 64:128, :].reshape(1024, 128)
    v = qkv[:, 128:192, :].reshape(1024, 128)
    dm = dmix[...].reshape(1024, 128)
    pk = pers[hb, 0]
    pv = pers[hb, 1]
    live = live_rows(length)
    qf, kf, vf, dmf = (a.astype(f32) for a in (q, kk, v, dm))
    q_u, q_r = unit_rows(qf)
    k_u, k_r = unit_rows(kf)
    k_l = k_u * live

    dk_s[...] = jnp.zeros_like(dk_s)
    dv_s[...] = jnp.zeros_like(dv_s)
    d_pk = jnp.zeros((16, 128), f32)
    d_pv = jnp.zeros((16, 128), f32)
    for i in range(4):
        span = 256 * (i + 1)
        qs = slice(256 * i, span)
        p = probs[:span, qs]
        own_p = own[:, qs]
        dp = nt(v[:span], dm[qs])
        own_dp = nt(pv, dm[qs])
        pf, own_pf = p.astype(f32), own_p.astype(f32)
        delta = jnp.sum(pf * dp, axis=0, keepdims=True) + jnp.sum(
            own_pf * own_dp, axis=0, keepdims=True
        )
        ds = (pf * (dp - delta)).astype(bf16)
        own_ds = (own_pf * (own_dp - delta)).astype(bf16)
        dq = tn(kk[:span], ds) + tn(pk, own_ds)
        dq_s[qs, :] = dq.T * SCALE
        dk_s[:span, :] += nn(ds, q[qs]) * SCALE
        dv_s[:span, :] += nn(p, dm[qs])
        d_pk += nn(own_ds, q[qs]) * SCALE
        d_pv += nn(own_p, dm[qs])
    d_own[0] = d_pk
    d_own[1] = d_pv

    adj_m = jnp.zeros((128, 128), f32)
    adj_v = jnp.zeros((128, 128), f32)
    d_decay = jnp.zeros((1, 128), f32)
    d_moment = jnp.zeros((1, 128), f32)
    for b in reversed(range(16)):
        rows = slice(64 * b, 64 * b + 64)
        total = adj_m + adj_v
        adj[b] = total
        g_f = jnp.sum(adj_m * m0[b])
        g_m = jnp.sum(total * s0[b])
        f_row, m_row = rate_f[b : b + 1, :], rate_m[b : b + 1, :]
        d_decay += decay_pick[b : b + 1, :] * (g_f * f_row * (1.0 - f_row))
        d_moment += moment_pick[b : b + 1, :] * (g_m * m_row * (1.0 - m_row))
        adj_m = (
            f_row * adj_m
            - RATE * nn(outer[b], total, HIGHEST)
            + tn(q_u[rows], dmf[rows], HIGHEST)
        )
        adj_v = m_row * total
    d_plan[...] = jnp.concatenate([d_decay, d_moment, jnp.zeros((6, 128), f32)], axis=0)
    for b in range(16):
        rows = slice(64 * b, 64 * b + 64)
        total = adj[b]
        d_outer = -RATE * nt(total, m0[b], HIGHEST)
        d_qu = nt(dmf[rows], m0[b], HIGHEST)
        d_kl = nn(k_l[rows], d_outer + d_outer.T, HIGHEST) + RATE * nt(vf[rows], total, HIGHEST)
        d_v = RATE * nn(k_l[rows], total, HIGHEST)
        dq = dq_s[rows, :] + unit_back(qf[rows], q_r[rows], d_qu)
        dk = dk_s[rows, :] + unit_back(kf[rows], k_r[rows], d_kl * live[rows])
        dv = dv_s[rows, :] + d_v
        dqkv[b, 0:64, :] = dq.astype(bf16)
        dqkv[b, 64:128, :] = dk.astype(bf16)
        dqkv[b, 128:192, :] = dv.astype(bf16)


def pair_backward(qkv, dmix, pers, meta, probs, own, m0, s0, outer):
    return vmem_call(
        pair_backward_kernel,
        "pair_backward",
        like((16, 192, 128)) + like((2, 16, 128), (8, 128), dtype=f32),
        [
            pltpu.VMEM((1024, 128), f32),
            pltpu.VMEM((1024, 128), f32),
            pltpu.VMEM((1024, 128), f32),
            pltpu.VMEM((16, 128, 128), f32),
            pltpu.VMEM((16, 128), f32),
            pltpu.VMEM((16, 128), f32),
        ],
        qkv, dmix, pers, meta, probs, own, m0, s0, outer,
    )


def scaled(values):
    return lax.rsqrt(jnp.mean(values * values, axis=-1, keepdims=True) + EPS)


def norm_back(values, gain, grad):
    r = scaled(values)
    inner = grad * gain
    back = r * inner - (r * r * r) * values * jnp.mean(values * inner, axis=-1, keepdims=True)
    return back, jnp.sum(grad * values * r, axis=0)


def shards(
    inputs, gain_attn, w_query, w_key, w_value, w_out, persist_key, persist_value, gain_ffn,
    w_gate, w_up, w_down, decay_table, momentum_table, lengths, decay_index, momentum_index,
    cotangent,
):
    c, z, k = coords()
    f = 2 * z + k
    hb, zs, sb = pair_of(c)
    x = inputs.reshape(128, 1024)
    lanes = jnp.arange(128)

    def wide(v):
        return jnp.broadcast_to(v.reshape(2, 1).astype(f32), (2, 128))

    def placed(table):
        t = table.astype(f32)
        return sum(t[r][:, None] * (lanes[None, :] == 2 * f + r) for r in range(2))

    meta = jnp.concatenate(
        [
            gain_attn[None].astype(f32), gain_ffn[None].astype(f32), wide(lengths),
            wide(decay_index), wide(momentum_index), placed(decay_table), placed(momentum_table),
        ],
        axis=0,
    )

    def quarters(w):
        return jnp.pad(w.reshape(128, 4, 704).swapaxes(0, 1), ((0, 0), (0, 0), (0, 64)))

    (
        x_all, cot_all, meta_all, wq, wk, wv, wo, wg, wu, wd, pers,
    ) = comm_call(
        front_kernel,
        "front",
        1,
        like((4, 128, 1024), (4, 128, 1024))
        + like((8, 24, 128), dtype=f32)
        + like(*[(8, 128, 256)] * 3, (8, 128, 1024), *[(8, 128, 768)] * 2, (2, 352, 1024), (2, 2, 16, 128)),
        64,
        x, cotangent.reshape(128, 1024), meta, w_query, w_key, w_value, w_out,
        quarters(w_gate), quarters(w_up), w_down, jnp.stack([persist_key, persist_value]),
    )
    gain_one = meta_all[:, 0, :].reshape(1024)
    gain_two = meta_all[:, 1, :].reshape(1024)
    by_z = lax.dynamic_index_in_dim(meta_all.reshape(4, 2, 24, 128), k, 1, keepdims=False)
    places = c * 64 + jnp.arange(64)
    live = (places[None, None, :] < by_z[:, 2:4, :1]).astype(f32)

    xf = x_all.reshape(512, 1024).astype(f32)
    normed = (xf * scaled(xf) * gain_one).astype(bf16)
    w_qkv = jnp.concatenate([w.reshape(1024, 256) for w in (wq, wk, wv)], axis=1)
    qkv = nn(normed, w_qkv).astype(bf16)
    rows = qkv.reshape(4, 2, 64, 3, 2, 128).transpose(4, 0, 1, 3, 2, 5).reshape(16, 192, 128)
    plan = by_z[:, 4:8, :].reshape(4, 2, 2, 128).swapaxes(1, 2).astype(bf16)
    plan = jnp.pad(jnp.broadcast_to(plan[None], (2, 4, 2, 2, 128)).reshape(16, 2, 128), ((0, 0), (0, 14), (0, 0)))
    (pair,) = ctx_swap(2, "qkv_out", jnp.concatenate([rows, plan], axis=1))

    mixed, probs, own, m0, s0, outer = pair_forward(pair, pers, meta_all)
    mix_tok, mix_quart = mixed_home(3, mixed)
    mix_tok = mix_tok.reshape(8, 2, 64, 128).transpose(1, 2, 0, 3).reshape(128, 1024)
    mix_quart = mix_quart.reshape(2, 4, 2, 64, 128).transpose(1, 2, 3, 0, 4).reshape(512, 256)

    w_o = wo.reshape(1024, 1024)
    xt = x.astype(f32)
    resid = xt + nn(mix_tok, w_o)
    nf = (resid * scaled(resid) * gain_two).astype(bf16)
    (nf_all,) = z_swap(4, "ffn_gather", nf, gather=True)
    nf_all = nf_all.reshape(512, 1024)
    w_g, w_u = wg.reshape(1024, 768), wu.reshape(1024, 768)
    w_d = jnp.pad(wd.reshape(704, 1024), ((0, 64), (0, 0)))
    g, u = nn(nf_all, w_g), nn(nf_all, w_u)
    s = jax.nn.sigmoid(g)
    hidden = (g * s * u).astype(bf16)
    out_part = nn(hidden, w_d).astype(bf16)
    od = (cot_all.reshape(4, 2, 64, 1024).astype(f32) * live[..., None]).astype(bf16).reshape(512, 1024)
    dh = nt(od, w_d)
    d_g = (dh * u * s * (1.0 + g * (1.0 - s))).astype(bf16)
    d_u = (dh * g * s).astype(bf16)
    nf_part = (nt(d_g, w_g) + nt(d_u, w_u)).astype(bf16)
    out_in, nf_in = z_swap(5, "ffn_scatter", out_part.reshape(4, 128, 1024), nf_part.reshape(4, 128, 1024))
    output = (resid + jnp.sum(out_in.astype(f32), axis=0)).astype(bf16)
    d_nf = jnp.sum(nf_in.astype(f32), axis=0)
    out_grad = cotangent.reshape(128, 1024).astype(f32) * lax.dynamic_index_in_dim(
        live, z, 0, keepdims=False
    ).reshape(128, 1)
    back, g_gain_two = norm_back(resid, gain_two, d_nf)
    d_resid = out_grad + back
    d_branch = d_resid.astype(bf16)
    dmix = nt(d_branch, w_o).astype(bf16).reshape(2, 64, 8, 128).transpose(2, 0, 1, 3).reshape(16, 64, 128)
    dm_blocks, branch_all = grads_out(6, dmix, d_branch)
    dqkv, d_own, d_plan = pair_backward(pair, dm_blocks, pers, meta_all, probs, own, m0, s0, outer)
    (dq_home,) = ctx_swap(7, "dqkv_home", dqkv)
    dq_rows = dq_home.reshape(2, 4, 2, 3, 64, 128).transpose(1, 2, 4, 3, 0, 5).reshape(512, 768)
    dn_part = nt(dq_rows, w_qkv).astype(bf16)
    (dn_in,) = z_swap(8, "dnormed_scatter", dn_part.reshape(4, 128, 1024))
    back, g_gain_one = norm_back(xt, gain_one, jnp.sum(dn_in.astype(f32), axis=0))
    input_grad = d_resid + back

    g_qkv = tn(normed, dq_rows).astype(bf16).reshape(4, 2, 128, 768)
    g_gate = tn(nf_all, d_g).astype(bf16).reshape(4, 2, 128, 768)
    g_up = tn(nf_all, d_u).astype(bf16).reshape(4, 2, 128, 768)
    g_down = tn(hidden, od)[:704].astype(bf16).reshape(2, 352, 1024)
    g_out = tn(mix_quart, branch_all.reshape(512, 1024)).astype(bf16).reshape(2, 128, 1024)
    other = core_swap(9, "core_swap", g_gate, g_up, g_qkv, g_down, g_out)

    def both(mine, theirs, axis):
        own_half = lax.dynamic_index_in_dim(mine, k, axis, keepdims=False)
        return (own_half.astype(f32) + theirs.astype(f32)).astype(bf16)

    gate2, up2, qkv2 = (both(m, t, 1) for m, t in zip((g_gate, g_up, g_qkv), other[:3]))
    down2, out2 = both(g_down, other[3], 0), both(g_out, other[4], 0)
    gathered = reduce_ctx(10, jnp.stack([gate2, up2]), qkv2, down2, out2)
    gu_p, qkv_p, down_p, out_p = (jnp.sum(a.astype(f32), axis=0).astype(bf16) for a in gathered)
    gu_p, qkv_p = z_swap(11, "grad_z", gu_p, qkv_p)
    gu_f, qkv_f, down_f, out_f = ctx_gather(12, "grad_gather", gu_p, qkv_p, down_p, out_p)
    gu_f = gu_f.reshape(8, 2, 4, 16, 768)[..., :704].transpose(1, 0, 3, 2, 4).reshape(2, 128, 2816).astype(f32)
    qkv_f = qkv_f.reshape(8, 2, 4, 16, 384).transpose(0, 3, 2, 1, 4).reshape(128, 4, 3, 256)
    qkv_f = qkv_f.transpose(2, 0, 1, 3).reshape(3, 128, 1024).astype(f32)
    down_f = down_f.reshape(8, 2, 176, 128).transpose(1, 2, 0, 3).reshape(352, 1024).astype(f32)
    out_f = out_f.reshape(8, 2, 16, 512).transpose(0, 2, 1, 3).reshape(128, 1024).astype(f32)

    head = 2 * z + hb
    at_head = (jnp.arange(8) == head).astype(f32)
    small = jnp.concatenate(
        [
            g_gain_one, g_gain_two,
            (at_head[:, None, None, None] * d_own[None]).reshape(-1),
            (at_head[:, None, None] * d_plan[None, :2, :16]).reshape(-1),
        ]
    )
    small = lax.psum(small, ("ctx", "fsdp"))
    own_gain_one = lax.dynamic_slice(small, (f * 128,), (128,))
    own_gain_two = lax.dynamic_slice(small, (1024 + f * 128,), (128,))
    own_pers = lax.dynamic_slice(small, (2048 + f * 4096,), (4096,)).reshape(2, 16, 128)
    tables = small[2048 + 32768 :].reshape(8, 2, 16)
    own_tables = lax.dynamic_slice(tables, (0, 0, 2 * f), (8, 2, 2)).transpose(1, 2, 0)
    return (
        output.reshape(2, 64, 1024),
        input_grad.reshape(2, 64, 1024),
        own_gain_one,
        qkv_f[0], qkv_f[1], qkv_f[2],
        out_f,
        own_pers[0], own_pers[1],
        own_gain_two,
        gu_f[0], gu_f[1],
        down_f,
        own_tables[0], own_tables[1],
    )


def solution(mesh):
    rows, cols = P("fsdp", None), P(None, "fsdp")
    tokens = P("fsdp", "ctx", None)
    in_specs = (
        tokens, P("fsdp"), rows, rows, rows, rows, cols, cols, P("fsdp"), rows, rows, rows, rows, rows,
        P("fsdp"), P("fsdp", "ctx"), P("fsdp", "ctx"), tokens,
    )
    out_specs = (
        tokens, tokens, P("fsdp"), rows, rows, rows, rows, cols, cols, P("fsdp"), rows, rows, rows, rows, rows,
    )
    return jax.shard_map(shards, mesh=mesh, in_specs=in_specs, out_specs=out_specs, check_vma=False)
```

```python
import functools

import jax
import jax.numpy as jnp
from jax import lax
from jax.experimental import pallas as pl
from jax.experimental.pallas import tpu as pltpu
from jax.sharding import PartitionSpec as P

MESH = pl.DeviceIdType.MESH
HIGHEST = lax.Precision.HIGHEST
bf16, f32 = jnp.bfloat16, jnp.float32
EPS = 1e-06
RATE = 0.1
SCALE = 128**-0.5
VMEM_LIMIT = 63 << 20
SEMS = (90, 97, 13)


def coords():
    c, f = lax.axis_index("ctx"), lax.axis_index("fsdp")
    return c, lax.div(f, 2), lax.rem(f, 2)


def pair_of(c):
    return lax.div(c, 8), lax.rem(lax.div(c, 2), 4), lax.rem(c, 2)


def at_ctx(c, dx, dy):
    x, y = lax.div(c, 4), lax.rem(c, 4)
    return lax.rem(x + dx, 4) * 4 + lax.rem(y + dy, 4)


CTX_STEPS = [(dx, dy) for dx in range(4) for dy in range(4) if dx or dy]
CTX_STEPS.sort(key=lambda s: -(min(s[0], 4 - s[0]) + min(s[1], 4 - s[1])))
Z_STEPS = (1, 3, 2)


def device(c, z, k):
    return (c, 2 * z + k)


def nn(a, b, precision=None):
    return jnp.dot(a, b, preferred_element_type=f32, precision=precision)


def nt(a, b, precision=None):
    return lax.dot_general(
        a, b, (((1,), (1,)), ((), ())), preferred_element_type=f32, precision=precision
    )


def tn(a, b, precision=None):
    return lax.dot_general(
        a, b, (((0,), (0,)), ((), ())), preferred_element_type=f32, precision=precision
    )


def ds(index, size):
    return pl.ds(pl.multiple_of(index * size, size), size)


def remote(src, dst, ssem, rsem, peer):
    return pltpu.make_async_remote_copy(
        src_ref=src, dst_ref=dst, send_sem=ssem, recv_sem=rsem, device_id=peer, device_id_type=MESH
    )


class Net:
    def __init__(self, ssem, rsem, lsem, here):
        self.ssem, self.rsem, self.lsem, self.here = ssem, rsem, lsem, here
        self.s = self.r = self.l = 0
        self.due = []

    def slots(self, n=1):
        self.r += n
        return self.r - n

    def send(self, moves, size, r, s=None):
        if s is None:
            s = self.group(size)
        for src, dst, peer, *own in moves:
            at = own[0] if own else r
            remote(src, dst, self.ssem.at[s], self.rsem.at[at], peer).start()
        return s

    def group(self, size):
        s = self.s
        self.s += 1
        self.due.append((size, s))
        return s

    def own(self, src, dst, r):
        pltpu.make_async_copy(src, dst, self.rsem.at[r]).start()

    def landed(self, size, r):
        remote(size, size, self.ssem.at[0], self.rsem.at[r], self.here).wait_recv()

    def local(self, src, dst):
        copy = pltpu.make_async_copy(src, dst, self.lsem.at[self.l])
        self.l += 1
        copy.start()
        return copy

    def drain(self, count=None):
        count = len(self.due) if count is None else count
        for size, s in self.due[:count]:
            remote(size, size, self.ssem.at[s], self.rsem.at[0], self.here).wait_send()
        self.due = self.due[count:]


def scaled(values):
    return lax.rsqrt(jnp.mean(values * values, axis=-1, keepdims=True) + EPS)


def norm_back(values, gain, grad):
    r = scaled(values)
    inner = grad * gain
    back = r * inner - (r * r * r) * values * jnp.mean(values * inner, axis=-1, keepdims=True)
    return back, jnp.sum(grad * values * r, axis=0, keepdims=True)


def unit_rows(rows):
    r = lax.rsqrt(jnp.mean(rows * rows, axis=-1, keepdims=True) + EPS)
    return rows * r * SCALE, r


def unit_back(rows, r, grad):
    return SCALE * (r * grad - rows * (r * r * r) * jnp.mean(rows * grad, axis=-1, keepdims=True))


class Shared:
    def __init__(self, net, first, zdim, part1, part2, src, r1, t1, r2, t2, zr, final):
        self.net, self.first, self.zdim = net, first, zdim
        self.part1, self.part2 = part1, part2
        self.src, self.r1, self.t1, self.r2, self.t2, self.zr, self.final = src, r1, t1, r2, t2, zr, final
        self.slot = net.slots(5)

    def place(self, c, z, k):
        x, y = lax.div(c, 4), lax.rem(c, 4)
        self.c, self.z, self.k = c, z, k
        self.i, self.j = (x, y) if self.first == "x" else (y, x)

    def peer(self, second, d):
        along_x = (self.first == "x") != second
        return device(at_ctx(self.c, d if along_x else 0, 0 if along_x else d), self.z, self.k)

    def step1(self):
        self.net.send(
            [
                (self.src.at[self.part1(lax.rem(self.i + d, 4))], self.r1.at[d - 1], self.peer(False, d))
                for d in (2, 1, 3)
            ],
            self.r1,
            self.slot,
        )

    def step2(self):
        self.net.landed(self.r1, self.slot)
        total = self.src[self.part1(self.i)].astype(f32)
        for d in range(3):
            total += self.r1[d].astype(f32)
        self.t1[...] = total.astype(bf16)
        self.net.send(
            [
                (self.t1.at[self.part2(lax.rem(self.j + d, 4))], self.r2.at[d - 1], self.peer(True, d))
                for d in (2, 1, 3)
            ],
            self.r2,
            self.slot + 1,
        )

    def step3(self):
        self.net.landed(self.r2, self.slot + 1)
        total = self.t1[self.part2(self.j)].astype(f32)
        for d in range(3):
            total += self.r2[d].astype(f32)
        self.t2[...] = total.astype(bf16)
        if self.zdim:
            self.zr[self.z] = self.t2[self.z]
            moves = []
            for d in (2, 1, 3):
                zz = lax.rem(self.z + d, 4)
                moves.append((self.t2.at[zz], self.zr.at[self.z], device(self.c, zz, self.k)))
            self.net.send(moves, self.zr.at[pl.ds(0, 3)], self.slot + 2)

    def block(self, i):
        return self.final.at[self.part1_final(i)]

    def piece(self, i, j):
        return self.final.at[self.piece_final(i, j)]

    def step4(self):
        if self.zdim:
            self.net.landed(self.zr.at[pl.ds(0, 3)], self.slot + 2)
        src = self.zr if self.zdim else self.t2
        spot = self.piece(self.i, self.j)
        self.mine = self.net.local(src, spot)
        self.net.send([(src, spot, self.peer(True, d)) for d in (2, 1, 3)], self.r2, self.slot + 3)

    def step5(self):
        self.mine.wait()
        self.net.landed(self.r2, self.slot + 3)
        spot = self.block(self.i)
        self.net.send([(spot, spot, self.peer(False, d)) for d in (2, 1, 3)], self.r1, self.slot + 4)

    def step6(self):
        self.net.landed(self.r1, self.slot + 4)


def shared_shapes(zdim, block, piece):
    lead = (4,) if zdim else ()
    return [
        pltpu.VMEM((3, *lead, *block), bf16),
        pltpu.VMEM((*lead, *block), bf16),
        pltpu.VMEM((3, *lead, *piece), bf16),
        pltpu.VMEM((*lead, *piece), bf16),
        pltpu.VMEM((*lead, *piece), bf16),
    ]


def wide_shared(net, first, column, width, src, scratch, final):
    half = width // 2
    shared = Shared(
        net,
        first,
        True,
        lambda i: (slice(None), ds(i, 32), pl.ds(column, width)),
        lambda j: (slice(None), ds(lax.div(j, 2), 16), ds(lax.rem(j, 2), half)),
        src,
        *scratch,
        final,
    )
    shared.part1_final = lambda i: (slice(None), ds(i, 32), slice(None))
    shared.piece_final = lambda i, j: (
        slice(None),
        ds(2 * i + lax.div(j, 2), 16),
        ds(lax.rem(j, 2), half),
    )
    return shared


def down_shared(net, first, row, rows, src, scratch, final):
    half = rows // 2
    shared = Shared(
        net,
        first,
        False,
        lambda i: (pl.ds(row, rows), ds(i, 256)),
        lambda j: (ds(lax.div(j, 2), half), ds(lax.rem(j, 2), 128)),
        src,
        *scratch,
        final,
    )
    shared.part1_final = shared.part1
    shared.piece_final = lambda i, j: (
        pl.ds(pl.multiple_of(row + lax.div(j, 2) * half, 16), half),
        ds(2 * i + lax.rem(j, 2), 128),
    )
    return shared


def out_shared(net, src, scratch, final):
    shared = Shared(
        net,
        "y",
        False,
        lambda i: (ds(i, 32), slice(None)),
        lambda j: (ds(lax.div(j, 2), 16), ds(lax.rem(j, 2), 512)),
        src,
        *scratch,
        final,
    )
    shared.part1_final = lambda i: (ds(i, 32), slice(None))
    shared.piece_final = lambda i, j: (ds(2 * i + lax.div(j, 2), 16), ds(lax.rem(j, 2), 512))
    return shared


class Weight:
    def __init__(self, net, buf, block, parts, c, z, k):
        self.net, self.buf, self.block = net, buf, block
        self.c, self.z, self.k = c, z, k
        x, y = lax.div(c, 4), lax.rem(c, 4)
        self.parts = [(first, *((x, y) if first == "x" else (y, x)), col, width) for first, col, width in parts]
        self.slot = net.slots(2 + 3 * len(parts))

    def peer(self, along_x, d):
        return device(at_ctx(self.c, d if along_x else 0, 0 if along_x else d), self.z, self.k)

    def piece(self, i, j, col, width):
        half = width // 2
        return ds(2 * i + lax.div(j, 2), 16), pl.ds(
            pl.multiple_of(col + lax.rem(j, 2) * half, 128), half
        )

    def step0(self):
        n, k = self.net, self.k
        sibling = device(self.c, self.z, 1 - k)
        self.mine = n.local(self.block(self.z), self.buf.at[0, k])
        for p, (first, i, j, col, width) in enumerate(self.parts):
            rows, cols = self.piece(i, j, col, width)
            n.send(
                [
                    (
                        self.block(lax.rem(self.z + d, 4)).at[rows, cols],
                        self.buf.at[4 - d, k, rows, cols],
                        device(self.c, lax.rem(self.z + d, 4), k),
                    )
                    for d in Z_STEPS
                ],
                self.buf.at[pl.ds(1, 3), k, rows, cols],
                self.slot + 2 + 3 * p,
            )
        n.send([(self.block(self.z), self.buf.at[0, k], sibling)], self.buf.at[0, k], self.slot)

    def step1(self):
        for p, (first, i, j, col, width) in enumerate(self.parts):
            rows, cols = self.piece(i, j, col, width)
            spot = self.buf.at[pl.ds(1, 3), self.k, rows, cols]
            self.net.landed(spot, self.slot + 2 + 3 * p)
            size = self.buf.at[pl.ds(1, 3), self.k, pl.ds(0, 48), pl.ds(col, width // 2)]
            self.net.send(
                [(spot, spot, self.peer(first != "x", d)) for d in (2, 1, 3)], size, self.slot + 3 + 3 * p
            )

    def step2(self):
        for p, (first, i, j, col, width) in enumerate(self.parts):
            size = self.buf.at[pl.ds(1, 3), self.k, pl.ds(0, 48), pl.ds(col, width // 2)]
            self.net.landed(size, self.slot + 3 + 3 * p)
            spot = self.buf.at[pl.ds(1, 3), self.k, ds(i, 32), pl.ds(col, width)]
            size = self.buf.at[pl.ds(1, 3), self.k, pl.ds(0, 96), pl.ds(col, width)]
            self.net.send(
                [(spot, spot, self.peer(first == "x", d)) for d in (2, 1, 3)], size, self.slot + 4 + 3 * p
            )

    def step3(self):
        for p, (first, i, j, col, width) in enumerate(self.parts):
            size = self.buf.at[pl.ds(1, 3), self.k, pl.ds(0, 96), pl.ds(col, width)]
            self.net.landed(size, self.slot + 4 + 3 * p)
        spot = self.buf.at[pl.ds(1, 3), self.k]
        self.net.send([(spot, spot, device(self.c, self.z, 1 - self.k))], spot, self.slot + 1)

    def step4(self):
        self.mine.wait()
        self.net.landed(self.buf.at[0, 0], self.slot)
        self.net.landed(self.buf.at[pl.ds(1, 3), 0], self.slot + 1)


SHARED = dict(
    gate=(True, (32, 768), (16, 384)),
    up=(True, (32, 768), (16, 384)),
    q=(True, (32, 256), (16, 128)),
    k=(True, (32, 256), (16, 128)),
    v=(True, (32, 256), (16, 128)),
    down_a=(False, (192, 256), (96, 128)),
    down_b=(False, (160, 256), (80, 128)),
    out=(False, (32, 1024), (16, 512)),
)

SCRATCH = dict(
    meta=((4, 2, 24, 128), f32),
    plan=((4, 4, 4, 8, 128), f32),
    pers=((2, 2, 16, 128), bf16),
    x_all=((4, 128, 1024), bf16),
    cot_all=((4, 128, 1024), bf16),
    w_own=((4, 128, 768), bf16),
    w_all=((4, 2, 128, 768), bf16),
    wo_all=((4, 2, 128, 1024), bf16),
    stage=((4, 128, 1536), bf16),
    wgu_all=((4, 2, 128, 1536), bf16),
    wide=((128, 1024), f32),
    wd_all=((768, 1024), bf16),
    n_all=((4, 128, 1024), bf16),
    qkv_s=((3, 512, 256), bf16),
    qkv=((16, 3, 64, 128), bf16),
    probs=((1024, 1024), bf16),
    own=((16, 1024), bf16),
    m0=((16, 128, 128), bf16),
    s0=((16, 128, 128), bf16),
    qa=((16, 192, 128), bf16),
    outer=((16, 128, 128), f32),
    k_l=((16, 64, 128), bf16),
    bias=((1024, 128), f32),
    gf_rows=((16, 128), f32),
    gm_rows=((16, 128), f32),
    rate_f=((16, 128), f32),
    rate_m=((16, 128), f32),
    read_adj=((16, 128, 128), f32),
    reads=((1024, 128), f32),
    mixed=((16, 64, 128), bf16),
    mt=((128, 1024), bf16),
    mq=((512, 256), bf16),
    resid=((128, 1024), f32),
    nf_all=((4, 128, 1024), bf16),
    hid_all=((4, 128, 768), bf16),
    dh=((4, 128, 768), f32),
    dgu_all=((4, 128, 1536), bf16),
    od_all=((4, 128, 1024), bf16),
    nf_own=((128, 1024), f32),
    nf_s=((4, 128, 1024), bf16),
    nf_r=((3, 128, 1024), bf16),
    out_s=((4, 128, 1024), bf16),
    out_r=((3, 128, 1024), bf16),
    d_resid=((128, 1024), f32),
    dbr_all=((4, 128, 1024), bf16),
    dmix=((128, 1024), bf16),
    dm=((16, 64, 128), bf16),
    dq_a=((1024, 128), f32),
    dk_a=((1024, 128), f32),
    dv_a=((1024, 128), f32),
    adj=((16, 128, 128), bf16),
    dqkv=((16, 3, 64, 128), bf16),
    dq_home=((3, 512, 256), bf16),
    dq_l=((512, 768), bf16),
    dn_s=((4, 128, 1024), bf16),
    dn_r=((3, 128, 1024), bf16),
    gu_r=((4, 128, 1536), bf16),
    nf_gain=((1, 1024), f32),
    gu_1=((4, 128, 1536), bf16),
    gd=((768, 1024), bf16),
    gd_r=((352, 1024), bf16),
    gd_1=((352, 1024), bf16),
    gq_s=((4, 128, 768), bf16),
    gq_r=((4, 128, 768), bf16),
    gq_1=((4, 128, 768), bf16),
    go_s=((128, 1024), bf16),
    go_r=((128, 1024), bf16),
    go_1=((128, 1024), bf16),
    gains=((16, 128), f32),
    tables=((16, 128), f32),
    d_own=((32, 128), f32),
    keep=((64, 128), f32),
    give=((64, 128), f32),
    sm_s=((64, 128), f32),
    sm_x=((4, 64, 128), f32),
    sm_y=((4, 64, 128), f32),
    sm_z=((4, 32, 128), f32),
)

INPUTS = [
    "x", "cot", "wq", "wk", "wv", "wo", "wg", "wu", "wd", "pk", "pv", "ga", "gf", "dec", "mom",
    "lens", "didx", "midx",
]
OUTPUTS = dict(
    output=((128, 1024), bf16),
    input_grad=((128, 1024), f32),
    f_gate=((4, 128, 768), bf16),
    f_up=((4, 128, 768), bf16),
    f_q=((4, 128, 256), bf16),
    f_k=((4, 128, 256), bf16),
    f_v=((4, 128, 256), bf16),
    f_down=((352, 1024), bf16),
    f_out=((128, 1024), bf16),
    small=((64, 128), f32),
)


class Refs:
    pass


def layer_kernel(*refs):
    names = INPUTS + list(OUTPUTS) + list(SCRATCH)
    a = Refs()
    for name, ref in zip(names, refs):
        setattr(a, name, ref)
    rest = refs[len(names) :]
    ssem, rsem, lsem, plane_sem, cube_sem, own_sem = rest[-6:]
    c, z, k = coords()
    f = 2 * z + k
    hb, zs, sb = pair_of(c)
    x_at, y_at = lax.div(c, 4), lax.rem(c, 4)
    here, sibling = device(c, z, k), device(c, z, 1 - k)
    same_plane = zs == z
    net = Net(ssem, rsem, lsem, here)
    shared = {}
    sources = dict(
        gate=("x", 0, 768, a.gu_1, a.f_gate),
        up=("y", 768, 768, a.gu_1, a.f_up),
        q=("x", 0, 256, a.gq_1, a.f_q),
        k=("x", 256, 256, a.gq_1, a.f_k),
        v=("y", 512, 256, a.gq_1, a.f_v),
    )
    for n, name in enumerate(SHARED):
        scratch = rest[5 * n : 5 * n + 5]
        if name in sources:
            first, column, width, src, final = sources[name]
            shared[name] = wide_shared(net, first, column, width, src, scratch, final)
        elif name == "down_a":
            shared[name] = down_shared(net, "x", 0, 192, a.gd_1, scratch, a.f_down)
        elif name == "down_b":
            shared[name] = down_shared(net, "y", 192, 160, a.gd_1, scratch, a.f_down)
        else:
            shared[name] = out_shared(net, a.go_1, scratch, a.f_out)
        shared[name].place(c, z, k)

    def z_at(d):
        return lax.rem(z + d + 4, 4)

    def z_peer(d):
        return device(c, z_at(d), k)

    barrier = pltpu.get_barrier_semaphore()

    def along(axis, d):
        return device(at_ctx(c, d if axis == "x" else 0, 0 if axis == "x" else d), z, k)

    for d in Z_STEPS:
        for peer in (z_peer(d), along("x", d), along("y", d)):
            pl.semaphore_signal(barrier, inc=1, device_id=peer, device_id_type=MESH)
    pl.semaphore_signal(barrier, inc=1, device_id=sibling, device_id_type=MESH)

    for n, w in enumerate((a.wq, a.wk, a.wv)):
        for m in range(4):
            pltpu.make_async_copy(
                w.at[:, pl.ds(256 * m, 256)], a.w_own.at[m, :, pl.ds(256 * n, 256)], own_sem
            ).start()

    lane8 = lax.broadcasted_iota(jnp.int32, (8, 128), 1)
    row8 = lax.broadcasted_iota(jnp.int32, (8, 128), 0)
    eye8 = lax.broadcasted_iota(jnp.int32, (8, 8), 0) == lax.broadcasted_iota(jnp.int32, (8, 8), 1)

    def by_head(table):
        placed = jnp.zeros((8, 128), f32)
        for r in range(2):
            row = jnp.broadcast_to(table[r : r + 1, :].astype(f32), (8, 8))
            column = jnp.sum(jnp.where(eye8, row, 0.0), axis=1, keepdims=True)
            placed += jnp.where(lane8 == 2 * f + r, column, 0.0)
        return placed

    head_rows = jnp.where(row8 == 0, a.ga[...].astype(f32), 0.0)
    head_rows = jnp.where(row8 == 1, a.gf[...].astype(f32), head_rows)
    for n in range(2):
        head_rows = jnp.where(row8 == 2 + n, a.lens[n].astype(f32), head_rows)
    a.meta[z, k, 0:8, :] = head_rows
    a.meta[z, k, 8:16, :] = by_head(a.dec[...])
    a.meta[z, k, 16:24, :] = by_head(a.mom[...])
    plan = jnp.zeros((8, 128), f32)
    for n in range(2):
        plan = jnp.where(row8 == n, a.didx[n].astype(f32), plan)
        plan = jnp.where(row8 == 2 + n, a.midx[n].astype(f32), plan)
    a.plan[z, x_at, y_at] = plan
    a.pers[k, 0] = a.pk[...]
    a.pers[k, 1] = a.pv[...]
    a.x_all[z] = a.x[...]

    pl.semaphore_wait(barrier, 10)
    for d in Z_STEPS:
        pl.semaphore_signal(plane_sem, inc=1, device_id=along("y", d), device_id_type=MESH)

    r_meta, r_meta_s, r_x = net.slots(), net.slots(), net.slots(3)
    r_plan, r_pers, r_wd, r_cot = net.slots(3), net.slots(), net.slots(), net.slots()
    w_qkv = Weight(net, a.w_all, lambda zz: a.w_own.at[zz], [("x", 0, 512), ("y", 512, 256)], c, z, k)
    w_o = Weight(net, a.wo_all, lambda zz: a.wo, [("x", 0, 512), ("y", 512, 512)], c, z, k)
    w_gu = Weight(net, a.wgu_all, lambda zz: a.stage.at[zz], [("x", 0, 768), ("y", 768, 768)], c, z, k)

    pltpu.make_async_copy(a.w_own, a.w_own, own_sem).wait()
    w_qkv.step0()
    net.send(
        [(a.x_all.at[z], a.x_all.at[z], z_peer(d), r_x + d - 1) for d in Z_STEPS], a.x_all.at[pl.ds(0, 3)], None
    )
    spot = a.meta.at[z, k]
    net.send([(spot, spot, z_peer(d)) for d in Z_STEPS], a.meta.at[pl.ds(0, 3), 0], r_meta)
    w_o.step0()
    spot = a.plan.at[z, x_at, y_at]
    net.send([(spot, spot, along("x", d)) for d in Z_STEPS], a.plan.at[0, 0, pl.ds(0, 3)], r_plan)
    net.send([(a.pers.at[k], a.pers.at[k], sibling)], a.pers.at[0], r_pers)
    wd_rows = pl.ds(pl.multiple_of(k * 352, 32), 352)
    own_wd = net.local(a.wd, a.wd_all.at[wd_rows, :])
    net.send([(a.wd, a.wd_all.at[wd_rows, :], sibling)], a.gd_r, r_wd)
    a.wd_all[704:768, :] = jnp.zeros((64, 1024), bf16)
    w_qkv.step1()
    net.landed(a.meta.at[pl.ds(0, 3), 0], r_meta)
    spot = a.meta.at[:, k]
    net.send([(spot, spot, sibling)], spot, r_meta_s)
    net.landed(a.plan.at[0, 0, pl.ds(0, 3)], r_plan)
    spot = a.plan.at[z, :, y_at]
    net.send([(spot, spot, along("y", d)) for d in Z_STEPS], a.plan.at[0, pl.ds(0, 3)], r_plan + 1)
    w_qkv.step2()
    w_o.step1()
    for n in range(4):
        for m, w in enumerate((a.wg, a.wu)):
            block = jnp.concatenate([w[:, 704 * n : 704 * n + 704], jnp.zeros((128, 64), bf16)], axis=1)
            a.stage[n, :, 768 * m : 768 * m + 768] = block
    w_gu.step0()
    own_cot = net.local(a.cot, a.cot_all.at[z])
    net.send([(a.cot, a.cot_all.at[z], z_peer(d)) for d in Z_STEPS], a.cot_all.at[pl.ds(0, 3)], r_cot)
    early = len(net.due)

    pl.semaphore_wait(plane_sem, 3)
    for d in Z_STEPS:
        pl.semaphore_signal(cube_sem, inc=1, device_id=z_peer(d), device_id_type=MESH)
    net.landed(a.plan.at[0, pl.ds(0, 3)], r_plan + 1)
    net.send([(a.plan.at[z], a.plan.at[z], z_peer(d)) for d in Z_STEPS], a.plan.at[pl.ds(0, 3)], r_plan + 2)
    net.landed(a.meta.at[:, k], r_meta_s)

    def gain_row(n):
        return jnp.concatenate([a.meta[i // 2, i % 2, n : n + 1, :] for i in range(8)], axis=1)

    gain_one, gain_two = gain_row(0), gain_row(1)
    w_qkv.step3()

    def ahead(e):
        return ds(z_at(e), 256)

    def whole(ref, e):
        return ref[e].reshape(256, ref.shape[-1])

    for d in (0, *Z_STEPS):
        zz = z_at(-d)
        if d:
            net.landed(a.x_all.at[0], r_x + d - 1)
        xf = a.x_all[zz].astype(f32)
        a.n_all[zz] = (xf * scaled(xf) * gain_one).astype(bf16)
    w_qkv.step4()
    for d in (0, *Z_STEPS):
        zz = z_at(-d)
        rows = sum(nn(a.n_all[zz, :, ahead(e)], whole(a.w_all, e)) for e in range(4)).astype(bf16)
        for n in range(3):
            a.qkv_s[n, ds(zz, 128), :] = rows[:, 256 * n : 256 * n + 256]

    r_qkv = net.slots()

    def pair_block(ref, cc):
        hb2, zs2, sb2 = pair_of(cc)
        return ref.at[:, ds(zs2 * 2 + sb2, 64), ds(hb2, 128)]

    net.own(pair_block(a.qkv_s, c), a.qkv.at[c], r_qkv)
    net.send(
        [
            (pair_block(a.qkv_s, at_ctx(c, dx, dy)), a.qkv.at[c], device(at_ctx(c, dx, dy), z, k))
            for dx, dy in CTX_STEPS
        ],
        a.qkv.at[pl.ds(0, 15)],
        r_qkv,
    )

    w_o.step2()
    w_gu.step1()

    net.landed(a.plan.at[pl.ds(0, 3)], r_plan + 2)
    net.landed(a.pers.at[0], r_pers)
    head = 2 * z + hb
    length = a.meta[zs, k, pl.ds(2 + sb, 1), :][:, :1]
    decay, moment = (sum(a.meta[i // 2, i % 2, pl.ds(at + head, 1), :] for i in range(8)) for at in (8, 16))
    lanes = lax.broadcasted_iota(jnp.int32, (16, 128), 1).astype(f32)
    decay_at = a.plan[zs, :, :, pl.ds(sb, 1), :].reshape(16, 128)
    moment_at = a.plan[zs, :, :, pl.ds(2 + sb, 1), :].reshape(16, 128)
    decay_pick = jnp.where(decay_at == lanes, 1.0, 0.0)
    moment_pick = jnp.where(moment_at == lanes, 1.0, 0.0)
    retention = jax.nn.sigmoid(jnp.sum(decay_pick * decay, axis=1, keepdims=True))
    momentum = jax.nn.sigmoid(jnp.sum(moment_pick * moment, axis=1, keepdims=True))
    a.rate_f[...] = jnp.broadcast_to(retention, (16, 128))
    a.rate_m[...] = jnp.broadcast_to(momentum, (16, 128))
    pk, pv = a.pers[hb, 0], a.pers[hb, 1]
    places = lax.broadcasted_iota(jnp.int32, (1024, 1), 0).astype(f32)
    live = jnp.where(places < length, 1.0, 0.0)
    a.bias[...] = jnp.broadcast_to(jnp.where(places < length, 0.0, -1e30), (1024, 128))
    early_late = lax.broadcasted_iota(jnp.int32, (256, 256), 0) <= lax.broadcasted_iota(jnp.int32, (256, 256), 1)

    net.landed(a.qkv, r_qkv)
    w_gu.step2()

    def rows_of(n):
        return a.qkv[:, n].reshape(1024, 128)

    q, kk, v = rows_of(0), rows_of(1), rows_of(2)
    a.qa[:, 0:64] = unit_rows(q.astype(f32))[0].astype(bf16).reshape(16, 64, 128)
    a.k_l[...] = (unit_rows(kk.astype(f32))[0] * live).astype(bf16).reshape(16, 64, 128)
    for b in range(16):
        got = tn(a.k_l[b], jnp.concatenate([a.k_l[b], a.qkv[b, 2]], axis=1))
        a.qa[b, 64:192] = got[:, :128].astype(bf16)
        a.outer[b] = got[:, 128:]
    w_o.step3()
    pl.semaphore_wait(cube_sem, 3)
    r_home, r_mq = net.slots(), net.slots()
    home_s = net.s
    net.s += 1
    home_spot = a.mt.at[ds(sb, 64), ds(head, 128)]
    quart_spot = a.mq.at[ds(zs * 2 + sb, 64), ds(hb, 128)]

    def go_home(cc):
        return remote(a.mixed.at[cc], home_spot, ssem.at[home_s], rsem.at[r_home], device(cc, zs, k))

    memory = jnp.zeros((128, 128), f32)
    velocity = jnp.zeros((128, 128), f32)
    for i in range(4):
        for b in range(4 * i, 4 * i + 4):
            low = memory.astype(bf16)
            a.m0[b] = low
            a.s0[b] = velocity.astype(bf16)
            got = nn(a.qa[b], low)
            a.reads[64 * b : 64 * b + 64, :] = got[:64]
            velocity = a.rate_m[b : b + 1, :] * velocity - RATE * (got[64:] - a.outer[b])
            memory = a.rate_f[b : b + 1, :] * memory + velocity
        span = 256 * (i + 1)
        qs = slice(256 * i, span)
        scores = nt(kk[:span], q[qs]) * SCALE + jnp.concatenate([a.bias[:span, :]] * 2, axis=1)
        last = jnp.where(early_late, scores[256 * i :], -1e30)
        scores = jnp.concatenate([scores[: 256 * i], last], axis=0) if i else last
        own_scores = nt(pk, q[qs]) * SCALE
        top = jnp.maximum(
            jnp.max(scores, axis=0, keepdims=True), jnp.max(own_scores, axis=0, keepdims=True)
        )
        e = jnp.exp(scores - top)
        own_e = jnp.exp(own_scores - top)
        total = jnp.sum(e, axis=0, keepdims=True) + jnp.sum(own_e, axis=0, keepdims=True)
        share = 1.0 / total
        p = (e * share).astype(bf16)
        own_p = (own_e * share).astype(bf16)
        a.probs[:span, qs] = p
        a.own[:, qs] = own_p
        att = tn(v[:span], p) + tn(pv, own_p)
        a.mixed[4 * i : 4 * i + 4] = (att.T + a.reads[qs, :]).astype(bf16).reshape(4, 64, 128)
        for row in (i - 1, i) if i % 2 else ():
            for dy in range(4):
                cc = 4 * row + lax.rem(y_at + dy, 4)
                if dy:
                    go_home(cc).start()
                else:
                    stays = same_plane & (x_at == row)

                    @pl.when(stays)
                    def _():
                        net.own(a.mixed.at[cc], home_spot, r_home)

                    @pl.when(jnp.logical_not(stays))
                    def _():
                        go_home(cc).start()

    net.own(a.mixed.at[c], quart_spot, r_mq)
    net.send(
        [
            (a.mixed.at[at_ctx(c, dx, dy)], quart_spot, device(at_ctx(c, dx, dy), z, k))
            for dx, dy in CTX_STEPS
        ],
        a.mixed.at[pl.ds(0, 15)],
        r_mq,
    )
    w_gu.step3()

    w_o.step4()
    net.landed(a.mt, r_home)
    r_nf = net.slots(3)
    xf = a.x[...].astype(f32)
    resid = xf + sum(nn(a.mt[:, ahead(e)], whole(a.wo_all, e)) for e in range(4))
    a.resid[...] = resid
    a.nf_all[z] = (resid * scaled(resid) * gain_two).astype(bf16)
    net.send(
        [(a.nf_all.at[z], a.nf_all.at[z], z_peer(d), r_nf + d - 1) for d in Z_STEPS],
        a.nf_all.at[pl.ds(0, 3)],
        None,
    )
    own_wd.wait()
    own_cot.wait()
    w_gu.step4()
    net.landed(a.gd_r, r_wd)

    def live_chunk(zz):
        at = (lax.broadcasted_iota(jnp.int32, (64, 1), 0) + c * 64).astype(f32)
        return jnp.concatenate(
            [jnp.where(at < a.meta[zz, k, 2 + n : 3 + n, :][:, :1], 1.0, 0.0) for n in range(2)], axis=0
        )

    net.landed(a.cot_all.at[pl.ds(0, 3)], r_cot)
    for zz in range(4):
        od = (a.cot_all[zz].astype(f32) * live_chunk(zz)).astype(bf16)
        a.od_all[zz] = od
    a.dh[...] = nt(a.od_all[...].reshape(512, 1024), a.wd_all[...]).reshape(4, 128, 768)
    r_nfp, r_out = net.slots(), net.slots()
    nfp_s = net.group(a.nf_s.at[pl.ds(0, 3)])
    for group in ((0,), (1, 3), (2,)):
        places = [z_at(-d) for d in group]
        for d in group:
            if d:
                net.landed(a.nf_all.at[0], r_nf + d - 1)

        def stacked(read):
            parts = [read(zz) for zz in places]
            return jnp.concatenate(parts, axis=0) if len(parts) > 1 else parts[0]

        gu = sum(nn(stacked(lambda zz: a.nf_all[zz, :, ahead(e)]), whole(a.wgu_all, e)) for e in range(4))
        dh = stacked(lambda zz: a.dh[zz])
        g, u = gu[:, :768], gu[:, 768:]
        s = jax.nn.sigmoid(g)
        gs = g * s
        hidden = (gs * u).astype(bf16)
        d_gu = jnp.concatenate(
            [(dh * u * (s + gs * (1.0 - s))).astype(bf16), (dh * gs).astype(bf16)], axis=1
        )
        for n, zz in enumerate(places):
            a.hid_all[zz] = hidden[128 * n : 128 * n + 128]
            a.dgu_all[zz] = d_gu[128 * n : 128 * n + 128]
        for e in range(4):
            part = nt(d_gu, whole(a.wgu_all, e))
            for n, d in enumerate(group):
                if d:
                    a.nf_s[places[n], :, ahead(e)] = part[128 * n : 128 * n + 128].astype(bf16)
                else:
                    a.nf_own[:, ahead(e)] = part
        for n, d in enumerate(group):
            if d:
                net.send([(a.nf_s.at[places[n]], a.nf_r.at[d - 1], z_peer(-d))], None, r_nfp, nfp_s)

    r_gu_c, r_gd_c = net.slots(), net.slots()
    net.drain(early)

    def all_rows(ref):
        return ref[...].reshape(512, ref.shape[-1])

    def gu_tile(n, half):
        return tn(a.nf_all[:, :, ds(2 * n + half, 128)].reshape(512, 128), all_rows(a.dgu_all))

    for n in range(4):
        a.stage[n] = gu_tile(n, 1 - k).astype(bf16)
    net.send([(a.stage, a.gu_r, sibling)], a.stage, r_gu_c)
    a.gd[...] = tn(all_rows(a.hid_all), all_rows(a.od_all)).astype(bf16)
    my_rows = pl.ds(pl.multiple_of(k * 352, 32), 352)
    their_rows = pl.ds(pl.multiple_of((1 - k) * 352, 32), 352)
    net.send([(a.gd.at[their_rows, :], a.gd_r, sibling)], a.gd_r, r_gd_c)

    d_nf = a.nf_own[...]
    net.landed(a.nf_r, r_nfp)
    for d in range(3):
        d_nf += a.nf_r[d].astype(f32)
    back, nf_gain = norm_back(a.resid[...], gain_two, d_nf)
    a.nf_gain[...] = nf_gain
    d_resid = a.od_all[z].astype(f32) + back
    a.d_resid[...] = d_resid
    a.dbr_all[z] = d_resid.astype(bf16)
    for e in range(4):
        a.dmix[:, ahead(e)] = nt(a.dbr_all[z], whole(a.wo_all, e)).astype(bf16)
    r_dm, r_dbr = net.slots(), net.slots()
    dm_s = net.s
    net.s += 1
    for d in (*Z_STEPS, 0):
        for n in range(4):
            owner = (n // 2) * 8 + z * 2 + n % 2
            src = a.dmix.at[ds(n % 2, 64), ds(2 * z_at(d) + n // 2, 128)]
            copy = remote(src, a.dm.at[c], ssem.at[dm_s], rsem.at[r_dm], device(owner, z_at(d), k))
            if d:
                copy.start()
            else:

                @pl.when(owner == c)
                def _():
                    net.own(src, a.dm.at[c], r_dm)

                @pl.when(owner != c)
                def _():
                    copy.start()

    for d in Z_STEPS:
        zz = z_at(-d)
        a.out_s[zz] = nn(a.hid_all[zz], a.wd_all[...]).astype(bf16)
    net.landed(a.gu_r, r_gu_c)
    for n in range(4):
        a.gu_1[n] = (gu_tile(n, k) + a.gu_r[n].astype(f32)).astype(bf16)
    net.landed(a.gd_r, r_gd_c)
    a.gd_1[...] = (a.gd[my_rows, :].astype(f32) + a.gd_r[...].astype(f32)).astype(bf16)
    net.landed(a.dm, r_dm)
    ffn = [shared[n] for n in ("gate", "up", "down_a", "down_b")]
    q_w, k_w, val, w_out = (shared[n] for n in ("q", "k", "v", "out"))
    for one in ffn:
        one.step1()
    net.send([(a.dbr_all.at[z], a.dbr_all.at[z], z_peer(d)) for d in Z_STEPS], a.dbr_all.at[pl.ds(0, 3)], r_dbr)

    dm = a.dm[...].reshape(1024, 128)
    a.dk_a[...] = jnp.zeros((1024, 128), f32)
    a.dv_a[...] = jnp.zeros((1024, 128), f32)
    for b in range(16):
        a.read_adj[b] = tn(a.qa[b, 0:64], a.dm[b])
    d_pk = jnp.zeros((16, 128), f32)
    d_pv = jnp.zeros((16, 128), f32)
    adj_m = jnp.zeros((128, 128), f32)
    adj_v = jnp.zeros((128, 128), f32)
    for i in range(4):
        for b in range(15 - 4 * i, 11 - 4 * i, -1):
            total = adj_m + adj_v
            low = total.astype(bf16)
            a.adj[b] = low
            a.gf_rows[b : b + 1, :] = jnp.sum(adj_m * a.m0[b].astype(f32), axis=0, keepdims=True)
            a.gm_rows[b : b + 1, :] = jnp.sum(total * a.s0[b].astype(f32), axis=0, keepdims=True)
            adj_m = a.rate_f[b : b + 1, :] * adj_m - RATE * nn(a.qa[b, 64:192], low) + a.read_adj[b]
            adj_v = a.rate_m[b : b + 1, :] * total
        span = 256 * (i + 1)
        qs = slice(256 * i, span)
        p = a.probs[:span, qs]
        own_p = a.own[:, qs]
        dp = nt(v[:span], dm[qs])
        own_dp = nt(pv, dm[qs])
        pf, own_pf = p.astype(f32), own_p.astype(f32)
        delta = jnp.sum(pf * dp, axis=0, keepdims=True) + jnp.sum(
            own_pf * own_dp, axis=0, keepdims=True
        )
        d_s = (pf * (dp - delta)).astype(bf16)
        own_ds = (own_pf * (own_dp - delta)).astype(bf16)
        dq = tn(kk[:span], d_s) + tn(pk, own_ds)
        a.dq_a[qs, :] = dq.T * SCALE
        a.dk_a[:span, :] += nn(d_s, q[qs]) * SCALE
        a.dv_a[:span, :] += nn(p, dm[qs])
        d_pk += nn(own_ds, q[qs]) * SCALE
        d_pv += nn(own_p, dm[qs])
    a.d_own[0:16, :] = d_pk
    a.d_own[16:32, :] = d_pv

    r_dq, r_dkv = net.slots(), net.slots()
    spots = [at_ctx(c, dx, dy) for dx, dy in CTX_STEPS] + [c]
    dq_s = net.group(a.dqkv.at[pl.ds(0, 15), 0])
    dkv_s = net.group(a.dqkv.at[pl.ds(0, 15), pl.ds(1, 2)])

    def at_home(first, count):
        return a.dq_home.at[pl.ds(first, count), ds(zs * 2 + sb, 64), ds(hb, 128)]

    def send_home(n, b, first, count, r, s):
        src, dst = a.dqkv.at[b, pl.ds(first, count)], at_home(first, count)
        if n == 15:
            net.own(src, dst, r)
        else:
            net.send([(src, dst, device(b, z, k))], None, r, s)

    for b in range(16):
        qf = a.qkv[b, 0].astype(f32)
        d_qu = nt(a.dm[b], a.m0[b])
        rows = slice(64 * b, 64 * b + 64)
        a.dqkv[b, 0] = (a.dq_a[rows, :] + unit_back(qf, unit_rows(qf)[1], d_qu)).astype(bf16)
    for n, b in enumerate(spots):
        send_home(n, b, 0, 1, r_dq, dq_s)
    for b in range(16):
        rows = slice(64 * b, 64 * b + 64)
        total, k_l = a.adj[b], a.k_l[b]
        d_outer = -RATE * nt(total, a.m0[b])
        kf = a.qkv[b, 1].astype(f32)
        sym = (d_outer + d_outer.T).astype(bf16)
        got = nn(k_l, jnp.concatenate([sym, total], axis=1))
        d_kl = got[:, :128] + RATE * nt(a.qkv[b, 2], total)
        a.dqkv[b, 1] = (a.dk_a[rows, :] + unit_back(kf, unit_rows(kf)[1], d_kl * live[rows])).astype(bf16)
        a.dqkv[b, 2] = (a.dv_a[rows, :] + RATE * got[:, 128:]).astype(bf16)
    for n, b in enumerate(spots):
        send_home(n, b, 1, 2, r_dkv, dkv_s)
    d_plan = []
    for rows, rate, pick in ((a.gf_rows, a.rate_f, decay_pick), (a.gm_rows, a.rate_m, moment_pick)):
        total = jnp.sum(rows[...], axis=1, keepdims=True) * rate[...] * (1.0 - rate[...])
        d_plan.append(jnp.sum(pick * total, axis=0, keepdims=True))
    d_decay, d_moment = d_plan

    r_gq, r_gkv, r_go, r_dn, r_sm = net.slots(), net.slots(), net.slots(), net.slots(), net.slots(4)

    def qkv_tile(n, half, first, count):
        return tn(
            a.n_all[:, :, ds(2 * n + half, 128)].reshape(512, 128), a.dq_l[:, 256 * first : 256 * (first + count)]
        )

    net.landed(a.dq_home.at[0], r_dq)
    a.dq_l[:, 0:256] = a.dq_home[0]
    for n in range(4):
        a.gq_s[n, :, 0:256] = qkv_tile(n, 1 - k, 0, 1).astype(bf16)
    spot = pl.ds(0, 256)
    net.send([(a.gq_s.at[:, :, spot], a.gq_r.at[:, :, spot], sibling)], a.gq_s.at[:, :, spot], r_gq)
    for one in ffn:
        one.step2()
    net.landed(a.gq_r.at[:, :, spot], r_gq)
    for n in range(4):
        a.gq_1[n, :, 0:256] = (qkv_tile(n, k, 0, 1) + a.gq_r[n, :, 0:256].astype(f32)).astype(bf16)

    q_w.step1()

    def out_tile(half):
        return tn(a.mq[:, ds(half, 128)], all_rows(a.dbr_all))

    net.landed(a.dbr_all.at[pl.ds(0, 3)], r_dbr)
    net.landed(a.mixed, r_mq)
    a.go_s[...] = out_tile(1 - k).astype(bf16)
    net.send([(a.go_s, a.go_r, sibling)], a.go_s, r_go)
    for one in ffn:
        one.step3()

    net.landed(a.dq_home.at[pl.ds(1, 2)], r_dkv)
    for n in (1, 2):
        a.dq_l[:, 256 * n : 256 * n + 256] = a.dq_home[n]
    for n in range(4):
        a.gq_s[n, :, 256:768] = qkv_tile(n, 1 - k, 1, 2).astype(bf16)
    spot = pl.ds(256, 512)
    net.send([(a.gq_s.at[:, :, spot], a.gq_r.at[:, :, spot], sibling)], a.gq_s.at[:, :, spot], r_gkv)
    gain_grad = jnp.zeros((1, 1024), f32)
    dn_s = net.group(a.dn_s.at[pl.ds(0, 3)])
    for d in (*Z_STEPS, 0):
        zz = z_at(-d)
        for e in range(4):
            a.wide[:, ahead(e)] = nt(a.dq_l[ds(zz, 128), :], whole(a.w_all, e))
        part = a.wide[...]
        if d:
            a.dn_s[zz] = part.astype(bf16)
            net.send([(a.dn_s.at[zz], a.dn_r.at[d - 1], z_peer(-d))], None, r_dn, dn_s)
        else:
            a.nf_own[...] = part
        rows_f = a.x_all[zz].astype(f32)
        gain_grad += jnp.sum(part * (rows_f * scaled(rows_f)), axis=0, keepdims=True)
    net.landed(a.gq_r.at[:, :, spot], r_gkv)
    for n in range(4):
        a.gq_1[n, :, 256:768] = (qkv_tile(n, k, 1, 2) + a.gq_r[n, :, 256:768].astype(f32)).astype(bf16)
    k_w.step1()
    val.step1()
    net.send(
        [(a.out_s.at[z_at(-d)], a.out_r.at[d - 1], z_peer(-d)) for d in Z_STEPS], a.out_s.at[pl.ds(0, 3)], r_out
    )
    for i in range(8):
        columns = slice(128 * i, 128 * i + 128)
        a.gains[i : i + 1, :] = gain_grad[:, columns]
        a.gains[8 + i : 9 + i, :] = a.nf_gain[:, columns]
    head_at = row8 == head
    a.keep[0:32, :] = jnp.where(hb == k, a.d_own[...], 0.0)
    a.give[0:32, :] = jnp.where(hb == k, 0.0, a.d_own[...])
    for ref in (a.keep, a.give):
        ref[32:48, :] = a.gains[...]
        ref[48:56, :] = jnp.where(head_at, d_decay, 0.0)
        ref[56:64, :] = jnp.where(head_at, d_moment, 0.0)
    net.send([(a.give, a.sm_s, sibling)], a.give, r_sm)
    net.landed(a.go_r, r_go)
    a.go_1[...] = (out_tile(k) + a.go_r[...].astype(f32)).astype(bf16)
    w_out.step1()
    q_w.step2()
    net.landed(a.sm_s, r_sm)
    a.sm_x[x_at] = a.keep[...] + a.sm_s[...]
    net.send(
        [(a.sm_x.at[x_at], a.sm_x.at[x_at], along("x", d)) for d in Z_STEPS], a.sm_x.at[pl.ds(0, 3)], r_sm + 1
    )

    k_w.step2()
    val.step2()
    for one in ffn:
        one.step4()
    net.landed(a.sm_x.at[pl.ds(0, 3)], r_sm + 1)
    a.sm_y[y_at] = a.sm_x[0] + a.sm_x[1] + a.sm_x[2] + a.sm_x[3]
    net.send(
        [(a.sm_y.at[y_at], a.sm_y.at[y_at], along("y", d)) for d in Z_STEPS], a.sm_y.at[pl.ds(0, 3)], r_sm + 2
    )
    w_out.step2()
    for one in (q_w, k_w, val):
        one.step3()
    for one in ffn:
        one.step5()
    net.landed(a.sm_y.at[pl.ds(0, 3)], r_sm + 2)
    plane = a.sm_y[0] + a.sm_y[1] + a.sm_y[2] + a.sm_y[3]
    a.small[0:32, :] = plane[0:32]
    a.sm_z[z] = plane[32:64]
    net.send([(a.sm_z.at[z], a.sm_z.at[z], z_peer(d)) for d in Z_STEPS], a.sm_z.at[pl.ds(0, 3)], r_sm + 3)
    w_out.step3()
    for one in (q_w, k_w, val, w_out):
        one.step4()
    d_n = a.nf_own[...]
    net.landed(a.dn_r, r_dn)
    for d in range(3):
        d_n += a.dn_r[d].astype(f32)
    back, _ = norm_back(a.x[...].astype(f32), gain_one, d_n)
    a.input_grad[...] = a.d_resid[...] + back
    for one in (q_w, k_w, val, w_out):
        one.step5()
    out_sum = a.resid[...] + nn(a.hid_all[z], a.wd_all[...])
    net.landed(a.out_r, r_out)
    for d in range(3):
        out_sum += a.out_r[d].astype(f32)
    a.output[...] = out_sum.astype(bf16)
    net.landed(a.sm_z.at[pl.ds(0, 3)], r_sm + 3)
    a.small[32:64, :] = a.sm_z[0] + a.sm_z[1] + a.sm_z[2] + a.sm_z[3]
    for one in (*ffn, w_out, q_w, k_w, val):
        one.step6()
    net.drain()
    assert (net.s, net.r, net.l) == SEMS, (net.s, net.r, net.l)

    for slot, ref in ((home_s, a.mixed), (dm_s, a.dm)):

        @pl.when(same_plane)
        def _():
            size = ref.at[pl.ds(0, 15)]
            remote(size, size, ssem.at[slot], rsem.at[0], here).wait_send()

        @pl.when(jnp.logical_not(same_plane))
        def _():
            remote(ref, ref, ssem.at[slot], rsem.at[0], here).wait_send()


def finish_kernel(*refs):
    ins, outs = refs[:10], refs[10:25]
    buf_in, buf_out, sem_in, sem_out = refs[25:35], refs[35:48], refs[48], refs[49]
    c, z, k = coords()
    f = 2 * z + k
    loads = [pltpu.make_async_copy(ins[n], buf_in[n], sem_in.at[n]) for n in range(10)]
    for copy in (*loads[2:], *loads[:2]):
        copy.start()
    gate, up, q, kk, v, down, w_out, small = buf_in[2:]
    gain1, gq, gk, gv, go, pk, pv, gain2, gg, gu, gd, dec, mom = buf_out
    sent = []

    def store(*indices):
        for n in indices:
            copy = pltpu.make_async_copy(buf_out[n], outs[2 + n], sem_out.at[2 + n])
            copy.start()
            sent.append(copy)

    for at, (src, dst, n) in enumerate(((gate, gg, 8), (up, gu, 9))):
        loads[2 + at].wait()
        for m in range(4):
            dst[:, 704 * m : 704 * m + 704] = src[m, :, 0:704].astype(f32)
        store(n)
    for at, (src, dst, n) in enumerate(((q, gq, 1), (kk, gk, 2), (v, gv, 3))):
        loads[4 + at].wait()
        for m in range(4):
            dst[:, 256 * m : 256 * m + 256] = src[m].astype(f32)
        store(n)
    for at, (src, dst, n) in enumerate(((down, gd, 10), (w_out, go, 4))):
        loads[7 + at].wait()
        dst[...] = src[...].astype(f32)
        store(n)
    loads[9].wait()
    pk[...] = small[0:16, :]
    pv[...] = small[16:32, :]
    gain1[...] = small[pl.ds(32 + f, 1), :]
    gain2[...] = small[pl.ds(40 + f, 1), :]
    eye = lax.broadcasted_iota(jnp.int32, (8, 8), 0) == lax.broadcasted_iota(jnp.int32, (8, 8), 1)
    lane = lax.broadcasted_iota(jnp.int32, (8, 128), 1)
    for ref, at in ((dec, 48), (mom, 56)):
        for r in range(2):
            column = jnp.sum(jnp.where(lane == 2 * f + r, small[at : at + 8, :], 0.0), axis=1, keepdims=True)
            ref[r : r + 1, :] = jnp.sum(jnp.where(eye, column, 0.0), axis=0, keepdims=True)
    store(0, 5, 6, 7, 11, 12)
    for n in range(2):
        loads[n].wait()
        copy = pltpu.make_async_copy(buf_in[n], outs[n], sem_out.at[n])
        copy.start()
        sent.append(copy)
    for copy in sent:
        copy.wait()


def shards(
    inputs, gain_attn, w_query, w_key, w_value, w_out, persist_key, persist_value, gain_ffn,
    w_gate, w_up, w_down, decay_table, momentum_table, lengths, decay_index, momentum_index,
    cotangent,
):
    operands = dict(
        x=inputs.reshape(128, 1024), cot=cotangent.reshape(128, 1024),
        wq=w_query, wk=w_key, wv=w_value, wo=w_out, wg=w_gate, wu=w_up, wd=w_down,
        pk=persist_key, pv=persist_value, ga=gain_attn.reshape(1, 128), gf=gain_ffn.reshape(1, 128),
        dec=decay_table, mom=momentum_table, lens=lengths, didx=decay_index.reshape(2), midx=momentum_index.reshape(2),
    )
    far = {"cot", "wq", "wk", "wv", "wo", "wd"}
    scalars = {"lens", "didx", "midx"}

    def space(name):
        return pl.ANY if name in far else pltpu.SMEM if name in scalars else pltpu.VMEM

    near = {"output", "input_grad", "small"}
    scratch = [pltpu.VMEM(shape, dtype) for shape, dtype in SCRATCH.values()]
    for zdim, block, piece in SHARED.values():
        scratch += shared_shapes(zdim, block, piece)
    scratch += [pltpu.SemaphoreType.DMA((n,)) for n in SEMS]
    scratch += [pltpu.SemaphoreType.REGULAR, pltpu.SemaphoreType.REGULAR, pltpu.SemaphoreType.DMA]
    results = pl.pallas_call(
        layer_kernel,
        out_shape=[jax.ShapeDtypeStruct(s, t) for s, t in OUTPUTS.values()],
        in_specs=[pl.BlockSpec(memory_space=space(n)) for n in INPUTS],
        out_specs=[pl.BlockSpec(memory_space=pltpu.VMEM if n in near else pl.ANY) for n in OUTPUTS],
        scratch_shapes=scratch,
        compiler_params=pltpu.CompilerParams(
            collective_id=1, has_side_effects=True, vmem_limit_bytes=VMEM_LIMIT
        ),
        name="layer",
    )(*[operands[n] for n in INPUTS])
    shapes = [
        (1, 128), (128, 1024), (128, 1024), (128, 1024), (128, 1024), (16, 128), (16, 128), (1, 128),
        (128, 2816), (128, 2816), (352, 1024), (2, 8), (2, 8),
    ]
    far_away = pl.BlockSpec(memory_space=pl.ANY)
    output, input_grad, *grads = pl.pallas_call(
        finish_kernel,
        out_shape=[jax.ShapeDtypeStruct(*OUTPUTS[n]) for n in ("output", "input_grad")]
        + [jax.ShapeDtypeStruct(s, f32) for s in shapes],
        in_specs=[far_away] * 10,
        out_specs=[far_away] * 15,
        scratch_shapes=[pltpu.VMEM(*v) for v in OUTPUTS.values()]
        + [pltpu.VMEM(s, f32) for s in shapes]
        + [pltpu.SemaphoreType.DMA((10,)), pltpu.SemaphoreType.DMA((15,))],
        compiler_params=pltpu.CompilerParams(vmem_limit_bytes=VMEM_LIMIT),
        name="finish",
    )(*results)
    gain1, gq, gk, gv, go, pk, pv, gain2, gg, gu, gd, dec, mom = grads
    return (
        output.reshape(2, 64, 1024), input_grad.reshape(2, 64, 1024), gain1.reshape(128),
        gq, gk, gv, go, pk, pv, gain2.reshape(128), gg, gu, gd, dec, mom,
    )


def solution(mesh):
    rows, cols = P("fsdp", None), P(None, "fsdp")
    tokens = P("fsdp", "ctx", None)
    in_specs = (
        tokens, P("fsdp"), rows, rows, rows, rows, cols, cols, P("fsdp"), rows, rows, rows, rows, rows,
        P("fsdp"), P("fsdp", "ctx"), P("fsdp", "ctx"), tokens,
    )
    out_specs = (
        tokens, tokens, P("fsdp"), rows, rows, rows, rows, cols, cols, P("fsdp"), rows, rows, rows, rows, rows,
    )
    return jax.shard_map(shards, mesh=mesh, in_specs=in_specs, out_specs=out_specs, check_vma=False)
```

```python
import functools

import jax
import jax.numpy as jnp
from jax import lax
from jax.experimental import pallas as pl
from jax.experimental.pallas import tpu as pltpu
from jax.sharding import PartitionSpec as P

MESH = pl.DeviceIdType.MESH
HIGHEST = lax.Precision.HIGHEST
bf16, f32 = jnp.bfloat16, jnp.float32
EPS = 1e-06
RATE = 0.1
SCALE = 128**-0.5
VMEM_LIMIT = 63 << 20
SEMS = (84, 91, 20)


def coords():
    c, f = lax.axis_index("ctx"), lax.axis_index("fsdp")
    return c, lax.div(f, 2), lax.rem(f, 2)


def pair_of(c, z):
    return lax.div(c, 8), lax.rem(lax.div(c, 2) + 8 - z, 4), lax.rem(c, 2)


def at_ctx(c, dx, dy):
    x, y = lax.div(c, 4), lax.rem(c, 4)
    return lax.rem(x + dx, 4) * 4 + lax.rem(y + dy, 4)


CTX_STEPS = [(dx, dy) for dx in range(4) for dy in range(4) if dx or dy]
CTX_STEPS.sort(key=lambda s: -(min(s[0], 4 - s[0]) + min(s[1], 4 - s[1])))
Z_STEPS = (1, 3, 2)


def device(c, z, k):
    return (c, 2 * z + k)


def nn(a, b, precision=None):
    return jnp.dot(a, b, preferred_element_type=f32, precision=precision)


def nt(a, b, precision=None):
    return lax.dot_general(
        a, b, (((1,), (1,)), ((), ())), preferred_element_type=f32, precision=precision
    )


def tn(a, b, precision=None):
    return lax.dot_general(
        a, b, (((0,), (0,)), ((), ())), preferred_element_type=f32, precision=precision
    )


def ds(index, size):
    return pl.ds(pl.multiple_of(index * size, size), size)


def remote(src, dst, ssem, rsem, peer):
    return pltpu.make_async_remote_copy(
        src_ref=src, dst_ref=dst, send_sem=ssem, recv_sem=rsem, device_id=peer, device_id_type=MESH
    )


class Net:
    def __init__(self, ssem, rsem, lsem, here):
        self.ssem, self.rsem, self.lsem, self.here = ssem, rsem, lsem, here
        self.s = self.r = self.l = 0
        self.due = []

    def slots(self, n=1):
        self.r += n
        return self.r - n

    def send(self, moves, size, r, s=None):
        if s is None:
            s = self.group(size)
        for src, dst, peer, *own in moves:
            at = own[0] if own else r
            remote(src, dst, self.ssem.at[s], self.rsem.at[at], peer).start()
        return s

    def group(self, size):
        s = self.s
        self.s += 1
        self.due.append((size, s))
        return s

    def own(self, src, dst, r):
        pltpu.make_async_copy(src, dst, self.rsem.at[r]).start()

    def landed(self, size, r):
        remote(size, size, self.ssem.at[0], self.rsem.at[r], self.here).wait_recv()

    def local(self, src, dst):
        copy = pltpu.make_async_copy(src, dst, self.lsem.at[self.l])
        self.l += 1
        copy.start()
        return copy

    def drain(self, count=None):
        count = len(self.due) if count is None else count
        for size, s in self.due[:count]:
            remote(size, size, self.ssem.at[s], self.rsem.at[0], self.here).wait_send()
        self.due = self.due[count:]


def scaled(values):
    return lax.rsqrt(jnp.mean(values * values, axis=-1, keepdims=True) + EPS)


def norm_back(values, gain, grad):
    r = scaled(values)
    inner = grad * gain
    back = r * inner - (r * r * r) * values * jnp.mean(values * inner, axis=-1, keepdims=True)
    return back, jnp.sum(grad * values * r, axis=0, keepdims=True)


def unit_rows(rows):
    r = lax.rsqrt(jnp.mean(rows * rows, axis=-1, keepdims=True) + EPS)
    return rows * r * SCALE, r


def unit_back(rows, r, grad):
    return SCALE * (r * grad - rows * (r * r * r) * jnp.mean(rows * grad, axis=-1, keepdims=True))


class Shared:
    def __init__(self, net, first, zdim, part1, part2, src, r1, t1, r2, t2, zr, final):
        self.net, self.first, self.zdim = net, first, zdim
        self.part1, self.part2 = part1, part2
        self.src, self.r1, self.t1, self.r2, self.t2, self.zr, self.final = src, r1, t1, r2, t2, zr, final
        self.slot = net.slots(5)

    def place(self, c, z, k):
        x, y = lax.div(c, 4), lax.rem(c, 4)
        self.c, self.z, self.k = c, z, k
        self.i, self.j = (x, y) if self.first == "x" else (y, x)

    def peer(self, second, d):
        along_x = (self.first == "x") != second
        return device(at_ctx(self.c, d if along_x else 0, 0 if along_x else d), self.z, self.k)

    def step1(self):
        self.net.send(
            [
                (self.src.at[self.part1(lax.rem(self.i + d, 4))], self.r1.at[d - 1], self.peer(False, d))
                for d in (2, 1, 3)
            ],
            self.r1,
            self.slot,
        )

    def step2(self):
        self.net.landed(self.r1, self.slot)
        total = self.src[self.part1(self.i)].astype(f32)
        for d in range(3):
            total += self.r1[d].astype(f32)
        self.t1[...] = total.astype(bf16)
        self.net.send(
            [
                (self.t1.at[self.part2(lax.rem(self.j + d, 4))], self.r2.at[d - 1], self.peer(True, d))
                for d in (2, 1, 3)
            ],
            self.r2,
            self.slot + 1,
        )

    def step3(self):
        self.net.landed(self.r2, self.slot + 1)
        total = self.t1[self.part2(self.j)].astype(f32)
        for d in range(3):
            total += self.r2[d].astype(f32)
        self.t2[...] = total.astype(bf16)
        if self.zdim:
            self.zr[self.z] = self.t2[self.z]
            moves = []
            for d in (2, 1, 3):
                zz = lax.rem(self.z + d, 4)
                moves.append((self.t2.at[zz], self.zr.at[self.z], device(self.c, zz, self.k)))
            self.net.send(moves, self.zr.at[pl.ds(0, 3)], self.slot + 2)

    def block(self, i):
        return self.final.at[self.part1_final(i)]

    def piece(self, i, j):
        return self.final.at[self.piece_final(i, j)]

    def step4(self):
        if self.zdim:
            self.net.landed(self.zr.at[pl.ds(0, 3)], self.slot + 2)
        src = self.zr if self.zdim else self.t2
        spot = self.piece(self.i, self.j)
        self.mine = self.net.local(src, spot)
        self.net.send([(src, spot, self.peer(True, d)) for d in (2, 1, 3)], self.r2, self.slot + 3)

    def step5(self):
        self.mine.wait()
        self.net.landed(self.r2, self.slot + 3)
        spot = self.block(self.i)
        self.net.send([(spot, spot, self.peer(False, d)) for d in (2, 1, 3)], self.r1, self.slot + 4)

    def step6(self):
        self.net.landed(self.r1, self.slot + 4)


def shared_shapes(zdim, block, piece):
    lead = (4,) if zdim else ()
    return [
        pltpu.VMEM((3, *lead, *block), bf16),
        pltpu.VMEM((*lead, *block), bf16),
        pltpu.VMEM((3, *lead, *piece), bf16),
        pltpu.VMEM((*lead, *piece), bf16),
        pltpu.VMEM((*lead, *piece), bf16),
    ]


def wide_shared(net, first, column, width, src, scratch, final):
    half = width // 2
    shared = Shared(
        net,
        first,
        True,
        lambda i: (slice(None), ds(i, 32), pl.ds(column, width)),
        lambda j: (slice(None), ds(lax.div(j, 2), 16), ds(lax.rem(j, 2), half)),
        src,
        *scratch,
        final,
    )
    shared.part1_final = lambda i: (slice(None), ds(i, 32), slice(None))
    shared.piece_final = lambda i, j: (
        slice(None),
        ds(2 * i + lax.div(j, 2), 16),
        ds(lax.rem(j, 2), half),
    )
    return shared


def down_shared(net, first, row, rows, src, scratch, final):
    half = rows // 2
    shared = Shared(
        net,
        first,
        False,
        lambda i: (pl.ds(row, rows), ds(i, 256)),
        lambda j: (ds(lax.div(j, 2), half), ds(lax.rem(j, 2), 128)),
        src,
        *scratch,
        final,
    )
    shared.part1_final = shared.part1
    shared.piece_final = lambda i, j: (
        pl.ds(pl.multiple_of(row + lax.div(j, 2) * half, 16), half),
        ds(2 * i + lax.rem(j, 2), 128),
    )
    return shared


def out_shared(net, src, scratch, final):
    shared = Shared(
        net,
        "y",
        False,
        lambda i: (ds(i, 32), slice(None)),
        lambda j: (ds(lax.div(j, 2), 16), ds(lax.rem(j, 2), 512)),
        src,
        *scratch,
        final,
    )
    shared.part1_final = lambda i: (ds(i, 32), slice(None))
    shared.piece_final = lambda i, j: (ds(2 * i + lax.div(j, 2), 16), ds(lax.rem(j, 2), 512))
    return shared


class Weight:
    def __init__(self, net, buf, sources, c, z, k):
        self.net, self.buf, self.sources = net, buf, sources
        self.c, self.z, self.k = c, z, k
        self.half = buf.shape[-1] // 2
        self.slot = net.slots(6)

    def axes(self):
        for n, at in enumerate((lax.div(self.c, 4), lax.rem(self.c, 4))):
            yield n, ds(at, 32), pl.ds(n * self.half, self.half)

    def size(self, rows):
        return self.buf.at[pl.ds(1, 3), 0, pl.ds(0, rows), pl.ds(0, self.half)]

    def step0(self):
        net, k = self.net, self.k
        sibling = device(self.c, self.z, 1 - k)
        for n, rows, _ in self.axes():
            moves = []
            for d in Z_STEPS:
                zz = lax.rem(self.z + d, 4)
                for src, start, column, width in self.sources(zz):
                    if column // self.half == n:
                        spot = self.buf.at[4 - d, k, rows, pl.ds(column, width)]
                        moves.append((src.at[rows, pl.ds(start, width)], spot, device(self.c, zz, k)))
            net.send(moves, self.size(32), self.slot + n)
        self.mine = []
        moves = []
        for src, start, column, width in self.sources(self.z):
            block, spot = src.at[:, pl.ds(start, width)], self.buf.at[0, k, :, pl.ds(column, width)]
            self.mine.append(net.local(block, spot))
            moves.append((block, spot, sibling))
        net.send(moves, self.buf.at[0, k], self.slot + 4)

    def step1(self):
        for n, rows, columns in self.axes():
            self.net.landed(self.size(32), self.slot + n)
            spot = self.buf.at[pl.ds(1, 3), self.k, rows, columns]
            moves = []
            for d in (2, 1, 3):
                peer = device(at_ctx(self.c, 0 if n else d, d if n else 0), self.z, self.k)
                moves.append((spot, spot, peer))
            self.net.send(moves, self.size(96), self.slot + 2 + n)

    def step2(self):
        for n in range(2):
            self.net.landed(self.size(96), self.slot + 2 + n)
        spot = self.buf.at[pl.ds(1, 3), self.k]
        self.net.send([(spot, spot, device(self.c, self.z, 1 - self.k))], spot, self.slot + 5)

    def step3(self):
        for copy in self.mine:
            copy.wait()
        self.net.landed(self.buf.at[0, 0], self.slot + 4)
        self.net.landed(self.buf.at[pl.ds(1, 3), 0], self.slot + 5)


SHARED = dict(
    gate=(True, (32, 768), (16, 384)),
    up=(True, (32, 768), (16, 384)),
    q=(True, (32, 256), (16, 128)),
    k=(True, (32, 256), (16, 128)),
    v=(True, (32, 256), (16, 128)),
    down_a=(False, (192, 256), (96, 128)),
    down_b=(False, (160, 256), (80, 128)),
    out=(False, (32, 1024), (16, 512)),
)

SCRATCH = dict(
    meta=((4, 2, 24, 128), f32),
    plan=((4, 4, 4, 8, 128), f32),
    pers=((2, 2, 16, 128), bf16),
    x_all=((4, 128, 1024), bf16),
    cot_all=((4, 128, 1024), bf16),
    w_ffn=((2, 128, 2816), bf16),
    w_all=((4, 2, 128, 768), bf16),
    wo_all=((4, 2, 128, 1024), bf16),
    stage=((4, 128, 1536), bf16),
    wgu_all=((4, 2, 128, 1536), bf16),
    wide=((128, 1024), f32),
    wd_all=((768, 1024), bf16),
    n_all=((4, 128, 1024), bf16),
    n_t=((8, 128, 512), bf16),
    qkv_s=((3, 512, 256), bf16),
    qkv=((16, 3, 64, 128), bf16),
    probs=((1024, 1024), bf16),
    own=((16, 1024), bf16),
    m0=((16, 128, 128), bf16),
    s0=((16, 128, 128), bf16),
    qa=((16, 192, 128), bf16),
    outer=((16, 128, 128), f32),
    k_l=((16, 64, 128), bf16),
    bias=((1024, 128), f32),
    gf_rows=((16, 128), f32),
    gm_rows=((16, 128), f32),
    rate_f=((16, 128), f32),
    rate_m=((16, 128), f32),
    read_adj=((16, 128, 128), f32),
    reads=((1024, 128), f32),
    mixed=((16, 64, 128), bf16),
    mt=((128, 1024), bf16),
    mq=((512, 256), bf16),
    resid=((128, 1024), f32),
    nf_all=((4, 128, 1024), bf16),
    hid_all=((4, 128, 768), bf16),
    dh=((4, 128, 768), f32),
    dgu_all=((4, 128, 1536), bf16),
    od_all=((4, 128, 1024), bf16),
    nf_own=((128, 1024), f32),
    nf_s=((4, 128, 1024), bf16),
    nf_r=((3, 128, 1024), bf16),
    out_s=((4, 128, 1024), bf16),
    out_r=((3, 128, 1024), bf16),
    d_resid=((128, 1024), f32),
    dbr_all=((4, 128, 1024), bf16),
    dmix=((4, 2, 2, 64, 128), bf16),
    dm=((16, 64, 128), bf16),
    dq_a=((1024, 128), f32),
    dk_a=((1024, 128), f32),
    dv_a=((1024, 128), f32),
    adj=((16, 128, 128), bf16),
    dqkv=((16, 3, 64, 128), bf16),
    dq_home=((3, 512, 256), bf16),
    dq_l=((512, 768), bf16),
    dn_s=((4, 128, 1024), bf16),
    dn_r=((3, 128, 1024), bf16),
    gu_r=((4, 128, 1536), bf16),
    nf_gain=((1, 1024), f32),
    gu_1=((4, 128, 1536), bf16),
    gd=((768, 1024), bf16),
    gd_r=((352, 1024), bf16),
    gd_1=((352, 1024), bf16),
    gq_s=((4, 128, 768), bf16),
    gq_r=((4, 128, 768), bf16),
    gq_1=((4, 128, 768), bf16),
    go_s=((128, 1024), bf16),
    go_r=((128, 1024), bf16),
    go_1=((128, 1024), bf16),
    gains=((16, 128), f32),
    tables=((16, 128), f32),
    d_own=((32, 128), f32),
    keep=((64, 128), f32),
    give=((64, 128), f32),
    sm_s=((64, 128), f32),
    sm_x=((4, 64, 128), f32),
    sm_y=((4, 64, 128), f32),
    sm_z=((4, 32, 128), f32),
)

INPUTS = [
    "x", "cot", "wq", "wk", "wv", "wo", "wg", "wu", "wd", "pk", "pv", "ga", "gf", "dec", "mom",
    "lens", "didx", "midx",
]
OUTPUTS = dict(
    output=((128, 1024), bf16),
    input_grad=((128, 1024), f32),
    f_gate=((4, 128, 768), bf16),
    f_up=((4, 128, 768), bf16),
    f_q=((4, 128, 256), bf16),
    f_k=((4, 128, 256), bf16),
    f_v=((4, 128, 256), bf16),
    f_down=((352, 1024), bf16),
    f_out=((128, 1024), bf16),
    small=((64, 128), f32),
)


class Refs:
    pass


def layer_kernel(*refs):
    names = INPUTS + list(OUTPUTS) + list(SCRATCH)
    a = Refs()
    for name, ref in zip(names, refs):
        setattr(a, name, ref)
    rest = refs[len(names) :]
    ssem, rsem, lsem, plane_sem, cube_sem = rest[-5:]
    c, z, k = coords()
    f = 2 * z + k
    hb, zs, sb = pair_of(c, z)
    x_at, y_at = lax.div(c, 4), lax.rem(c, 4)
    here, sibling = device(c, z, k), device(c, z, 1 - k)
    same_plane = zs == z
    net = Net(ssem, rsem, lsem, here)
    shared = {}
    sources = dict(
        gate=("x", 0, 768, a.gu_1, a.f_gate),
        up=("y", 768, 768, a.gu_1, a.f_up),
        q=("x", 0, 256, a.gq_1, a.f_q),
        k=("x", 256, 256, a.gq_1, a.f_k),
        v=("y", 512, 256, a.gq_1, a.f_v),
    )
    for n, name in enumerate(SHARED):
        scratch = rest[5 * n : 5 * n + 5]
        if name in sources:
            first, column, width, src, final = sources[name]
            shared[name] = wide_shared(net, first, column, width, src, scratch, final)
        elif name == "down_a":
            shared[name] = down_shared(net, "x", 0, 192, a.gd_1, scratch, a.f_down)
        elif name == "down_b":
            shared[name] = down_shared(net, "y", 192, 160, a.gd_1, scratch, a.f_down)
        else:
            shared[name] = out_shared(net, a.go_1, scratch, a.f_out)
        shared[name].place(c, z, k)

    def z_at(d):
        return lax.rem(z + d + 4, 4)

    def z_peer(d):
        return device(c, z_at(d), k)

    barrier = pltpu.get_barrier_semaphore()

    def along(axis, d):
        return device(at_ctx(c, d if axis == "x" else 0, 0 if axis == "x" else d), z, k)

    for d in Z_STEPS:
        for peer in (z_peer(d), along("x", d), along("y", d)):
            pl.semaphore_signal(barrier, inc=1, device_id=peer, device_id_type=MESH)
    pl.semaphore_signal(barrier, inc=1, device_id=sibling, device_id_type=MESH)

    into_ffn = [net.local(w, a.w_ffn.at[n]) for n, w in enumerate((a.wg, a.wu))]

    lane8 = lax.broadcasted_iota(jnp.int32, (8, 128), 1)
    row8 = lax.broadcasted_iota(jnp.int32, (8, 128), 0)
    eye8 = lax.broadcasted_iota(jnp.int32, (8, 8), 0) == lax.broadcasted_iota(jnp.int32, (8, 8), 1)

    def by_head(table):
        placed = jnp.zeros((8, 128), f32)
        for r in range(2):
            row = jnp.broadcast_to(table[r : r + 1, :].astype(f32), (8, 8))
            column = jnp.sum(jnp.where(eye8, row, 0.0), axis=1, keepdims=True)
            placed += jnp.where(lane8 == 2 * f + r, column, 0.0)
        return placed

    head_rows = jnp.where(row8 == 0, a.ga[...].astype(f32), 0.0)
    head_rows = jnp.where(row8 == 1, a.gf[...].astype(f32), head_rows)
    for n in range(2):
        head_rows = jnp.where(row8 == 2 + n, a.lens[n].astype(f32), head_rows)
    a.meta[z, k, 0:8, :] = head_rows
    a.meta[z, k, 8:16, :] = by_head(a.dec[...])
    a.meta[z, k, 16:24, :] = by_head(a.mom[...])
    plan = jnp.zeros((8, 128), f32)
    for n in range(2):
        plan = jnp.where(row8 == n, a.didx[n].astype(f32), plan)
        plan = jnp.where(row8 == 2 + n, a.midx[n].astype(f32), plan)
    a.plan[z, x_at, y_at] = plan
    a.pers[k, 0] = a.pk[...]
    a.pers[k, 1] = a.pv[...]
    a.x_all[z] = a.x[...]

    pl.semaphore_wait(barrier, 10)
    for d in Z_STEPS:
        pl.semaphore_signal(plane_sem, inc=1, device_id=along("y", d), device_id_type=MESH)

    r_meta, r_meta_s, r_x = net.slots(), net.slots(), net.slots(3)
    r_plan, r_pers, r_wd, r_cot = net.slots(3), net.slots(), net.slots(), net.slots()
    def from_qkv(zz):
        start = pl.multiple_of(zz * 256, 256)
        middle = pl.multiple_of(zz * 256 + 128, 128)
        return [
            (a.wq, start, 0, 256), (a.wk, start, 256, 128), (a.wk, middle, 384, 128), (a.wv, start, 512, 256),
        ]

    w_qkv = Weight(net, a.w_all, from_qkv, c, z, k)
    w_o = Weight(net, a.wo_all, lambda zz: [(a.wo, 0, 0, 512), (a.wo, 512, 512, 512)], c, z, k)
    w_gu = Weight(
        net, a.wgu_all, lambda zz: [(a.stage.at[zz], 0, 0, 768), (a.stage.at[zz], 768, 768, 768)], c, z, k
    )
    w_qkv.step0()
    spot = a.meta.at[z, k]
    net.send([(spot, spot, z_peer(d)) for d in Z_STEPS], a.meta.at[pl.ds(0, 3), 0], r_meta)
    spot = a.plan.at[z, x_at, y_at]
    net.send([(spot, spot, along("x", d)) for d in Z_STEPS], a.plan.at[0, 0, pl.ds(0, 3)], r_plan)
    w_qkv.step1()
    net.send(
        [(a.x_all.at[z], a.x_all.at[z], z_peer(d), r_x + d - 1) for d in Z_STEPS], a.x_all.at[pl.ds(0, 3)], None
    )
    w_o.step0()

    def stage_ffn(blocks):
        for n in blocks:
            for m in range(2):
                block = a.w_ffn[m, :, 704 * n : 704 * n + 704]
                a.stage[n, :, 768 * m : 768 * m + 768] = jnp.concatenate(
                    [block, jnp.zeros((128, 64), bf16)], axis=1
                )

    for copy in into_ffn:
        copy.wait()
    stage_ffn((0, 1))
    net.landed(a.meta.at[pl.ds(0, 3), 0], r_meta)
    spot = a.meta.at[:, k]
    net.send([(spot, spot, sibling)], spot, r_meta_s)
    net.landed(a.plan.at[0, 0, pl.ds(0, 3)], r_plan)
    spot = a.plan.at[z, :, y_at]
    net.send([(spot, spot, along("y", d)) for d in Z_STEPS], a.plan.at[0, pl.ds(0, 3)], r_plan + 1)
    w_qkv.step2()
    stage_ffn((2, 3))
    w_gu.step0()
    net.send([(a.pers.at[k], a.pers.at[k], sibling)], a.pers.at[0], r_pers)
    wd_rows = pl.ds(pl.multiple_of(k * 352, 32), 352)
    own_wd = net.local(a.wd, a.wd_all.at[wd_rows, :])
    net.send([(a.wd, a.wd_all.at[wd_rows, :], sibling)], a.gd_r, r_wd)
    a.wd_all[704:768, :] = jnp.zeros((64, 1024), bf16)
    pl.semaphore_wait(plane_sem, 3)
    for d in Z_STEPS:
        pl.semaphore_signal(cube_sem, inc=1, device_id=z_peer(d), device_id_type=MESH)
    net.landed(a.plan.at[0, pl.ds(0, 3)], r_plan + 1)
    net.send([(a.plan.at[z], a.plan.at[z], z_peer(d)) for d in Z_STEPS], a.plan.at[pl.ds(0, 3)], r_plan + 2)
    net.landed(a.meta.at[:, k], r_meta_s)

    def gain_row(n):
        return jnp.concatenate([a.meta[i // 2, i % 2, n : n + 1, :] for i in range(8)], axis=1)

    gain_one, gain_two = gain_row(0), gain_row(1)

    def ahead(e):
        return ds(z_at(e), 256)

    def whole(ref, e):
        return ref[e].reshape(256, ref.shape[-1])

    for d in (0, *Z_STEPS):
        zz = z_at(-d)
        if d:
            net.landed(a.x_all.at[0], r_x + d - 1)
        xf = a.x_all[zz].astype(f32)
        a.n_all[zz] = (xf * scaled(xf) * gain_one).astype(bf16)
    w_qkv.step3()
    for d in (0, *Z_STEPS):
        zz = z_at(-d)
        rows = sum(nn(a.n_all[zz, :, ahead(e)], whole(a.w_all, e)) for e in range(4)).astype(bf16)
        for n in range(3):
            a.qkv_s[n, ds(zz, 128), :] = rows[:, 256 * n : 256 * n + 256]

    r_qkv = net.slots()

    def pair_block(ref, cc):
        hb2, zs2, sb2 = pair_of(cc, z)
        return ref.at[:, ds(zs2 * 2 + sb2, 64), ds(hb2, 128)]

    net.own(pair_block(a.qkv_s, c), a.qkv.at[c], r_qkv)
    net.send(
        [
            (pair_block(a.qkv_s, at_ctx(c, dx, dy)), a.qkv.at[c], device(at_ctx(c, dx, dy), z, k))
            for dx, dy in CTX_STEPS
        ],
        a.qkv.at[pl.ds(0, 15)],
        r_qkv,
    )

    w_o.step1()
    own_cot = net.local(a.cot, a.cot_all.at[z])
    net.send([(a.cot, a.cot_all.at[z], z_peer(d)) for d in Z_STEPS], a.cot_all.at[pl.ds(0, 3)], r_cot)
    early = len(net.due)
    for i in range(8):
        a.n_t[i] = a.n_all[:, :, 128 * i : 128 * i + 128].reshape(512, 128).T

    net.landed(a.plan.at[pl.ds(0, 3)], r_plan + 2)
    net.landed(a.pers.at[0], r_pers)
    head = 2 * z + hb
    length = a.meta[zs, k, pl.ds(2 + sb, 1), :][:, :1]
    decay, moment = (sum(a.meta[i // 2, i % 2, pl.ds(at + head, 1), :] for i in range(8)) for at in (8, 16))
    lanes = lax.broadcasted_iota(jnp.int32, (16, 128), 1).astype(f32)
    decay_at = a.plan[zs, :, :, pl.ds(sb, 1), :].reshape(16, 128)
    moment_at = a.plan[zs, :, :, pl.ds(2 + sb, 1), :].reshape(16, 128)
    decay_pick = jnp.where(decay_at == lanes, 1.0, 0.0)
    moment_pick = jnp.where(moment_at == lanes, 1.0, 0.0)
    retention = jax.nn.sigmoid(jnp.sum(decay_pick * decay, axis=1, keepdims=True))
    momentum = jax.nn.sigmoid(jnp.sum(moment_pick * moment, axis=1, keepdims=True))
    a.rate_f[...] = jnp.broadcast_to(retention, (16, 128))
    a.rate_m[...] = jnp.broadcast_to(momentum, (16, 128))
    pk, pv = a.pers[hb, 0], a.pers[hb, 1]
    places = lax.broadcasted_iota(jnp.int32, (1024, 1), 0).astype(f32)
    live = jnp.where(places < length, 1.0, 0.0)
    a.bias[...] = jnp.broadcast_to(jnp.where(places < length, 0.0, -1e30), (1024, 128))
    early_late = lax.broadcasted_iota(jnp.int32, (256, 256), 0) <= lax.broadcasted_iota(jnp.int32, (256, 256), 1)

    net.landed(a.qkv, r_qkv)

    def rows_of(n):
        return a.qkv[:, n].reshape(1024, 128)

    q, kk, v = rows_of(0), rows_of(1), rows_of(2)
    a.qa[:, 0:64] = unit_rows(q.astype(f32))[0].astype(bf16).reshape(16, 64, 128)
    a.k_l[...] = (unit_rows(kk.astype(f32))[0] * live).astype(bf16).reshape(16, 64, 128)
    for b in range(16):
        got = tn(a.k_l[b], jnp.concatenate([a.k_l[b], a.qkv[b, 2]], axis=1))
        a.qa[b, 64:192] = got[:, :128].astype(bf16)
        a.outer[b] = got[:, 128:]
    w_gu.step1()
    pl.semaphore_wait(cube_sem, 3)
    r_home, r_mq = net.slots(), net.slots()
    home_s = net.s
    net.s += 1
    home_spot = a.mt.at[ds(sb, 64), ds(head, 128)]
    quart_spot = a.mq.at[ds(zs * 2 + sb, 64), ds(hb, 128)]

    def go_home(cc):
        return remote(a.mixed.at[cc], home_spot, ssem.at[home_s], rsem.at[r_home], device(cc, zs, k))

    memory = jnp.zeros((128, 128), f32)
    velocity = jnp.zeros((128, 128), f32)
    for i in range(4):
        for b in range(4 * i, 4 * i + 4):
            low = memory.astype(bf16)
            a.m0[b] = low
            a.s0[b] = velocity.astype(bf16)
            got = nn(a.qa[b], low)
            a.reads[64 * b : 64 * b + 64, :] = got[:64]
            velocity = a.rate_m[b : b + 1, :] * velocity - RATE * (got[64:] - a.outer[b])
            memory = a.rate_f[b : b + 1, :] * memory + velocity
        span = 256 * (i + 1)
        qs = slice(256 * i, span)
        scores = nt(kk[:span], q[qs]) * SCALE + jnp.concatenate([a.bias[:span, :]] * 2, axis=1)
        last = jnp.where(early_late, scores[256 * i :], -1e30)
        scores = jnp.concatenate([scores[: 256 * i], last], axis=0) if i else last
        own_scores = nt(pk, q[qs]) * SCALE
        top = jnp.maximum(
            jnp.max(scores, axis=0, keepdims=True), jnp.max(own_scores, axis=0, keepdims=True)
        )
        e = jnp.exp(scores - top)
        own_e = jnp.exp(own_scores - top)
        total = jnp.sum(e, axis=0, keepdims=True) + jnp.sum(own_e, axis=0, keepdims=True)
        share = 1.0 / total
        p = (e * share).astype(bf16)
        own_p = (own_e * share).astype(bf16)
        a.probs[:span, qs] = p
        a.own[:, qs] = own_p
        att = tn(v[:span], p) + tn(pv, own_p)
        a.mixed[4 * i : 4 * i + 4] = (att.T + a.reads[qs, :]).astype(bf16).reshape(4, 64, 128)
        for row in (i - 1, i) if i % 2 else ():
            for dy in range(4):
                cc = 4 * row + lax.rem(y_at + dy, 4)
                if dy:
                    go_home(cc).start()
                else:
                    stays = same_plane & (x_at == row)

                    @pl.when(stays)
                    def _():
                        net.own(a.mixed.at[cc], home_spot, r_home)

                    @pl.when(jnp.logical_not(stays))
                    def _():
                        go_home(cc).start()

        if i == 1:
            w_o.step2()

    net.own(a.mixed.at[c], quart_spot, r_mq)
    net.send(
        [
            (a.mixed.at[at_ctx(c, dx, dy)], quart_spot, device(at_ctx(c, dx, dy), z, k))
            for dx, dy in CTX_STEPS
        ],
        a.mixed.at[pl.ds(0, 15)],
        r_mq,
    )
    w_gu.step2()

    w_o.step3()
    net.landed(a.mt, r_home)
    r_nf = net.slots(3)
    xf = a.x[...].astype(f32)
    resid = xf + sum(nn(a.mt[:, ahead(e)], whole(a.wo_all, e)) for e in range(4))
    a.resid[...] = resid
    a.nf_all[z] = (resid * scaled(resid) * gain_two).astype(bf16)
    net.send(
        [(a.nf_all.at[z], a.nf_all.at[z], z_peer(d), r_nf + d - 1) for d in (2, 1, 3)],
        a.nf_all.at[pl.ds(0, 3)],
        None,
    )
    own_wd.wait()
    own_cot.wait()
    w_gu.step3()
    net.landed(a.gd_r, r_wd)

    def live_chunk(zz):
        at = (lax.broadcasted_iota(jnp.int32, (64, 1), 0) + c * 64).astype(f32)
        return jnp.concatenate(
            [jnp.where(at < a.meta[zz, k, 2 + n : 3 + n, :][:, :1], 1.0, 0.0) for n in range(2)], axis=0
        )

    net.landed(a.cot_all.at[pl.ds(0, 3)], r_cot)
    for zz in range(4):
        od = (a.cot_all[zz].astype(f32) * live_chunk(zz)).astype(bf16)
        a.od_all[zz] = od
    a.dh[...] = nt(a.od_all[...].reshape(512, 1024), a.wd_all[...]).reshape(4, 128, 768)
    r_nfp, r_out = net.slots(), net.slots()
    nfp_s = net.group(a.nf_s.at[pl.ds(0, 3)])
    for group in ((0,), (2,), (1, 3)):
        places = [z_at(-d) for d in group]
        for d in group:
            if d:
                net.landed(a.nf_all.at[0], r_nf + d - 1)

        def stacked(read):
            parts = [read(zz) for zz in places]
            return jnp.concatenate(parts, axis=0) if len(parts) > 1 else parts[0]

        gu = sum(nn(stacked(lambda zz: a.nf_all[zz, :, ahead(e)]), whole(a.wgu_all, e)) for e in range(4))
        dh = stacked(lambda zz: a.dh[zz])
        g, u = gu[:, :768], gu[:, 768:]
        s = jax.nn.sigmoid(g)
        gs = g * s
        hidden = (gs * u).astype(bf16)
        d_gu = jnp.concatenate(
            [(dh * u * (s + gs * (1.0 - s))).astype(bf16), (dh * gs).astype(bf16)], axis=1
        )
        for n, zz in enumerate(places):
            a.hid_all[zz] = hidden[128 * n : 128 * n + 128]
            a.dgu_all[zz] = d_gu[128 * n : 128 * n + 128]
        for e in range(4):
            part = nt(d_gu, whole(a.wgu_all, e))
            for n, d in enumerate(group):
                if d:
                    a.nf_s[places[n], :, ahead(e)] = part[128 * n : 128 * n + 128].astype(bf16)
                else:
                    a.nf_own[:, ahead(e)] = part
        for n, d in enumerate(group):
            if d:
                net.send([(a.nf_s.at[places[n]], a.nf_r.at[d - 1], z_peer(-d))], None, r_nfp, nfp_s)

    r_gu_c, r_gd_c = net.slots(), net.slots()
    net.drain(early)

    def all_rows(ref):
        return ref[...].reshape(512, ref.shape[-1])

    def gu_tile(n, half):
        return tn(a.nf_all[:, :, ds(2 * n + half, 128)].reshape(512, 128), all_rows(a.dgu_all))

    for n in range(4):
        a.stage[n] = gu_tile(n, 1 - k).astype(bf16)
    net.send([(a.stage, a.gu_r, sibling)], a.stage, r_gu_c)
    a.gd[...] = tn(all_rows(a.hid_all), all_rows(a.od_all)).astype(bf16)
    my_rows = pl.ds(pl.multiple_of(k * 352, 32), 352)
    their_rows = pl.ds(pl.multiple_of((1 - k) * 352, 32), 352)
    net.send([(a.gd.at[their_rows, :], a.gd_r, sibling)], a.gd_r, r_gd_c)

    net.landed(a.gu_r, r_gu_c)
    for n in range(4):
        a.gu_1[n] = (gu_tile(n, k) + a.gu_r[n].astype(f32)).astype(bf16)
    net.landed(a.gd_r, r_gd_c)
    a.gd_1[...] = (a.gd[my_rows, :].astype(f32) + a.gd_r[...].astype(f32)).astype(bf16)

    d_nf = a.nf_own[...]
    net.landed(a.nf_r, r_nfp)
    for d in range(3):
        d_nf += a.nf_r[d].astype(f32)
    back, nf_gain = norm_back(a.resid[...], gain_two, d_nf)
    a.nf_gain[...] = nf_gain
    d_resid = a.od_all[z].astype(f32) + back
    a.d_resid[...] = d_resid
    a.dbr_all[z] = d_resid.astype(bf16)
    for e in range(4):
        part = nt(a.dbr_all[z], whole(a.wo_all, e)).astype(bf16)
        for n in range(4):
            a.dmix[e, n // 2, n % 2] = part[64 * (n % 2) : 64 * (n % 2) + 64, 128 * (n // 2) : 128 * (n // 2) + 128]
    r_dm, r_dbr = net.slots(), net.slots()
    dm_s = net.s
    net.s += 1
    for d in (*Z_STEPS, 0):
        for n in range(4):
            owner = (n // 2) * 8 + lax.rem(z + z_at(d), 4) * 2 + n % 2
            src = a.dmix.at[d, n // 2, n % 2]
            copy = remote(src, a.dm.at[c], ssem.at[dm_s], rsem.at[r_dm], device(owner, z_at(d), k))
            if d:
                copy.start()
            else:

                @pl.when(owner == c)
                def _():
                    net.own(src, a.dm.at[c], r_dm)

                @pl.when(owner != c)
                def _():
                    copy.start()

    ffn = [shared[n] for n in ("gate", "up", "down_a", "down_b")]
    q_w, k_w, val, w_out = (shared[n] for n in ("q", "k", "v", "out"))
    for one in ffn:
        one.step1()
    net.landed(a.dm, r_dm)
    net.send([(a.dbr_all.at[z], a.dbr_all.at[z], z_peer(d)) for d in Z_STEPS], a.dbr_all.at[pl.ds(0, 3)], r_dbr)

    dm = a.dm[...].reshape(1024, 128)
    a.dk_a[...] = jnp.zeros((1024, 128), f32)
    a.dv_a[...] = jnp.zeros((1024, 128), f32)
    for b in range(16):
        a.read_adj[b] = tn(a.qa[b, 0:64], a.dm[b])
    d_pk = jnp.zeros((16, 128), f32)
    d_pv = jnp.zeros((16, 128), f32)
    adj_m = jnp.zeros((128, 128), f32)
    adj_v = jnp.zeros((128, 128), f32)
    for i in range(4):
        for b in range(15 - 4 * i, 11 - 4 * i, -1):
            total = adj_m + adj_v
            low = total.astype(bf16)
            a.adj[b] = low
            a.gf_rows[b : b + 1, :] = jnp.sum(adj_m * a.m0[b].astype(f32), axis=0, keepdims=True)
            a.gm_rows[b : b + 1, :] = jnp.sum(total * a.s0[b].astype(f32), axis=0, keepdims=True)
            adj_m = a.rate_f[b : b + 1, :] * adj_m - RATE * nn(a.qa[b, 64:192], low) + a.read_adj[b]
            adj_v = a.rate_m[b : b + 1, :] * total
        span = 256 * (i + 1)
        qs = slice(256 * i, span)
        p = a.probs[:span, qs]
        own_p = a.own[:, qs]
        dp = nt(v[:span], dm[qs])
        own_dp = nt(pv, dm[qs])
        pf, own_pf = p.astype(f32), own_p.astype(f32)
        delta = jnp.sum(pf * dp, axis=0, keepdims=True) + jnp.sum(
            own_pf * own_dp, axis=0, keepdims=True
        )
        d_s = (pf * (dp - delta)).astype(bf16)
        own_ds = (own_pf * (own_dp - delta)).astype(bf16)
        dq = tn(kk[:span], d_s) + tn(pk, own_ds)
        a.dq_a[qs, :] = dq.T * SCALE
        a.dk_a[:span, :] += nn(d_s, q[qs]) * SCALE
        a.dv_a[:span, :] += nn(p, dm[qs])
        d_pk += nn(own_ds, q[qs]) * SCALE
        d_pv += nn(own_p, dm[qs])
    a.d_own[0:16, :] = d_pk
    a.d_own[16:32, :] = d_pv

    r_dq, r_dkv = net.slots(), net.slots()
    spots = [at_ctx(c, dx, dy) for dx, dy in CTX_STEPS] + [c]
    dq_s = net.group(a.dqkv.at[pl.ds(0, 15), 0])
    dkv_s = net.group(a.dqkv.at[pl.ds(0, 15), pl.ds(1, 2)])

    def at_home(first, count):
        return a.dq_home.at[pl.ds(first, count), ds(zs * 2 + sb, 64), ds(hb, 128)]

    def send_home(n, b, first, count, r, s):
        src, dst = a.dqkv.at[b, pl.ds(first, count)], at_home(first, count)
        if n == 15:
            net.own(src, dst, r)
        else:
            net.send([(src, dst, device(b, z, k))], None, r, s)

    for b in range(16):
        qf = a.qkv[b, 0].astype(f32)
        d_qu = nt(a.dm[b], a.m0[b])
        rows = slice(64 * b, 64 * b + 64)
        a.dqkv[b, 0] = (a.dq_a[rows, :] + unit_back(qf, unit_rows(qf)[1], d_qu)).astype(bf16)
    for n, b in enumerate(spots):
        send_home(n, b, 0, 1, r_dq, dq_s)
    for one in ffn:
        one.step2()
    for b in range(16):
        rows = slice(64 * b, 64 * b + 64)
        total, k_l = a.adj[b], a.k_l[b]
        d_outer = -RATE * nt(total, a.m0[b])
        kf = a.qkv[b, 1].astype(f32)
        sym = (d_outer + d_outer.T).astype(bf16)
        got = nn(k_l, jnp.concatenate([sym, total], axis=1))
        d_kl = got[:, :128] + RATE * nt(a.qkv[b, 2], total)
        a.dqkv[b, 1] = (a.dk_a[rows, :] + unit_back(kf, unit_rows(kf)[1], d_kl * live[rows])).astype(bf16)
        a.dqkv[b, 2] = (a.dv_a[rows, :] + RATE * got[:, 128:]).astype(bf16)
    for n, b in enumerate(spots):
        send_home(n, b, 1, 2, r_dkv, dkv_s)
    d_plan = []
    for rows, rate, pick in ((a.gf_rows, a.rate_f, decay_pick), (a.gm_rows, a.rate_m, moment_pick)):
        total = jnp.sum(rows[...], axis=1, keepdims=True) * rate[...] * (1.0 - rate[...])
        d_plan.append(jnp.sum(pick * total, axis=0, keepdims=True))
    d_decay, d_moment = d_plan

    r_gq, r_gkv, r_go, r_dn, r_sm = net.slots(), net.slots(), net.slots(), net.slots(), net.slots(4)

    def qkv_tile(n, half, first, count):
        return nn(a.n_t[2 * n + half], a.dq_l[:, 256 * first : 256 * (first + count)])

    for one in ffn:
        one.step3()
    for d in Z_STEPS:
        zz = z_at(-d)
        a.out_s[zz] = nn(a.hid_all[zz], a.wd_all[...]).astype(bf16)
    net.send(
        [(a.out_s.at[z_at(-d)], a.out_r.at[d - 1], z_peer(-d)) for d in Z_STEPS], a.out_s.at[pl.ds(0, 3)], r_out
    )
    net.landed(a.dq_home.at[0], r_dq)
    a.dq_l[:, 0:256] = a.dq_home[0]
    for n in range(4):
        a.gq_s[n, :, 0:256] = qkv_tile(n, 1 - k, 0, 1).astype(bf16)
    spot = pl.ds(0, 256)
    net.send([(a.gq_s.at[:, :, spot], a.gq_r.at[:, :, spot], sibling)], a.gq_s.at[:, :, spot], r_gq)

    def out_tile(half):
        return tn(a.mq[:, ds(half, 128)], all_rows(a.dbr_all))

    net.landed(a.dbr_all.at[pl.ds(0, 3)], r_dbr)
    net.landed(a.mixed, r_mq)
    a.go_s[...] = out_tile(1 - k).astype(bf16)
    net.send([(a.go_s, a.go_r, sibling)], a.go_s, r_go)
    for one in ffn:
        one.step4()
    net.landed(a.gq_r.at[:, :, spot], r_gq)
    for n in range(4):
        a.gq_1[n, :, 0:256] = (qkv_tile(n, k, 0, 1) + a.gq_r[n, :, 0:256].astype(f32)).astype(bf16)
    q_w.step1()

    net.landed(a.dq_home.at[pl.ds(1, 2)], r_dkv)
    for n in (1, 2):
        a.dq_l[:, 256 * n : 256 * n + 256] = a.dq_home[n]
    for n in range(4):
        a.gq_s[n, :, 256:768] = qkv_tile(n, 1 - k, 1, 2).astype(bf16)
    spot = pl.ds(256, 512)
    net.send([(a.gq_s.at[:, :, spot], a.gq_r.at[:, :, spot], sibling)], a.gq_s.at[:, :, spot], r_gkv)
    dn_s = net.group(a.dn_s.at[pl.ds(0, 3)])

    def dn_part(zz):
        for e in range(4):
            a.wide[:, ahead(e)] = nt(a.dq_l[ds(zz, 128), :], whole(a.w_all, e))
        part = a.wide[...]
        rows_f = a.x_all[zz].astype(f32)
        return part, jnp.sum(part * (rows_f * scaled(rows_f)), axis=0, keepdims=True)

    gain_grad = jnp.zeros((1, 1024), f32)

    def dn_send(d):
        part, gain = dn_part(z_at(-d))
        a.dn_s[z_at(-d)] = part.astype(bf16)
        net.send([(a.dn_s.at[z_at(-d)], a.dn_r.at[d - 1], z_peer(-d))], None, r_dn, dn_s)
        return gain

    gain_grad += dn_send(2)
    gain_grad += dn_send(1)
    net.landed(a.gq_r.at[:, :, spot], r_gkv)
    for n in range(4):
        a.gq_1[n, :, 256:768] = (qkv_tile(n, k, 1, 2) + a.gq_r[n, :, 256:768].astype(f32)).astype(bf16)
    k_w.step1()
    val.step1()
    for one in ffn:
        one.step5()
    gain_grad += dn_send(3)
    part, gain = dn_part(z)
    a.nf_own[...] = part
    gain_grad += gain
    for i in range(8):
        columns = slice(128 * i, 128 * i + 128)
        a.gains[i : i + 1, :] = gain_grad[:, columns]
        a.gains[8 + i : 9 + i, :] = a.nf_gain[:, columns]
    head_at = row8 == head
    a.keep[0:32, :] = jnp.where(hb == k, a.d_own[...], 0.0)
    a.give[0:32, :] = jnp.where(hb == k, 0.0, a.d_own[...])
    for ref in (a.keep, a.give):
        ref[32:48, :] = a.gains[...]
        ref[48:56, :] = jnp.where(head_at, d_decay, 0.0)
        ref[56:64, :] = jnp.where(head_at, d_moment, 0.0)
    net.send([(a.give, a.sm_s, sibling)], a.give, r_sm)
    net.landed(a.go_r, r_go)
    a.go_1[...] = (out_tile(k) + a.go_r[...].astype(f32)).astype(bf16)
    w_out.step1()
    q_w.step2()
    net.landed(a.sm_s, r_sm)
    a.sm_x[x_at] = a.keep[...] + a.sm_s[...]
    net.send(
        [(a.sm_x.at[x_at], a.sm_x.at[x_at], along("x", d)) for d in Z_STEPS], a.sm_x.at[pl.ds(0, 3)], r_sm + 1
    )

    k_w.step2()
    val.step2()
    out_sum = a.resid[...] + nn(a.hid_all[z], a.wd_all[...])
    net.landed(a.out_r, r_out)
    for d in range(3):
        out_sum += a.out_r[d].astype(f32)
    a.output[...] = out_sum.astype(bf16)
    net.landed(a.sm_x.at[pl.ds(0, 3)], r_sm + 1)
    a.sm_y[y_at] = a.sm_x[0] + a.sm_x[1] + a.sm_x[2] + a.sm_x[3]
    net.send(
        [(a.sm_y.at[y_at], a.sm_y.at[y_at], along("y", d)) for d in Z_STEPS], a.sm_y.at[pl.ds(0, 3)], r_sm + 2
    )
    for one in (q_w, k_w, val):
        one.step3()
    w_out.step2()
    net.landed(a.sm_y.at[pl.ds(0, 3)], r_sm + 2)
    plane = a.sm_y[0] + a.sm_y[1] + a.sm_y[2] + a.sm_y[3]
    a.small[0:32, :] = plane[0:32]
    a.sm_z[z] = plane[32:64]
    net.send([(a.sm_z.at[z], a.sm_z.at[z], z_peer(d)) for d in Z_STEPS], a.sm_z.at[pl.ds(0, 3)], r_sm + 3)
    for one in (q_w, k_w, val):
        one.step4()
    w_out.step3()
    w_out.step4()
    d_n = a.nf_own[...]
    net.landed(a.dn_r, r_dn)
    for d in range(3):
        d_n += a.dn_r[d].astype(f32)
    back, _ = norm_back(a.x[...].astype(f32), gain_one, d_n)
    a.input_grad[...] = a.d_resid[...] + back
    for one in (q_w, k_w, val, w_out):
        one.step5()
    net.landed(a.sm_z.at[pl.ds(0, 3)], r_sm + 3)
    a.small[32:64, :] = a.sm_z[0] + a.sm_z[1] + a.sm_z[2] + a.sm_z[3]
    for one in (*ffn, w_out, q_w, k_w, val):
        one.step6()
    net.drain()
    assert (net.s, net.r, net.l) == SEMS, (net.s, net.r, net.l)

    for slot, ref in ((home_s, a.mixed), (dm_s, a.dm)):

        @pl.when(same_plane)
        def _():
            size = ref.at[pl.ds(0, 15)]
            remote(size, size, ssem.at[slot], rsem.at[0], here).wait_send()

        @pl.when(jnp.logical_not(same_plane))
        def _():
            remote(ref, ref, ssem.at[slot], rsem.at[0], here).wait_send()


def finish_kernel(*refs):
    ins, outs = refs[:10], refs[10:25]
    buf_in, buf_out, sem_in, sem_out = refs[25:35], refs[35:48], refs[48], refs[49]
    c, z, k = coords()
    f = 2 * z + k
    loads = [pltpu.make_async_copy(ins[n], buf_in[n], sem_in.at[n]) for n in range(10)]
    for copy in (*loads[2:], *loads[:2]):
        copy.start()
    gate, up, q, kk, v, down, w_out, small = buf_in[2:]
    gain1, gq, gk, gv, go, pk, pv, gain2, gg, gu, gd, dec, mom = buf_out
    sent = []

    def store(*indices):
        for n in indices:
            copy = pltpu.make_async_copy(buf_out[n], outs[2 + n], sem_out.at[2 + n])
            copy.start()
            sent.append(copy)

    for at, (src, dst, n) in enumerate(((gate, gg, 8), (up, gu, 9))):
        loads[2 + at].wait()
        for m in range(4):
            dst[:, 704 * m : 704 * m + 704] = src[m, :, 0:704].astype(f32)
        store(n)
    for at, (src, dst, n) in enumerate(((q, gq, 1), (kk, gk, 2), (v, gv, 3))):
        loads[4 + at].wait()
        for m in range(4):
            dst[:, 256 * m : 256 * m + 256] = src[m].astype(f32)
        store(n)
    for at, (src, dst, n) in enumerate(((down, gd, 10), (w_out, go, 4))):
        loads[7 + at].wait()
        dst[...] = src[...].astype(f32)
        store(n)
    loads[9].wait()
    pk[...] = small[0:16, :]
    pv[...] = small[16:32, :]
    gain1[...] = small[pl.ds(32 + f, 1), :]
    gain2[...] = small[pl.ds(40 + f, 1), :]
    eye = lax.broadcasted_iota(jnp.int32, (8, 8), 0) == lax.broadcasted_iota(jnp.int32, (8, 8), 1)
    lane = lax.broadcasted_iota(jnp.int32, (8, 128), 1)
    for ref, at in ((dec, 48), (mom, 56)):
        for r in range(2):
            column = jnp.sum(jnp.where(lane == 2 * f + r, small[at : at + 8, :], 0.0), axis=1, keepdims=True)
            ref[r : r + 1, :] = jnp.sum(jnp.where(eye, column, 0.0), axis=0, keepdims=True)
    store(0, 5, 6, 7, 11, 12)
    for n in range(2):
        loads[n].wait()
        copy = pltpu.make_async_copy(buf_in[n], outs[n], sem_out.at[n])
        copy.start()
        sent.append(copy)
    for copy in sent:
        copy.wait()


def shards(
    inputs, gain_attn, w_query, w_key, w_value, w_out, persist_key, persist_value, gain_ffn,
    w_gate, w_up, w_down, decay_table, momentum_table, lengths, decay_index, momentum_index,
    cotangent,
):
    operands = dict(
        x=inputs.reshape(128, 1024), cot=cotangent.reshape(128, 1024),
        wq=w_query, wk=w_key, wv=w_value, wo=w_out, wg=w_gate, wu=w_up, wd=w_down,
        pk=persist_key, pv=persist_value, ga=gain_attn.reshape(1, 128), gf=gain_ffn.reshape(1, 128),
        dec=decay_table, mom=momentum_table, lens=lengths, didx=decay_index.reshape(2), midx=momentum_index.reshape(2),
    )
    far = {"cot", "wq", "wk", "wv", "wo", "wd", "wg", "wu"}
    scalars = {"lens", "didx", "midx"}

    def space(name):
        return pl.ANY if name in far else pltpu.SMEM if name in scalars else pltpu.VMEM

    near = {"output", "input_grad", "small"}
    scratch = [pltpu.VMEM(shape, dtype) for shape, dtype in SCRATCH.values()]
    for zdim, block, piece in SHARED.values():
        scratch += shared_shapes(zdim, block, piece)
    scratch += [pltpu.SemaphoreType.DMA((n,)) for n in SEMS]
    scratch += [pltpu.SemaphoreType.REGULAR, pltpu.SemaphoreType.REGULAR]
    results = pl.pallas_call(
        layer_kernel,
        out_shape=[jax.ShapeDtypeStruct(s, t) for s, t in OUTPUTS.values()],
        in_specs=[pl.BlockSpec(memory_space=space(n)) for n in INPUTS],
        out_specs=[pl.BlockSpec(memory_space=pltpu.VMEM if n in near else pl.ANY) for n in OUTPUTS],
        scratch_shapes=scratch,
        compiler_params=pltpu.CompilerParams(
            collective_id=1, has_side_effects=True, vmem_limit_bytes=VMEM_LIMIT
        ),
        name="layer",
    )(*[operands[n] for n in INPUTS])
    shapes = [
        (1, 128), (128, 1024), (128, 1024), (128, 1024), (128, 1024), (16, 128), (16, 128), (1, 128),
        (128, 2816), (128, 2816), (352, 1024), (2, 8), (2, 8),
    ]
    far_away = pl.BlockSpec(memory_space=pl.ANY)
    output, input_grad, *grads = pl.pallas_call(
        finish_kernel,
        out_shape=[jax.ShapeDtypeStruct(*OUTPUTS[n]) for n in ("output", "input_grad")]
        + [jax.ShapeDtypeStruct(s, f32) for s in shapes],
        in_specs=[far_away] * 10,
        out_specs=[far_away] * 15,
        scratch_shapes=[pltpu.VMEM(*v) for v in OUTPUTS.values()]
        + [pltpu.VMEM(s, f32) for s in shapes]
        + [pltpu.SemaphoreType.DMA((10,)), pltpu.SemaphoreType.DMA((15,))],
        compiler_params=pltpu.CompilerParams(vmem_limit_bytes=VMEM_LIMIT),
        name="finish",
    )(*results)
    gain1, gq, gk, gv, go, pk, pv, gain2, gg, gu, gd, dec, mom = grads
    return (
        output.reshape(2, 64, 1024), input_grad.reshape(2, 64, 1024), gain1.reshape(128),
        gq, gk, gv, go, pk, pv, gain2.reshape(128), gg, gu, gd, dec, mom,
    )


def solution(mesh):
    rows, cols = P("fsdp", None), P(None, "fsdp")
    tokens = P("fsdp", "ctx", None)
    in_specs = (
        tokens, P("fsdp"), rows, rows, rows, rows, cols, cols, P("fsdp"), rows, rows, rows, rows, rows,
        P("fsdp"), P("fsdp", "ctx"), P("fsdp", "ctx"), tokens,
    )
    out_specs = (
        tokens, tokens, P("fsdp"), rows, rows, rows, rows, cols, cols, P("fsdp"), rows, rows, rows, rows, rows,
    )
    return jax.shard_map(shards, mesh=mesh, in_specs=in_specs, out_specs=out_specs, check_vma=False)
```

```python
import functools

import jax
import jax.numpy as jnp
from jax import lax
from jax.experimental import pallas as pl
from jax.experimental.pallas import tpu as pltpu
from jax.sharding import PartitionSpec as P

MESH = pl.DeviceIdType.MESH
HIGHEST = lax.Precision.HIGHEST
bf16, f32 = jnp.bfloat16, jnp.float32
EPS = 1e-06
RATE = 0.1
SCALE = 128**-0.5
VMEM_LIMIT = 63 << 20
SEMS = (84, 91, 22)


def coords():
    c, f = lax.axis_index("ctx"), lax.axis_index("fsdp")
    return c, lax.div(f, 2), lax.rem(f, 2)


def pair_of(c, z):
    return lax.div(c, 8), lax.rem(lax.div(c, 2) + 8 - z, 4), lax.rem(c, 2)


def at_ctx(c, dx, dy):
    x, y = lax.div(c, 4), lax.rem(c, 4)
    return lax.rem(x + dx, 4) * 4 + lax.rem(y + dy, 4)


CTX_STEPS = [(dx, dy) for dx in range(4) for dy in range(4) if dx or dy]
CTX_STEPS.sort(key=lambda s: -(min(s[0], 4 - s[0]) + min(s[1], 4 - s[1])))
Z_STEPS = (1, 3, 2)


def device(c, z, k):
    return (c, 2 * z + k)


def nn(a, b, precision=None):
    return jnp.dot(a, b, preferred_element_type=f32, precision=precision)


def nt(a, b, precision=None):
    return lax.dot_general(
        a, b, (((1,), (1,)), ((), ())), preferred_element_type=f32, precision=precision
    )


def tn(a, b, precision=None):
    return lax.dot_general(
        a, b, (((0,), (0,)), ((), ())), preferred_element_type=f32, precision=precision
    )


def ds(index, size):
    return pl.ds(pl.multiple_of(index * size, size), size)


def remote(src, dst, ssem, rsem, peer):
    return pltpu.make_async_remote_copy(
        src_ref=src, dst_ref=dst, send_sem=ssem, recv_sem=rsem, device_id=peer, device_id_type=MESH
    )


class Net:
    def __init__(self, ssem, rsem, lsem, here):
        self.ssem, self.rsem, self.lsem, self.here = ssem, rsem, lsem, here
        self.s = self.r = self.l = 0
        self.due = []

    def slots(self, n=1):
        self.r += n
        return self.r - n

    def send(self, moves, size, r, s=None):
        if s is None:
            s = self.group(size)
        for src, dst, peer, *own in moves:
            at = own[0] if own else r
            remote(src, dst, self.ssem.at[s], self.rsem.at[at], peer).start()
        return s

    def group(self, size):
        s = self.s
        self.s += 1
        self.due.append((size, s))
        return s

    def own(self, src, dst, r):
        pltpu.make_async_copy(src, dst, self.rsem.at[r]).start()

    def landed(self, size, r):
        remote(size, size, self.ssem.at[0], self.rsem.at[r], self.here).wait_recv()

    def local(self, src, dst):
        copy = pltpu.make_async_copy(src, dst, self.lsem.at[self.l])
        self.l += 1
        copy.start()
        return copy

    def drain(self, count=None):
        count = len(self.due) if count is None else count
        for size, s in self.due[:count]:
            remote(size, size, self.ssem.at[s], self.rsem.at[0], self.here).wait_send()
        self.due = self.due[count:]


def scaled(values):
    return lax.rsqrt(jnp.mean(values * values, axis=-1, keepdims=True) + EPS)


def norm_back(values, gain, grad):
    r = scaled(values)
    inner = grad * gain
    back = r * inner - (r * r * r) * values * jnp.mean(values * inner, axis=-1, keepdims=True)
    return back, jnp.sum(grad * values * r, axis=0, keepdims=True)


def unit_rows(rows):
    r = lax.rsqrt(jnp.mean(rows * rows, axis=-1, keepdims=True) + EPS)
    return rows * r * SCALE, r


def unit_back(rows, r, grad):
    return SCALE * (r * grad - rows * (r * r * r) * jnp.mean(rows * grad, axis=-1, keepdims=True))


class Shared:
    def __init__(self, net, first, zdim, part1, part2, src, r1, t1, r2, t2, zr, final):
        self.net, self.first, self.zdim = net, first, zdim
        self.part1, self.part2 = part1, part2
        self.src, self.r1, self.t1, self.r2, self.t2, self.zr, self.final = src, r1, t1, r2, t2, zr, final
        self.slot = net.slots(5)

    def place(self, c, z, k):
        x, y = lax.div(c, 4), lax.rem(c, 4)
        self.c, self.z, self.k = c, z, k
        self.i, self.j = (x, y) if self.first == "x" else (y, x)

    def peer(self, second, d):
        along_x = (self.first == "x") != second
        return device(at_ctx(self.c, d if along_x else 0, 0 if along_x else d), self.z, self.k)

    def step1(self):
        self.net.send(
            [
                (self.src.at[self.part1(lax.rem(self.i + d, 4))], self.r1.at[d - 1], self.peer(False, d))
                for d in (2, 1, 3)
            ],
            self.r1,
            self.slot,
        )

    def step2(self):
        self.net.landed(self.r1, self.slot)
        total = self.src[self.part1(self.i)].astype(f32)
        for d in range(3):
            total += self.r1[d].astype(f32)
        self.t1[...] = total.astype(bf16)
        self.net.send(
            [
                (self.t1.at[self.part2(lax.rem(self.j + d, 4))], self.r2.at[d - 1], self.peer(True, d))
                for d in (2, 1, 3)
            ],
            self.r2,
            self.slot + 1,
        )

    def step3(self):
        self.net.landed(self.r2, self.slot + 1)
        total = self.t1[self.part2(self.j)].astype(f32)
        for d in range(3):
            total += self.r2[d].astype(f32)
        self.t2[...] = total.astype(bf16)
        if self.zdim:
            self.zr[self.z] = self.t2[self.z]
            moves = []
            for d in (2, 1, 3):
                zz = lax.rem(self.z + d, 4)
                moves.append((self.t2.at[zz], self.zr.at[self.z], device(self.c, zz, self.k)))
            self.net.send(moves, self.zr.at[pl.ds(0, 3)], self.slot + 2)

    def block(self, i):
        return self.final.at[self.part1_final(i)]

    def piece(self, i, j):
        return self.final.at[self.piece_final(i, j)]

    def step4(self):
        if self.zdim:
            self.net.landed(self.zr.at[pl.ds(0, 3)], self.slot + 2)
        src = self.zr if self.zdim else self.t2
        spot = self.piece(self.i, self.j)
        self.mine = self.net.local(src, spot)
        self.net.send([(src, spot, self.peer(True, d)) for d in (2, 1, 3)], self.r2, self.slot + 3)

    def step5(self):
        self.mine.wait()
        self.net.landed(self.r2, self.slot + 3)
        spot = self.block(self.i)
        self.net.send([(spot, spot, self.peer(False, d)) for d in (2, 1, 3)], self.r1, self.slot + 4)

    def step6(self):
        self.net.landed(self.r1, self.slot + 4)


def shared_shapes(zdim, block, piece):
    lead = (4,) if zdim else ()
    return [
        pltpu.VMEM((3, *lead, *block), bf16),
        pltpu.VMEM((*lead, *block), bf16),
        pltpu.VMEM((3, *lead, *piece), bf16),
        pltpu.VMEM((*lead, *piece), bf16),
        pltpu.VMEM((*lead, *piece), bf16),
    ]


def wide_shared(net, first, column, width, src, scratch, final):
    half = width // 2
    shared = Shared(
        net,
        first,
        True,
        lambda i: (slice(None), ds(i, 32), pl.ds(column, width)),
        lambda j: (slice(None), ds(lax.div(j, 2), 16), ds(lax.rem(j, 2), half)),
        src,
        *scratch,
        final,
    )
    shared.part1_final = lambda i: (slice(None), ds(i, 32), slice(None))
    shared.piece_final = lambda i, j: (
        slice(None),
        ds(2 * i + lax.div(j, 2), 16),
        ds(lax.rem(j, 2), half),
    )
    return shared


def down_shared(net, first, row, rows, src, scratch, final):
    half = rows // 2
    shared = Shared(
        net,
        first,
        False,
        lambda i: (pl.ds(row, rows), ds(i, 256)),
        lambda j: (ds(lax.div(j, 2), half), ds(lax.rem(j, 2), 128)),
        src,
        *scratch,
        final,
    )
    shared.part1_final = shared.part1
    shared.piece_final = lambda i, j: (
        pl.ds(pl.multiple_of(row + lax.div(j, 2) * half, 16), half),
        ds(2 * i + lax.rem(j, 2), 128),
    )
    return shared


def out_shared(net, src, scratch, final):
    shared = Shared(
        net,
        "y",
        False,
        lambda i: (ds(i, 32), slice(None)),
        lambda j: (ds(lax.div(j, 2), 16), ds(lax.rem(j, 2), 512)),
        src,
        *scratch,
        final,
    )
    shared.part1_final = lambda i: (ds(i, 32), slice(None))
    shared.piece_final = lambda i, j: (ds(2 * i + lax.div(j, 2), 16), ds(lax.rem(j, 2), 512))
    return shared


class Weight:
    def __init__(self, net, buf, sources, c, z, k):
        self.net, self.buf, self.sources = net, buf, sources
        self.c, self.z, self.k = c, z, k
        self.half = buf.shape[-1] // 2
        self.slot = net.slots(6)

    def axes(self):
        for n, at in enumerate((lax.div(self.c, 4), lax.rem(self.c, 4))):
            yield n, ds(at, 32), pl.ds(n * self.half, self.half)

    def size(self, rows):
        return self.buf.at[pl.ds(1, 3), 0, pl.ds(0, rows), pl.ds(0, self.half)]

    def step0(self):
        net, k = self.net, self.k
        sibling = device(self.c, self.z, 1 - k)
        for n, rows, _ in self.axes():
            moves = []
            for d in Z_STEPS:
                zz = lax.rem(self.z + d, 4)
                for src, start, column, width in self.sources(zz):
                    if column // self.half == n:
                        spot = self.buf.at[4 - d, k, rows, pl.ds(column, width)]
                        moves.append((src.at[rows, pl.ds(start, width)], spot, device(self.c, zz, k)))
            net.send(moves, self.size(32), self.slot + n)
        self.mine = []
        moves = []
        for src, start, column, width in self.sources(self.z):
            block, spot = src.at[:, pl.ds(start, width)], self.buf.at[0, k, :, pl.ds(column, width)]
            self.mine.append(net.local(block, spot))
            moves.append((block, spot, sibling))
        net.send(moves, self.buf.at[0, k], self.slot + 4)

    def step1(self):
        for n, rows, columns in self.axes():
            self.net.landed(self.size(32), self.slot + n)
            spot = self.buf.at[pl.ds(1, 3), self.k, rows, columns]
            moves = []
            for d in (2, 1, 3):
                peer = device(at_ctx(self.c, 0 if n else d, d if n else 0), self.z, self.k)
                moves.append((spot, spot, peer))
            self.net.send(moves, self.size(96), self.slot + 2 + n)

    def step2(self):
        for n in range(2):
            self.net.landed(self.size(96), self.slot + 2 + n)
        spot = self.buf.at[pl.ds(1, 3), self.k]
        self.net.send([(spot, spot, device(self.c, self.z, 1 - self.k))], spot, self.slot + 5)

    def step3(self):
        for copy in self.mine:
            copy.wait()
        self.net.landed(self.buf.at[0, 0], self.slot + 4)
        self.net.landed(self.buf.at[pl.ds(1, 3), 0], self.slot + 5)


SHARED = dict(
    gate=(True, (32, 768), (16, 384)),
    up=(True, (32, 768), (16, 384)),
    q=(True, (32, 256), (16, 128)),
    k=(True, (32, 256), (16, 128)),
    v=(True, (32, 256), (16, 128)),
    down_a=(False, (192, 256), (96, 128)),
    down_b=(False, (160, 256), (80, 128)),
    out=(False, (32, 1024), (16, 512)),
)

SCRATCH = dict(
    meta=((4, 2, 24, 128), f32),
    plan=((4, 4, 4, 8, 128), f32),
    pers=((2, 2, 16, 128), bf16),
    x_all=((4, 128, 1024), bf16),
    cot_all=((4, 128, 1024), bf16),
    w_ffn=((2, 128, 2816), bf16),
    w_all=((4, 2, 128, 768), bf16),
    wo_all=((4, 2, 128, 1024), bf16),
    stage=((4, 128, 1536), bf16),
    wgu_all=((4, 2, 128, 1536), bf16),
    wide=((128, 1024), f32),
    wd_all=((768, 1024), bf16),
    n_all=((4, 128, 1024), bf16),
    n_t=((8, 128, 512), bf16),
    qkv_s=((3, 512, 256), bf16),
    qkv=((16, 3, 64, 128), bf16),
    probs=((1024, 1024), bf16),
    own=((16, 1024), bf16),
    m0=((16, 128, 128), bf16),
    s0=((16, 128, 128), bf16),
    qa=((16, 192, 128), bf16),
    outer=((16, 128, 128), f32),
    k_l=((16, 64, 128), bf16),
    bias=((1024, 128), f32),
    gf_rows=((16, 128), f32),
    gm_rows=((16, 128), f32),
    rate_f=((16, 128), f32),
    rate_m=((16, 128), f32),
    read_adj=((16, 128, 128), f32),
    reads=((1024, 128), f32),
    mixed=((16, 64, 128), bf16),
    mt=((128, 1024), bf16),
    mq=((512, 256), bf16),
    resid=((128, 1024), f32),
    nf_all=((4, 128, 1024), bf16),
    hid_all=((4, 128, 768), bf16),
    dh=((4, 128, 768), f32),
    dgu_all=((4, 128, 1536), bf16),
    od_all=((4, 128, 1024), bf16),
    nf_own=((128, 1024), f32),
    nf_s=((4, 128, 1024), bf16),
    nf_r=((3, 128, 1024), bf16),
    out_s=((4, 128, 1024), bf16),
    out_r=((3, 128, 1024), bf16),
    d_resid=((128, 1024), f32),
    out_v=((128, 1024), bf16),
    dbr_all=((4, 128, 1024), bf16),
    dmix=((4, 2, 2, 64, 128), bf16),
    dm=((16, 64, 128), bf16),
    dq_a=((1024, 128), f32),
    dk_a=((1024, 128), f32),
    dv_a=((1024, 128), f32),
    adj=((16, 128, 128), bf16),
    dqkv=((16, 3, 64, 128), bf16),
    dq_home=((3, 512, 256), bf16),
    dq_l=((512, 768), bf16),
    dn_s=((4, 128, 1024), bf16),
    dn_r=((3, 128, 1024), bf16),
    gu_r=((4, 128, 1536), bf16),
    nf_gain=((1, 1024), f32),
    gu_1=((4, 128, 1536), bf16),
    gd=((768, 1024), bf16),
    gd_r=((352, 1024), bf16),
    gd_1=((352, 1024), bf16),
    gq_s=((4, 128, 768), bf16),
    gq_r=((4, 128, 768), bf16),
    gq_1=((4, 128, 768), bf16),
    go_s=((128, 1024), bf16),
    go_r=((128, 1024), bf16),
    go_1=((128, 1024), bf16),
    gains=((16, 128), f32),
    tables=((16, 128), f32),
    d_own=((32, 128), f32),
    keep=((64, 128), f32),
    give=((64, 128), f32),
    sm_s=((64, 128), f32),
    sm_x=((4, 64, 128), f32),
    sm_y=((4, 64, 128), f32),
    sm_z=((4, 32, 128), f32),
)

INPUTS = [
    "x", "cot", "wq", "wk", "wv", "wo", "wg", "wu", "wd", "pk", "pv", "ga", "gf", "dec", "mom",
    "lens", "didx", "midx",
]
OUTPUTS = dict(
    output=((128, 1024), bf16),
    input_grad=((128, 1024), f32),
    f_gate=((4, 128, 768), bf16),
    f_up=((4, 128, 768), bf16),
    f_q=((4, 128, 256), bf16),
    f_k=((4, 128, 256), bf16),
    f_v=((4, 128, 256), bf16),
    f_down=((352, 1024), bf16),
    f_out=((128, 1024), bf16),
    small=((64, 128), f32),
)


class Refs:
    pass


def layer_kernel(*refs):
    names = INPUTS + list(OUTPUTS) + list(SCRATCH)
    a = Refs()
    for name, ref in zip(names, refs):
        setattr(a, name, ref)
    rest = refs[len(names) :]
    ssem, rsem, lsem, plane_sem, cube_sem = rest[-5:]
    c, z, k = coords()
    f = 2 * z + k
    hb, zs, sb = pair_of(c, z)
    x_at, y_at = lax.div(c, 4), lax.rem(c, 4)
    here, sibling = device(c, z, k), device(c, z, 1 - k)
    same_plane = zs == z
    net = Net(ssem, rsem, lsem, here)
    shared = {}
    sources = dict(
        gate=("x", 0, 768, a.gu_1, a.f_gate),
        up=("y", 768, 768, a.gu_1, a.f_up),
        q=("x", 0, 256, a.gq_1, a.f_q),
        k=("x", 256, 256, a.gq_1, a.f_k),
        v=("y", 512, 256, a.gq_1, a.f_v),
    )
    for n, name in enumerate(SHARED):
        scratch = rest[5 * n : 5 * n + 5]
        if name in sources:
            first, column, width, src, final = sources[name]
            shared[name] = wide_shared(net, first, column, width, src, scratch, final)
        elif name == "down_a":
            shared[name] = down_shared(net, "x", 0, 192, a.gd_1, scratch, a.f_down)
        elif name == "down_b":
            shared[name] = down_shared(net, "y", 192, 160, a.gd_1, scratch, a.f_down)
        else:
            shared[name] = out_shared(net, a.go_1, scratch, a.f_out)
        shared[name].place(c, z, k)

    def z_at(d):
        return lax.rem(z + d + 4, 4)

    def z_peer(d):
        return device(c, z_at(d), k)

    barrier = pltpu.get_barrier_semaphore()

    def along(axis, d):
        return device(at_ctx(c, d if axis == "x" else 0, 0 if axis == "x" else d), z, k)

    for d in Z_STEPS:
        for peer in (z_peer(d), along("x", d), along("y", d)):
            pl.semaphore_signal(barrier, inc=1, device_id=peer, device_id_type=MESH)
    pl.semaphore_signal(barrier, inc=1, device_id=sibling, device_id_type=MESH)

    into_ffn = [net.local(w, a.w_ffn.at[n]) for n, w in enumerate((a.wg, a.wu))]

    lane8 = lax.broadcasted_iota(jnp.int32, (8, 128), 1)
    row8 = lax.broadcasted_iota(jnp.int32, (8, 128), 0)
    eye8 = lax.broadcasted_iota(jnp.int32, (8, 8), 0) == lax.broadcasted_iota(jnp.int32, (8, 8), 1)

    def by_head(table):
        placed = jnp.zeros((8, 128), f32)
        for r in range(2):
            row = jnp.broadcast_to(table[r : r + 1, :].astype(f32), (8, 8))
            column = jnp.sum(jnp.where(eye8, row, 0.0), axis=1, keepdims=True)
            placed += jnp.where(lane8 == 2 * f + r, column, 0.0)
        return placed

    head_rows = jnp.where(row8 == 0, a.ga[...].astype(f32), 0.0)
    head_rows = jnp.where(row8 == 1, a.gf[...].astype(f32), head_rows)
    for n in range(2):
        head_rows = jnp.where(row8 == 2 + n, a.lens[n].astype(f32), head_rows)
    a.meta[z, k, 0:8, :] = head_rows
    a.meta[z, k, 8:16, :] = by_head(a.dec[...])
    a.meta[z, k, 16:24, :] = by_head(a.mom[...])
    plan = jnp.zeros((8, 128), f32)
    for n in range(2):
        plan = jnp.where(row8 == n, a.didx[n].astype(f32), plan)
        plan = jnp.where(row8 == 2 + n, a.midx[n].astype(f32), plan)
    a.plan[z, x_at, y_at] = plan
    a.pers[k, 0] = a.pk[...]
    a.pers[k, 1] = a.pv[...]
    a.x_all[z] = a.x[...]

    pl.semaphore_wait(barrier, 10)
    for d in Z_STEPS:
        pl.semaphore_signal(plane_sem, inc=1, device_id=along("y", d), device_id_type=MESH)

    r_meta, r_meta_s, r_x = net.slots(), net.slots(), net.slots(3)
    r_plan, r_pers, r_wd, r_cot = net.slots(3), net.slots(), net.slots(), net.slots()
    def from_qkv(zz):
        start = pl.multiple_of(zz * 256, 256)
        middle = pl.multiple_of(zz * 256 + 128, 128)
        return [
            (a.wq, start, 0, 256), (a.wk, start, 256, 128), (a.wk, middle, 384, 128), (a.wv, start, 512, 256),
        ]

    w_qkv = Weight(net, a.w_all, from_qkv, c, z, k)
    w_o = Weight(net, a.wo_all, lambda zz: [(a.wo, 0, 0, 512), (a.wo, 512, 512, 512)], c, z, k)
    w_gu = Weight(
        net, a.wgu_all, lambda zz: [(a.stage.at[zz], 0, 0, 768), (a.stage.at[zz], 768, 768, 768)], c, z, k
    )
    w_qkv.step0()
    spot = a.meta.at[z, k]
    net.send([(spot, spot, z_peer(d)) for d in Z_STEPS], a.meta.at[pl.ds(0, 3), 0], r_meta)
    spot = a.plan.at[z, x_at, y_at]
    net.send([(spot, spot, along("x", d)) for d in Z_STEPS], a.plan.at[0, 0, pl.ds(0, 3)], r_plan)
    w_qkv.step1()
    net.send(
        [(a.x_all.at[z], a.x_all.at[z], z_peer(d), r_x + d - 1) for d in Z_STEPS], a.x_all.at[pl.ds(0, 3)], None
    )
    w_o.step0()

    def stage_ffn(blocks):
        for n in blocks:
            for m in range(2):
                block = a.w_ffn[m, :, 704 * n : 704 * n + 704]
                a.stage[n, :, 768 * m : 768 * m + 768] = jnp.concatenate(
                    [block, jnp.zeros((128, 64), bf16)], axis=1
                )

    net.landed(a.meta.at[pl.ds(0, 3), 0], r_meta)
    spot = a.meta.at[:, k]
    net.send([(spot, spot, sibling)], spot, r_meta_s)
    net.landed(a.plan.at[0, 0, pl.ds(0, 3)], r_plan)
    spot = a.plan.at[z, :, y_at]
    net.send([(spot, spot, along("y", d)) for d in Z_STEPS], a.plan.at[0, pl.ds(0, 3)], r_plan + 1)
    w_qkv.step2()
    net.send([(a.pers.at[k], a.pers.at[k], sibling)], a.pers.at[0], r_pers)
    wd_rows = pl.ds(pl.multiple_of(k * 352, 32), 352)
    own_wd = net.local(a.wd, a.wd_all.at[wd_rows, :])
    net.send([(a.wd, a.wd_all.at[wd_rows, :], sibling)], a.gd_r, r_wd)
    a.wd_all[704:768, :] = jnp.zeros((64, 1024), bf16)
    pl.semaphore_wait(plane_sem, 3)
    for d in Z_STEPS:
        pl.semaphore_signal(cube_sem, inc=1, device_id=z_peer(d), device_id_type=MESH)
    net.landed(a.plan.at[0, pl.ds(0, 3)], r_plan + 1)
    net.send([(a.plan.at[z], a.plan.at[z], z_peer(d)) for d in Z_STEPS], a.plan.at[pl.ds(0, 3)], r_plan + 2)
    net.landed(a.meta.at[:, k], r_meta_s)

    def gain_row(n):
        return jnp.concatenate([a.meta[i // 2, i % 2, n : n + 1, :] for i in range(8)], axis=1)

    gain_one, gain_two = gain_row(0), gain_row(1)

    def ahead(e):
        return ds(z_at(e), 256)

    def whole(ref, e):
        return ref[e].reshape(256, ref.shape[-1])

    for d in (0, *Z_STEPS):
        zz = z_at(-d)
        if d:
            net.landed(a.x_all.at[0], r_x + d - 1)
        xf = a.x_all[zz].astype(f32)
        a.n_all[zz] = (xf * scaled(xf) * gain_one).astype(bf16)
    w_qkv.step3()
    for d in (0, *Z_STEPS):
        zz = z_at(-d)
        rows = sum(nn(a.n_all[zz, :, ahead(e)], whole(a.w_all, e)) for e in range(4)).astype(bf16)
        for n in range(3):
            a.qkv_s[n, ds(zz, 128), :] = rows[:, 256 * n : 256 * n + 256]

    r_qkv = net.slots()

    def pair_block(ref, cc):
        hb2, zs2, sb2 = pair_of(cc, z)
        return ref.at[:, ds(zs2 * 2 + sb2, 64), ds(hb2, 128)]

    net.own(pair_block(a.qkv_s, c), a.qkv.at[c], r_qkv)
    net.send(
        [
            (pair_block(a.qkv_s, at_ctx(c, dx, dy)), a.qkv.at[c], device(at_ctx(c, dx, dy), z, k))
            for dx, dy in CTX_STEPS
        ],
        a.qkv.at[pl.ds(0, 15)],
        r_qkv,
    )

    w_o.step1()
    for copy in into_ffn:
        copy.wait()
    stage_ffn(range(4))
    w_gu.step0()
    own_cot = net.local(a.cot, a.cot_all.at[z])
    net.send([(a.cot, a.cot_all.at[z], z_peer(d)) for d in Z_STEPS], a.cot_all.at[pl.ds(0, 3)], r_cot)
    early = len(net.due)
    for i in range(8):
        a.n_t[i] = a.n_all[:, :, 128 * i : 128 * i + 128].reshape(512, 128).T

    net.landed(a.plan.at[pl.ds(0, 3)], r_plan + 2)
    net.landed(a.pers.at[0], r_pers)
    head = 2 * z + hb
    length = a.meta[zs, k, pl.ds(2 + sb, 1), :][:, :1]
    decay, moment = (sum(a.meta[i // 2, i % 2, pl.ds(at + head, 1), :] for i in range(8)) for at in (8, 16))
    lanes = lax.broadcasted_iota(jnp.int32, (16, 128), 1).astype(f32)
    decay_at = a.plan[zs, :, :, pl.ds(sb, 1), :].reshape(16, 128)
    moment_at = a.plan[zs, :, :, pl.ds(2 + sb, 1), :].reshape(16, 128)
    decay_pick = jnp.where(decay_at == lanes, 1.0, 0.0)
    moment_pick = jnp.where(moment_at == lanes, 1.0, 0.0)
    retention = jax.nn.sigmoid(jnp.sum(decay_pick * decay, axis=1, keepdims=True))
    momentum = jax.nn.sigmoid(jnp.sum(moment_pick * moment, axis=1, keepdims=True))
    a.rate_f[...] = jnp.broadcast_to(retention, (16, 128))
    a.rate_m[...] = jnp.broadcast_to(momentum, (16, 128))
    pk, pv = a.pers[hb, 0], a.pers[hb, 1]
    places = lax.broadcasted_iota(jnp.int32, (1024, 1), 0).astype(f32)
    live = jnp.where(places < length, 1.0, 0.0)
    a.bias[...] = jnp.broadcast_to(jnp.where(places < length, 0.0, -1e30), (1024, 128))
    early_late = lax.broadcasted_iota(jnp.int32, (256, 256), 0) <= lax.broadcasted_iota(jnp.int32, (256, 256), 1)

    net.landed(a.qkv, r_qkv)

    def rows_of(n):
        return a.qkv[:, n].reshape(1024, 128)

    q, kk, v = rows_of(0), rows_of(1), rows_of(2)
    a.qa[:, 0:64] = unit_rows(q.astype(f32))[0].astype(bf16).reshape(16, 64, 128)
    a.k_l[...] = (unit_rows(kk.astype(f32))[0] * live).astype(bf16).reshape(16, 64, 128)
    for b in range(16):
        got = tn(a.k_l[b], jnp.concatenate([a.k_l[b], a.qkv[b, 2]], axis=1))
        a.qa[b, 64:192] = got[:, :128].astype(bf16)
        a.outer[b] = got[:, 128:]
    w_gu.step1()
    pl.semaphore_wait(cube_sem, 3)
    r_home, r_mq = net.slots(), net.slots()
    home_s = net.s
    net.s += 1
    home_spot = a.mt.at[ds(sb, 64), ds(head, 128)]
    quart_spot = a.mq.at[ds(zs * 2 + sb, 64), ds(hb, 128)]

    def go_home(cc):
        return remote(a.mixed.at[cc], home_spot, ssem.at[home_s], rsem.at[r_home], device(cc, zs, k))

    memory = jnp.zeros((128, 128), f32)
    velocity = jnp.zeros((128, 128), f32)
    for i in range(4):
        for b in range(4 * i, 4 * i + 4):
            low = memory.astype(bf16)
            a.m0[b] = low
            a.s0[b] = velocity.astype(bf16)
            got = nn(a.qa[b], low)
            a.reads[64 * b : 64 * b + 64, :] = got[:64]
            velocity = a.rate_m[b : b + 1, :] * velocity - RATE * (got[64:] - a.outer[b])
            memory = a.rate_f[b : b + 1, :] * memory + velocity
        span = 256 * (i + 1)
        qs = slice(256 * i, span)
        scores = nt(kk[:span], q[qs]) * SCALE + jnp.concatenate([a.bias[:span, :]] * 2, axis=1)
        last = jnp.where(early_late, scores[256 * i :], -1e30)
        scores = jnp.concatenate([scores[: 256 * i], last], axis=0) if i else last
        own_scores = nt(pk, q[qs]) * SCALE
        top = jnp.maximum(
            jnp.max(scores, axis=0, keepdims=True), jnp.max(own_scores, axis=0, keepdims=True)
        )
        e = jnp.exp(scores - top)
        own_e = jnp.exp(own_scores - top)
        total = jnp.sum(e, axis=0, keepdims=True) + jnp.sum(own_e, axis=0, keepdims=True)
        share = 1.0 / total
        p = (e * share).astype(bf16)
        own_p = (own_e * share).astype(bf16)
        a.probs[:span, qs] = p
        a.own[:, qs] = own_p
        att = tn(v[:span], p) + tn(pv, own_p)
        a.mixed[4 * i : 4 * i + 4] = (att.T + a.reads[qs, :]).astype(bf16).reshape(4, 64, 128)
        for row in (i - 1, i) if i % 2 else ():
            for dy in range(4):
                cc = 4 * row + lax.rem(y_at + dy, 4)
                if dy:
                    go_home(cc).start()
                else:
                    stays = same_plane & (x_at == row)

                    @pl.when(stays)
                    def _():
                        net.own(a.mixed.at[cc], home_spot, r_home)

                    @pl.when(jnp.logical_not(stays))
                    def _():
                        go_home(cc).start()

        if i == 1:
            w_o.step2()

    w_o.step3()
    net.landed(a.mt, r_home)
    r_nf = net.slots(3)
    xf = a.x[...].astype(f32)
    resid = xf + sum(nn(a.mt[:, ahead(e)], whole(a.wo_all, e)) for e in range(4))
    a.resid[...] = resid
    a.nf_all[z] = (resid * scaled(resid) * gain_two).astype(bf16)
    net.send(
        [(a.nf_all.at[z], a.nf_all.at[z], z_peer(d), r_nf + d - 1) for d in (2, 1, 3)],
        a.nf_all.at[pl.ds(0, 3)],
        None,
    )
    net.own(a.mixed.at[c], quart_spot, r_mq)
    net.send(
        [
            (a.mixed.at[at_ctx(c, dx, dy)], quart_spot, device(at_ctx(c, dx, dy), z, k))
            for dx, dy in CTX_STEPS
        ],
        a.mixed.at[pl.ds(0, 15)],
        r_mq,
    )
    w_gu.step2()
    own_wd.wait()
    own_cot.wait()
    w_gu.step3()
    net.landed(a.gd_r, r_wd)

    def live_chunk(zz):
        at = (lax.broadcasted_iota(jnp.int32, (64, 1), 0) + c * 64).astype(f32)
        return jnp.concatenate(
            [jnp.where(at < a.meta[zz, k, 2 + n : 3 + n, :][:, :1], 1.0, 0.0) for n in range(2)], axis=0
        )

    net.landed(a.cot_all.at[pl.ds(0, 3)], r_cot)
    for zz in range(4):
        od = (a.cot_all[zz].astype(f32) * live_chunk(zz)).astype(bf16)
        a.od_all[zz] = od
    a.dh[...] = nt(a.od_all[...].reshape(512, 1024), a.wd_all[...]).reshape(4, 128, 768)
    r_nfp, r_out = net.slots(), net.slots()
    nfp_s = net.group(a.nf_s.at[pl.ds(0, 3)])
    for group in ((0,), (2,), (1, 3)):
        places = [z_at(-d) for d in group]
        for d in group:
            if d:
                net.landed(a.nf_all.at[0], r_nf + d - 1)

        def stacked(read):
            parts = [read(zz) for zz in places]
            return jnp.concatenate(parts, axis=0) if len(parts) > 1 else parts[0]

        gu = sum(nn(stacked(lambda zz: a.nf_all[zz, :, ahead(e)]), whole(a.wgu_all, e)) for e in range(4))
        dh = stacked(lambda zz: a.dh[zz])
        g, u = gu[:, :768], gu[:, 768:]
        s = jax.nn.sigmoid(g)
        gs = g * s
        hidden = (gs * u).astype(bf16)
        d_gu = jnp.concatenate(
            [(dh * u * (s + gs * (1.0 - s))).astype(bf16), (dh * gs).astype(bf16)], axis=1
        )
        for n, zz in enumerate(places):
            a.hid_all[zz] = hidden[128 * n : 128 * n + 128]
            a.dgu_all[zz] = d_gu[128 * n : 128 * n + 128]
        for e in range(4):
            part = nt(d_gu, whole(a.wgu_all, e))
            for n, d in enumerate(group):
                if d:
                    a.nf_s[places[n], :, ahead(e)] = part[128 * n : 128 * n + 128].astype(bf16)
                else:
                    a.nf_own[:, ahead(e)] = part
        for n, d in enumerate(group):
            if d:
                net.send([(a.nf_s.at[places[n]], a.nf_r.at[d - 1], z_peer(-d))], None, r_nfp, nfp_s)

    r_gu_c, r_gd_c = net.slots(), net.slots()
    net.drain(early)

    def all_rows(ref):
        return ref[...].reshape(512, ref.shape[-1])

    def gu_tile(n, half):
        return tn(a.nf_all[:, :, ds(2 * n + half, 128)].reshape(512, 128), all_rows(a.dgu_all))

    for n in range(4):
        a.stage[n] = gu_tile(n, 1 - k).astype(bf16)
    net.send([(a.stage, a.gu_r, sibling)], a.stage, r_gu_c)
    a.gd[...] = tn(all_rows(a.hid_all), all_rows(a.od_all)).astype(bf16)
    my_rows = pl.ds(pl.multiple_of(k * 352, 32), 352)
    their_rows = pl.ds(pl.multiple_of((1 - k) * 352, 32), 352)
    net.send([(a.gd.at[their_rows, :], a.gd_r, sibling)], a.gd_r, r_gd_c)

    net.landed(a.gu_r, r_gu_c)
    for n in range(4):
        a.gu_1[n] = (gu_tile(n, k) + a.gu_r[n].astype(f32)).astype(bf16)
    net.landed(a.gd_r, r_gd_c)
    a.gd_1[...] = (a.gd[my_rows, :].astype(f32) + a.gd_r[...].astype(f32)).astype(bf16)

    d_nf = a.nf_own[...]
    net.landed(a.nf_r, r_nfp)
    for d in range(3):
        d_nf += a.nf_r[d].astype(f32)
    back, nf_gain = norm_back(a.resid[...], gain_two, d_nf)
    a.nf_gain[...] = nf_gain
    d_resid = a.od_all[z].astype(f32) + back
    a.d_resid[...] = d_resid
    a.dbr_all[z] = d_resid.astype(bf16)
    for e in range(4):
        part = nt(a.dbr_all[z], whole(a.wo_all, e)).astype(bf16)
        for n in range(4):
            a.dmix[e, n // 2, n % 2] = part[64 * (n % 2) : 64 * (n % 2) + 64, 128 * (n // 2) : 128 * (n // 2) + 128]
    r_dm, r_dbr = net.slots(), net.slots()
    dm_s = net.s
    net.s += 1
    for d in (*Z_STEPS, 0):
        for n in range(4):
            owner = (n // 2) * 8 + lax.rem(z + z_at(d), 4) * 2 + n % 2
            src = a.dmix.at[d, n // 2, n % 2]
            copy = remote(src, a.dm.at[c], ssem.at[dm_s], rsem.at[r_dm], device(owner, z_at(d), k))
            if d:
                copy.start()
            else:

                @pl.when(owner == c)
                def _():
                    net.own(src, a.dm.at[c], r_dm)

                @pl.when(owner != c)
                def _():
                    copy.start()

    ffn = [shared[n] for n in ("gate", "up", "down_a", "down_b")]
    q_w, k_w, val, w_out = (shared[n] for n in ("q", "k", "v", "out"))
    for one in ffn[:2]:
        one.step1()
    net.landed(a.dm, r_dm)
    for one in ffn[2:]:
        one.step1()
    net.send([(a.dbr_all.at[z], a.dbr_all.at[z], z_peer(d)) for d in Z_STEPS], a.dbr_all.at[pl.ds(0, 3)], r_dbr)

    dm = a.dm[...].reshape(1024, 128)
    a.dk_a[...] = jnp.zeros((1024, 128), f32)
    a.dv_a[...] = jnp.zeros((1024, 128), f32)
    for b in range(16):
        a.read_adj[b] = tn(a.qa[b, 0:64], a.dm[b])
    d_pk = jnp.zeros((16, 128), f32)
    d_pv = jnp.zeros((16, 128), f32)
    adj_m = jnp.zeros((128, 128), f32)
    adj_v = jnp.zeros((128, 128), f32)
    for i in range(4):
        for b in range(15 - 4 * i, 11 - 4 * i, -1):
            total = adj_m + adj_v
            low = total.astype(bf16)
            a.adj[b] = low
            a.gf_rows[b : b + 1, :] = jnp.sum(adj_m * a.m0[b].astype(f32), axis=0, keepdims=True)
            a.gm_rows[b : b + 1, :] = jnp.sum(total * a.s0[b].astype(f32), axis=0, keepdims=True)
            adj_m = a.rate_f[b : b + 1, :] * adj_m - RATE * nn(a.qa[b, 64:192], low) + a.read_adj[b]
            adj_v = a.rate_m[b : b + 1, :] * total
        span = 256 * (i + 1)
        qs = slice(256 * i, span)
        p = a.probs[:span, qs]
        own_p = a.own[:, qs]
        dp = nt(v[:span], dm[qs])
        own_dp = nt(pv, dm[qs])
        pf, own_pf = p.astype(f32), own_p.astype(f32)
        delta = jnp.sum(pf * dp, axis=0, keepdims=True) + jnp.sum(
            own_pf * own_dp, axis=0, keepdims=True
        )
        d_s = (pf * (dp - delta)).astype(bf16)
        own_ds = (own_pf * (own_dp - delta)).astype(bf16)
        dq = tn(kk[:span], d_s) + tn(pk, own_ds)
        a.dq_a[qs, :] = dq.T * SCALE
        a.dk_a[:span, :] += nn(d_s, q[qs]) * SCALE
        a.dv_a[:span, :] += nn(p, dm[qs])
        d_pk += nn(own_ds, q[qs]) * SCALE
        d_pv += nn(own_p, dm[qs])
    a.d_own[0:16, :] = d_pk
    a.d_own[16:32, :] = d_pv

    r_dq, r_dkv = net.slots(), net.slots()
    spots = [at_ctx(c, dx, dy) for dx, dy in CTX_STEPS] + [c]
    dq_s = net.group(a.dqkv.at[pl.ds(0, 15), 0])
    dkv_s = net.group(a.dqkv.at[pl.ds(0, 15), pl.ds(1, 2)])

    def at_home(first, count):
        return a.dq_home.at[pl.ds(first, count), ds(zs * 2 + sb, 64), ds(hb, 128)]

    def send_home(n, b, first, count, r, s):
        src, dst = a.dqkv.at[b, pl.ds(first, count)], at_home(first, count)
        if n == 15:
            net.own(src, dst, r)
        else:
            net.send([(src, dst, device(b, z, k))], None, r, s)

    for b in range(16):
        qf = a.qkv[b, 0].astype(f32)
        d_qu = nt(a.dm[b], a.m0[b])
        rows = slice(64 * b, 64 * b + 64)
        a.dqkv[b, 0] = (a.dq_a[rows, :] + unit_back(qf, unit_rows(qf)[1], d_qu)).astype(bf16)
    for n, b in enumerate(spots):
        send_home(n, b, 0, 1, r_dq, dq_s)
    for one in ffn:
        one.step2()
    for b in range(16):
        rows = slice(64 * b, 64 * b + 64)
        total, k_l = a.adj[b], a.k_l[b]
        d_outer = (-RATE * nt(total, a.m0[b])).astype(bf16)
        kf = a.qkv[b, 1].astype(f32)
        got = nn(k_l, jnp.concatenate([d_outer, total], axis=1))
        d_kl = got[:, :128] + nt(k_l, d_outer) + RATE * nt(a.qkv[b, 2], total)
        a.dqkv[b, 1] = (a.dk_a[rows, :] + unit_back(kf, unit_rows(kf)[1], d_kl * live[rows])).astype(bf16)
        a.dqkv[b, 2] = (a.dv_a[rows, :] + RATE * got[:, 128:]).astype(bf16)
    for n, b in enumerate(spots):
        send_home(n, b, 1, 2, r_dkv, dkv_s)
    d_plan = []
    for rows, rate, pick in ((a.gf_rows, a.rate_f, decay_pick), (a.gm_rows, a.rate_m, moment_pick)):
        total = jnp.sum(rows[...], axis=1, keepdims=True) * rate[...] * (1.0 - rate[...])
        d_plan.append(jnp.sum(pick * total, axis=0, keepdims=True))
    d_decay, d_moment = d_plan

    r_gq, r_gkv, r_go, r_dn, r_sm = net.slots(), net.slots(), net.slots(), net.slots(), net.slots(4)

    def qkv_tile(n, half, first, count):
        return nn(a.n_t[2 * n + half], a.dq_l[:, 256 * first : 256 * (first + count)])

    for one in ffn:
        one.step3()
    for d in Z_STEPS:
        zz = z_at(-d)
        a.out_s[zz] = nn(a.hid_all[zz], a.wd_all[...]).astype(bf16)
    net.send(
        [(a.out_s.at[z_at(-d)], a.out_r.at[d - 1], z_peer(-d)) for d in Z_STEPS], a.out_s.at[pl.ds(0, 3)], r_out
    )
    net.landed(a.dq_home.at[0], r_dq)
    a.dq_l[:, 0:256] = a.dq_home[0]
    for n in range(4):
        a.gq_s[n, :, 0:256] = qkv_tile(n, 1 - k, 0, 1).astype(bf16)
    spot = pl.ds(0, 256)
    net.send([(a.gq_s.at[:, :, spot], a.gq_r.at[:, :, spot], sibling)], a.gq_s.at[:, :, spot], r_gq)

    def out_tile(half):
        return tn(a.mq[:, ds(half, 128)], all_rows(a.dbr_all))

    net.landed(a.dbr_all.at[pl.ds(0, 3)], r_dbr)
    net.landed(a.mixed, r_mq)
    a.go_s[...] = out_tile(1 - k).astype(bf16)
    net.send([(a.go_s, a.go_r, sibling)], a.go_s, r_go)
    for one in ffn:
        one.step4()
    net.landed(a.gq_r.at[:, :, spot], r_gq)
    for n in range(4):
        a.gq_1[n, :, 0:256] = (qkv_tile(n, k, 0, 1) + a.gq_r[n, :, 0:256].astype(f32)).astype(bf16)
    q_w.step1()

    net.landed(a.dq_home.at[pl.ds(1, 2)], r_dkv)
    for n in (1, 2):
        a.dq_l[:, 256 * n : 256 * n + 256] = a.dq_home[n]
    for n in range(4):
        a.gq_s[n, :, 256:768] = qkv_tile(n, 1 - k, 1, 2).astype(bf16)
    spot = pl.ds(256, 512)
    net.send([(a.gq_s.at[:, :, spot], a.gq_r.at[:, :, spot], sibling)], a.gq_s.at[:, :, spot], r_gkv)
    for one in ffn:
        one.step5()
    dn_s = net.group(a.dn_s.at[pl.ds(0, 3)])

    def dn_part(zz):
        for e in range(4):
            a.wide[:, ahead(e)] = nt(a.dq_l[ds(zz, 128), :], whole(a.w_all, e))
        part = a.wide[...]
        rows_f = a.x_all[zz].astype(f32)
        return part, jnp.sum(part * (rows_f * scaled(rows_f)), axis=0, keepdims=True)

    gain_grad = jnp.zeros((1, 1024), f32)

    def dn_send(d):
        part, gain = dn_part(z_at(-d))
        a.dn_s[z_at(-d)] = part.astype(bf16)
        net.send([(a.dn_s.at[z_at(-d)], a.dn_r.at[d - 1], z_peer(-d))], None, r_dn, dn_s)
        return gain

    gain_grad += dn_send(2)
    gain_grad += dn_send(1)
    net.landed(a.gq_r.at[:, :, spot], r_gkv)
    for n in range(4):
        a.gq_1[n, :, 256:768] = (qkv_tile(n, k, 1, 2) + a.gq_r[n, :, 256:768].astype(f32)).astype(bf16)
    k_w.step1()
    val.step1()
    gain_grad += dn_send(3)
    part, gain = dn_part(z)
    a.nf_own[...] = part
    gain_grad += gain
    for i in range(8):
        columns = slice(128 * i, 128 * i + 128)
        a.gains[i : i + 1, :] = gain_grad[:, columns]
        a.gains[8 + i : 9 + i, :] = a.nf_gain[:, columns]
    head_at = row8 == head
    a.keep[0:32, :] = jnp.where(hb == k, a.d_own[...], 0.0)
    a.give[0:32, :] = jnp.where(hb == k, 0.0, a.d_own[...])
    for ref in (a.keep, a.give):
        ref[32:48, :] = a.gains[...]
        ref[48:56, :] = jnp.where(head_at, d_decay, 0.0)
        ref[56:64, :] = jnp.where(head_at, d_moment, 0.0)
    net.send([(a.give, a.sm_s, sibling)], a.give, r_sm)
    net.landed(a.go_r, r_go)
    a.go_1[...] = (out_tile(k) + a.go_r[...].astype(f32)).astype(bf16)
    w_out.step1()
    q_w.step2()
    net.landed(a.sm_s, r_sm)
    a.sm_x[x_at] = a.keep[...] + a.sm_s[...]
    net.send(
        [(a.sm_x.at[x_at], a.sm_x.at[x_at], along("x", d)) for d in Z_STEPS], a.sm_x.at[pl.ds(0, 3)], r_sm + 1
    )

    k_w.step2()
    val.step2()
    out_sum = a.resid[...] + nn(a.hid_all[z], a.wd_all[...])
    net.landed(a.out_r, r_out)
    for d in range(3):
        out_sum += a.out_r[d].astype(f32)
    a.out_v[...] = out_sum.astype(bf16)
    done = [net.local(a.out_v, a.output)]
    net.landed(a.sm_x.at[pl.ds(0, 3)], r_sm + 1)
    a.sm_y[y_at] = a.sm_x[0] + a.sm_x[1] + a.sm_x[2] + a.sm_x[3]
    net.send(
        [(a.sm_y.at[y_at], a.sm_y.at[y_at], along("y", d)) for d in Z_STEPS], a.sm_y.at[pl.ds(0, 3)], r_sm + 2
    )
    for one in (q_w, k_w, val):
        one.step3()
    w_out.step2()
    net.landed(a.sm_y.at[pl.ds(0, 3)], r_sm + 2)
    plane = a.sm_y[0] + a.sm_y[1] + a.sm_y[2] + a.sm_y[3]
    a.small[0:32, :] = plane[0:32]
    a.sm_z[z] = plane[32:64]
    net.send([(a.sm_z.at[z], a.sm_z.at[z], z_peer(d)) for d in Z_STEPS], a.sm_z.at[pl.ds(0, 3)], r_sm + 3)
    for one in (q_w, k_w, val):
        one.step4()
    w_out.step3()
    w_out.step4()
    d_n = a.nf_own[...]
    net.landed(a.dn_r, r_dn)
    for d in range(3):
        d_n += a.dn_r[d].astype(f32)
    back, _ = norm_back(a.x[...].astype(f32), gain_one, d_n)
    a.d_resid[...] = a.d_resid[...] + back
    done.append(net.local(a.d_resid, a.input_grad))
    for one in (q_w, k_w, val, w_out):
        one.step5()
    net.landed(a.sm_z.at[pl.ds(0, 3)], r_sm + 3)
    a.small[32:64, :] = a.sm_z[0] + a.sm_z[1] + a.sm_z[2] + a.sm_z[3]
    for one in (*ffn, w_out, q_w, k_w, val):
        one.step6()
    for copy in done:
        copy.wait()
    net.drain()
    assert (net.s, net.r, net.l) == SEMS, (net.s, net.r, net.l)

    for slot, ref in ((home_s, a.mixed), (dm_s, a.dm)):

        @pl.when(same_plane)
        def _():
            size = ref.at[pl.ds(0, 15)]
            remote(size, size, ssem.at[slot], rsem.at[0], here).wait_send()

        @pl.when(jnp.logical_not(same_plane))
        def _():
            remote(ref, ref, ssem.at[slot], rsem.at[0], here).wait_send()


def finish_kernel(*refs):
    ins, outs = refs[:10], refs[10:25]
    buf_in, buf_out, sem_in, sem_out = refs[25:35], refs[35:48], refs[48], refs[49]
    c, z, k = coords()
    f = 2 * z + k
    loads = [pltpu.make_async_copy(ins[n], buf_in[n], sem_in.at[n]) for n in range(10)]
    for copy in (*loads[2:], *loads[:2]):
        copy.start()
    gate, up, q, kk, v, down, w_out, small = buf_in[2:]
    gain1, gq, gk, gv, go, pk, pv, gain2, gg, gu, gd, dec, mom = buf_out
    sent = []

    def store(*indices):
        for n in indices:
            copy = pltpu.make_async_copy(buf_out[n], outs[2 + n], sem_out.at[2 + n])
            copy.start()
            sent.append(copy)

    for at, (src, dst, n) in enumerate(((gate, gg, 8), (up, gu, 9))):
        loads[2 + at].wait()
        for m in range(4):
            dst[:, 704 * m : 704 * m + 704] = src[m, :, 0:704].astype(f32)
        store(n)
    for at, (src, dst, n) in enumerate(((q, gq, 1), (kk, gk, 2), (v, gv, 3))):
        loads[4 + at].wait()
        for m in range(4):
            dst[:, 256 * m : 256 * m + 256] = src[m].astype(f32)
        store(n)
    for at, (src, dst, n) in enumerate(((down, gd, 10), (w_out, go, 4))):
        loads[7 + at].wait()
        dst[...] = src[...].astype(f32)
        store(n)
    loads[9].wait()
    pk[...] = small[0:16, :]
    pv[...] = small[16:32, :]
    gain1[...] = small[pl.ds(32 + f, 1), :]
    gain2[...] = small[pl.ds(40 + f, 1), :]
    eye = lax.broadcasted_iota(jnp.int32, (8, 8), 0) == lax.broadcasted_iota(jnp.int32, (8, 8), 1)
    lane = lax.broadcasted_iota(jnp.int32, (8, 128), 1)
    for ref, at in ((dec, 48), (mom, 56)):
        for r in range(2):
            column = jnp.sum(jnp.where(lane == 2 * f + r, small[at : at + 8, :], 0.0), axis=1, keepdims=True)
            ref[r : r + 1, :] = jnp.sum(jnp.where(eye, column, 0.0), axis=0, keepdims=True)
    store(0, 5, 6, 7, 11, 12)
    for n in range(2):
        loads[n].wait()
        copy = pltpu.make_async_copy(buf_in[n], outs[n], sem_out.at[n])
        copy.start()
        sent.append(copy)
    for copy in sent:
        copy.wait()


def shards(
    inputs, gain_attn, w_query, w_key, w_value, w_out, persist_key, persist_value, gain_ffn,
    w_gate, w_up, w_down, decay_table, momentum_table, lengths, decay_index, momentum_index,
    cotangent,
):
    operands = dict(
        x=inputs.reshape(128, 1024), cot=cotangent.reshape(128, 1024),
        wq=w_query, wk=w_key, wv=w_value, wo=w_out, wg=w_gate, wu=w_up, wd=w_down,
        pk=persist_key, pv=persist_value, ga=gain_attn.reshape(1, 128), gf=gain_ffn.reshape(1, 128),
        dec=decay_table, mom=momentum_table, lens=lengths, didx=decay_index.reshape(2), midx=momentum_index.reshape(2),
    )
    far = {"cot", "wq", "wk", "wv", "wo", "wd", "wg", "wu"}
    scalars = {"lens", "didx", "midx"}

    def space(name):
        return pl.ANY if name in far else pltpu.SMEM if name in scalars else pltpu.VMEM

    near = {"small"}
    scratch = [pltpu.VMEM(shape, dtype) for shape, dtype in SCRATCH.values()]
    for zdim, block, piece in SHARED.values():
        scratch += shared_shapes(zdim, block, piece)
    scratch += [pltpu.SemaphoreType.DMA((n,)) for n in SEMS]
    scratch += [pltpu.SemaphoreType.REGULAR, pltpu.SemaphoreType.REGULAR]
    results = pl.pallas_call(
        layer_kernel,
        out_shape=[jax.ShapeDtypeStruct(s, t) for s, t in OUTPUTS.values()],
        in_specs=[pl.BlockSpec(memory_space=space(n)) for n in INPUTS],
        out_specs=[pl.BlockSpec(memory_space=pltpu.VMEM if n in near else pl.ANY) for n in OUTPUTS],
        scratch_shapes=scratch,
        compiler_params=pltpu.CompilerParams(
            collective_id=1, has_side_effects=True, vmem_limit_bytes=VMEM_LIMIT
        ),
        name="layer",
    )(*[operands[n] for n in INPUTS])
    shapes = [
        (1, 128), (128, 1024), (128, 1024), (128, 1024), (128, 1024), (16, 128), (16, 128), (1, 128),
        (128, 2816), (128, 2816), (352, 1024), (2, 8), (2, 8),
    ]
    far_away = pl.BlockSpec(memory_space=pl.ANY)
    output, input_grad, *grads = pl.pallas_call(
        finish_kernel,
        out_shape=[jax.ShapeDtypeStruct(*OUTPUTS[n]) for n in ("output", "input_grad")]
        + [jax.ShapeDtypeStruct(s, f32) for s in shapes],
        in_specs=[far_away] * 10,
        out_specs=[far_away] * 15,
        scratch_shapes=[pltpu.VMEM(*v) for v in OUTPUTS.values()]
        + [pltpu.VMEM(s, f32) for s in shapes]
        + [pltpu.SemaphoreType.DMA((10,)), pltpu.SemaphoreType.DMA((15,))],
        compiler_params=pltpu.CompilerParams(vmem_limit_bytes=VMEM_LIMIT),
        name="finish",
    )(*results)
    gain1, gq, gk, gv, go, pk, pv, gain2, gg, gu, gd, dec, mom = grads
    return (
        output.reshape(2, 64, 1024), input_grad.reshape(2, 64, 1024), gain1.reshape(128),
        gq, gk, gv, go, pk, pv, gain2.reshape(128), gg, gu, gd, dec, mom,
    )


def solution(mesh):
    rows, cols = P("fsdp", None), P(None, "fsdp")
    tokens = P("fsdp", "ctx", None)
    in_specs = (
        tokens, P("fsdp"), rows, rows, rows, rows, cols, cols, P("fsdp"), rows, rows, rows, rows, rows,
        P("fsdp"), P("fsdp", "ctx"), P("fsdp", "ctx"), tokens,
    )
    out_specs = (
        tokens, tokens, P("fsdp"), rows, rows, rows, rows, cols, cols, P("fsdp"), rows, rows, rows, rows, rows,
    )
    return jax.shard_map(shards, mesh=mesh, in_specs=in_specs, out_specs=out_specs, check_vma=False)
```

```python
import functools

import jax
import jax.numpy as jnp
from jax import lax
from jax.experimental import pallas as pl
from jax.experimental.pallas import tpu as pltpu
from jax.sharding import PartitionSpec as P

MESH = pl.DeviceIdType.MESH
HIGHEST = lax.Precision.HIGHEST
bf16, f32 = jnp.bfloat16, jnp.float32
EPS = 1e-06
RATE = 0.1
SCALE = 128**-0.5
VMEM_LIMIT = 63 << 20
SEMS = (84, 91, 22)


def coords():
    c, f = lax.axis_index("ctx"), lax.axis_index("fsdp")
    return c, lax.div(f, 2), lax.rem(f, 2)


def pair_of(c, z):
    return lax.div(c, 8), lax.rem(lax.div(c, 2) + 8 - z, 4), lax.rem(c, 2)


def at_ctx(c, dx, dy):
    x, y = lax.div(c, 4), lax.rem(c, 4)
    return lax.rem(x + dx, 4) * 4 + lax.rem(y + dy, 4)


CTX_STEPS = [(dx, dy) for dx in range(4) for dy in range(4) if dx or dy]
CTX_STEPS.sort(key=lambda s: -(min(s[0], 4 - s[0]) + min(s[1], 4 - s[1])))
Z_STEPS = (1, 3, 2)


def device(c, z, k):
    return (c, 2 * z + k)


def nn(a, b, precision=None):
    return jnp.dot(a, b, preferred_element_type=f32, precision=precision)


def nt(a, b, precision=None):
    return lax.dot_general(
        a, b, (((1,), (1,)), ((), ())), preferred_element_type=f32, precision=precision
    )


def tn(a, b, precision=None):
    return lax.dot_general(
        a, b, (((0,), (0,)), ((), ())), preferred_element_type=f32, precision=precision
    )


def ds(index, size):
    return pl.ds(pl.multiple_of(index * size, size), size)


def remote(src, dst, ssem, rsem, peer):
    return pltpu.make_async_remote_copy(
        src_ref=src, dst_ref=dst, send_sem=ssem, recv_sem=rsem, device_id=peer, device_id_type=MESH
    )


class Net:
    def __init__(self, ssem, rsem, lsem, here):
        self.ssem, self.rsem, self.lsem, self.here = ssem, rsem, lsem, here
        self.s = self.r = self.l = 0
        self.due = []

    def slots(self, n=1):
        self.r += n
        return self.r - n

    def send(self, moves, size, r, s=None):
        if s is None:
            s = self.group(size)
        for src, dst, peer, *own in moves:
            at = own[0] if own else r
            remote(src, dst, self.ssem.at[s], self.rsem.at[at], peer).start()
        return s

    def group(self, size):
        s = self.s
        self.s += 1
        self.due.append((size, s))
        return s

    def own(self, src, dst, r):
        pltpu.make_async_copy(src, dst, self.rsem.at[r]).start()

    def landed(self, size, r):
        remote(size, size, self.ssem.at[0], self.rsem.at[r], self.here).wait_recv()

    def local(self, src, dst):
        copy = pltpu.make_async_copy(src, dst, self.lsem.at[self.l])
        self.l += 1
        copy.start()
        return copy

    def drain(self, count=None):
        count = len(self.due) if count is None else count
        for size, s in self.due[:count]:
            remote(size, size, self.ssem.at[s], self.rsem.at[0], self.here).wait_send()
        self.due = self.due[count:]


def scaled(values):
    return lax.rsqrt(jnp.mean(values * values, axis=-1, keepdims=True) + EPS)


def norm_back(values, gain, grad):
    r = scaled(values)
    inner = grad * gain
    back = r * inner - (r * r * r) * values * jnp.mean(values * inner, axis=-1, keepdims=True)
    return back, jnp.sum(grad * values * r, axis=0, keepdims=True)


def unit_rows(rows):
    r = lax.rsqrt(jnp.mean(rows * rows, axis=-1, keepdims=True) + EPS)
    return rows * r * SCALE, r


def unit_back(rows, r, grad):
    return SCALE * (r * grad - rows * (r * r * r) * jnp.mean(rows * grad, axis=-1, keepdims=True))


class Shared:
    def __init__(self, net, first, zdim, part1, part2, src, r1, t1, r2, t2, zr, final):
        self.net, self.first, self.zdim = net, first, zdim
        self.part1, self.part2 = part1, part2
        self.src, self.r1, self.t1, self.r2, self.t2, self.zr, self.final = src, r1, t1, r2, t2, zr, final
        self.slot = net.slots(5)

    def place(self, c, z, k):
        x, y = lax.div(c, 4), lax.rem(c, 4)
        self.c, self.z, self.k = c, z, k
        self.i, self.j = (x, y) if self.first == "x" else (y, x)

    def peer(self, second, d):
        along_x = (self.first == "x") != second
        return device(at_ctx(self.c, d if along_x else 0, 0 if along_x else d), self.z, self.k)

    def step1(self):
        self.net.send(
            [
                (self.src.at[self.part1(lax.rem(self.i + d, 4))], self.r1.at[d - 1], self.peer(False, d))
                for d in (2, 1, 3)
            ],
            self.r1,
            self.slot,
        )

    def step2(self):
        self.net.landed(self.r1, self.slot)
        total = self.src[self.part1(self.i)].astype(f32)
        for d in range(3):
            total += self.r1[d].astype(f32)
        self.t1[...] = total.astype(bf16)
        self.net.send(
            [
                (self.t1.at[self.part2(lax.rem(self.j + d, 4))], self.r2.at[d - 1], self.peer(True, d))
                for d in (2, 1, 3)
            ],
            self.r2,
            self.slot + 1,
        )

    def step3(self):
        self.net.landed(self.r2, self.slot + 1)
        total = self.t1[self.part2(self.j)].astype(f32)
        for d in range(3):
            total += self.r2[d].astype(f32)
        self.t2[...] = total.astype(bf16)
        if self.zdim:
            self.zr[self.z] = self.t2[self.z]
            moves = []
            for d in (2, 1, 3):
                zz = lax.rem(self.z + d, 4)
                moves.append((self.t2.at[zz], self.zr.at[self.z], device(self.c, zz, self.k)))
            self.net.send(moves, self.zr.at[pl.ds(0, 3)], self.slot + 2)

    def block(self, i):
        return self.final.at[self.part1_final(i)]

    def piece(self, i, j):
        return self.final.at[self.piece_final(i, j)]

    def step4(self):
        if self.zdim:
            self.net.landed(self.zr.at[pl.ds(0, 3)], self.slot + 2)
        src = self.zr if self.zdim else self.t2
        spot = self.piece(self.i, self.j)
        self.mine = self.net.local(src, spot)
        self.net.send([(src, spot, self.peer(True, d)) for d in (2, 1, 3)], self.r2, self.slot + 3)

    def step5(self):
        self.mine.wait()
        self.net.landed(self.r2, self.slot + 3)
        spot = self.block(self.i)
        self.net.send([(spot, spot, self.peer(False, d)) for d in (2, 1, 3)], self.r1, self.slot + 4)

    def step6(self):
        self.net.landed(self.r1, self.slot + 4)


def shared_shapes(zdim, block, piece):
    lead = (4,) if zdim else ()
    return [
        pltpu.VMEM((3, *lead, *block), bf16),
        pltpu.VMEM((*lead, *block), bf16),
        pltpu.VMEM((3, *lead, *piece), bf16),
        pltpu.VMEM((*lead, *piece), bf16),
        pltpu.VMEM((*lead, *piece), bf16),
    ]


def wide_shared(net, first, column, width, src, scratch, final):
    half = width // 2
    shared = Shared(
        net,
        first,
        True,
        lambda i: (slice(None), ds(i, 32), pl.ds(column, width)),
        lambda j: (slice(None), ds(lax.div(j, 2), 16), ds(lax.rem(j, 2), half)),
        src,
        *scratch,
        final,
    )
    shared.part1_final = lambda i: (slice(None), ds(i, 32), slice(None))
    shared.piece_final = lambda i, j: (
        slice(None),
        ds(2 * i + lax.div(j, 2), 16),
        ds(lax.rem(j, 2), half),
    )
    return shared


def down_shared(net, first, row, rows, src, scratch, final):
    half = rows // 2
    shared = Shared(
        net,
        first,
        False,
        lambda i: (pl.ds(row, rows), ds(i, 256)),
        lambda j: (ds(lax.div(j, 2), half), ds(lax.rem(j, 2), 128)),
        src,
        *scratch,
        final,
    )
    shared.part1_final = shared.part1
    shared.piece_final = lambda i, j: (
        pl.ds(pl.multiple_of(row + lax.div(j, 2) * half, 16), half),
        ds(2 * i + lax.rem(j, 2), 128),
    )
    return shared


def out_shared(net, src, scratch, final):
    shared = Shared(
        net,
        "y",
        False,
        lambda i: (ds(i, 32), slice(None)),
        lambda j: (ds(lax.div(j, 2), 16), ds(lax.rem(j, 2), 512)),
        src,
        *scratch,
        final,
    )
    shared.part1_final = lambda i: (ds(i, 32), slice(None))
    shared.piece_final = lambda i, j: (ds(2 * i + lax.div(j, 2), 16), ds(lax.rem(j, 2), 512))
    return shared


class Weight:
    def __init__(self, net, buf, sources, c, z, k):
        self.net, self.buf, self.sources = net, buf, sources
        self.c, self.z, self.k = c, z, k
        self.half = buf.shape[-1] // 2
        self.slot = net.slots(6)

    def axes(self):
        for n, at in enumerate((lax.div(self.c, 4), lax.rem(self.c, 4))):
            yield n, ds(at, 32), pl.ds(n * self.half, self.half)

    def size(self, rows):
        return self.buf.at[pl.ds(1, 3), 0, pl.ds(0, rows), pl.ds(0, self.half)]

    def step0(self):
        net, k = self.net, self.k
        sibling = device(self.c, self.z, 1 - k)
        for n, rows, _ in self.axes():
            moves = []
            for d in Z_STEPS:
                zz = lax.rem(self.z + d, 4)
                for src, start, column, width in self.sources(zz):
                    if column // self.half == n:
                        spot = self.buf.at[4 - d, k, rows, pl.ds(column, width)]
                        moves.append((src.at[rows, pl.ds(start, width)], spot, device(self.c, zz, k)))
            net.send(moves, self.size(32), self.slot + n)
        self.mine = []
        moves = []
        for src, start, column, width in self.sources(self.z):
            block, spot = src.at[:, pl.ds(start, width)], self.buf.at[0, k, :, pl.ds(column, width)]
            self.mine.append(net.local(block, spot))
            moves.append((block, spot, sibling))
        net.send(moves, self.buf.at[0, k], self.slot + 4)

    def step1(self):
        for n, rows, columns in self.axes():
            self.net.landed(self.size(32), self.slot + n)
            spot = self.buf.at[pl.ds(1, 3), self.k, rows, columns]
            moves = []
            for d in (2, 1, 3):
                peer = device(at_ctx(self.c, 0 if n else d, d if n else 0), self.z, self.k)
                moves.append((spot, spot, peer))
            self.net.send(moves, self.size(96), self.slot + 2 + n)

    def step2(self):
        for n in range(2):
            self.net.landed(self.size(96), self.slot + 2 + n)
        spot = self.buf.at[pl.ds(1, 3), self.k]
        self.net.send([(spot, spot, device(self.c, self.z, 1 - self.k))], spot, self.slot + 5)

    def step3(self):
        for copy in self.mine:
            copy.wait()
        self.net.landed(self.buf.at[0, 0], self.slot + 4)
        self.net.landed(self.buf.at[pl.ds(1, 3), 0], self.slot + 5)


SHARED = dict(
    gate=(True, (32, 768), (16, 384)),
    up=(True, (32, 768), (16, 384)),
    q=(True, (32, 256), (16, 128)),
    k=(True, (32, 256), (16, 128)),
    v=(True, (32, 256), (16, 128)),
    down_a=(False, (192, 256), (96, 128)),
    down_b=(False, (160, 256), (80, 128)),
    out=(False, (32, 1024), (16, 512)),
)

SCRATCH = dict(
    meta=((4, 2, 24, 128), f32),
    plan=((4, 4, 4, 8, 128), f32),
    pers=((2, 2, 16, 128), bf16),
    x_all=((4, 128, 1024), bf16),
    cot_all=((4, 128, 1024), bf16),
    w_ffn=((2, 128, 2816), bf16),
    w_all=((4, 2, 128, 768), bf16),
    wo_all=((4, 2, 128, 1024), bf16),
    stage=((4, 128, 1536), bf16),
    wgu_all=((4, 2, 128, 1536), bf16),
    wide=((128, 1024), f32),
    wd_all=((768, 1024), bf16),
    n_all=((4, 128, 1024), bf16),
    n_t=((8, 128, 512), bf16),
    qkv_s=((3, 512, 256), bf16),
    qkv=((16, 3, 64, 128), bf16),
    probs=((1024, 1024), bf16),
    own=((16, 1024), bf16),
    m0=((16, 128, 128), bf16),
    s0=((16, 128, 128), bf16),
    qa=((16, 192, 128), bf16),
    outer=((16, 128, 128), f32),
    k_l=((16, 64, 128), bf16),
    bias=((1024, 128), f32),
    gf_rows=((16, 128), f32),
    gm_rows=((16, 128), f32),
    rate_f=((16, 128), f32),
    rate_m=((16, 128), f32),
    read_adj=((16, 128, 128), f32),
    reads=((1024, 128), f32),
    mixed=((16, 64, 128), bf16),
    mt=((128, 1024), bf16),
    mq=((512, 256), bf16),
    resid=((128, 1024), f32),
    nf_all=((4, 128, 1024), bf16),
    hid_all=((4, 128, 768), bf16),
    dh=((4, 128, 768), f32),
    dgu_all=((4, 128, 1536), bf16),
    od_all=((4, 128, 1024), bf16),
    nf_own=((128, 1024), f32),
    nf_s=((4, 128, 1024), bf16),
    nf_r=((3, 128, 1024), bf16),
    out_s=((4, 128, 1024), bf16),
    out_r=((3, 128, 1024), bf16),
    d_resid=((128, 1024), f32),
    out_v=((128, 1024), bf16),
    dbr_all=((4, 128, 1024), bf16),
    dmix=((4, 2, 2, 64, 128), bf16),
    dm=((16, 64, 128), bf16),
    dq_a=((1024, 128), f32),
    dk_a=((1024, 128), f32),
    dv_a=((1024, 128), f32),
    adj=((16, 128, 128), bf16),
    dqkv=((16, 3, 64, 128), bf16),
    dq_home=((3, 512, 256), bf16),
    dq_l=((512, 768), bf16),
    dn_s=((4, 128, 1024), bf16),
    dn_r=((3, 128, 1024), bf16),
    gu_r=((4, 128, 1536), bf16),
    nf_gain=((1, 1024), f32),
    gu_1=((4, 128, 1536), bf16),
    gd=((768, 1024), bf16),
    gd_r=((352, 1024), bf16),
    gd_1=((352, 1024), bf16),
    gq_s=((4, 128, 768), bf16),
    gq_r=((4, 128, 768), bf16),
    gq_1=((4, 128, 768), bf16),
    go_s=((128, 1024), bf16),
    go_r=((128, 1024), bf16),
    go_1=((128, 1024), bf16),
    gains=((16, 128), f32),
    tables=((16, 128), f32),
    d_own=((32, 128), f32),
    keep=((64, 128), f32),
    give=((64, 128), f32),
    sm_s=((64, 128), f32),
    sm_x=((4, 64, 128), f32),
    sm_y=((4, 64, 128), f32),
    sm_z=((4, 32, 128), f32),
)

INPUTS = [
    "x", "cot", "wq", "wk", "wv", "wo", "wg", "wu", "wd", "pk", "pv", "ga", "gf", "dec", "mom",
    "lens", "didx", "midx",
]
OUTPUTS = dict(
    output=((128, 1024), bf16),
    input_grad=((128, 1024), f32),
    f_gate=((4, 128, 768), bf16),
    f_up=((4, 128, 768), bf16),
    f_q=((4, 128, 256), bf16),
    f_k=((4, 128, 256), bf16),
    f_v=((4, 128, 256), bf16),
    f_down=((352, 1024), bf16),
    f_out=((128, 1024), bf16),
    small=((64, 128), f32),
)


class Refs:
    pass


def layer_kernel(*refs):
    names = INPUTS + list(OUTPUTS) + list(SCRATCH)
    a = Refs()
    for name, ref in zip(names, refs):
        setattr(a, name, ref)
    rest = refs[len(names) :]
    ssem, rsem, lsem, plane_sem, cube_sem = rest[-5:]
    c, z, k = coords()
    f = 2 * z + k
    hb, zs, sb = pair_of(c, z)
    x_at, y_at = lax.div(c, 4), lax.rem(c, 4)
    here, sibling = device(c, z, k), device(c, z, 1 - k)
    same_plane = zs == z
    net = Net(ssem, rsem, lsem, here)
    shared = {}
    sources = dict(
        gate=("x", 0, 768, a.gu_1, a.f_gate),
        up=("y", 768, 768, a.gu_1, a.f_up),
        q=("x", 0, 256, a.gq_1, a.f_q),
        k=("x", 256, 256, a.gq_1, a.f_k),
        v=("y", 512, 256, a.gq_1, a.f_v),
    )
    for n, name in enumerate(SHARED):
        scratch = rest[5 * n : 5 * n + 5]
        if name in sources:
            first, column, width, src, final = sources[name]
            shared[name] = wide_shared(net, first, column, width, src, scratch, final)
        elif name == "down_a":
            shared[name] = down_shared(net, "x", 0, 192, a.gd_1, scratch, a.f_down)
        elif name == "down_b":
            shared[name] = down_shared(net, "y", 192, 160, a.gd_1, scratch, a.f_down)
        else:
            shared[name] = out_shared(net, a.go_1, scratch, a.f_out)
        shared[name].place(c, z, k)

    def z_at(d):
        return lax.rem(z + d + 4, 4)

    def z_peer(d):
        return device(c, z_at(d), k)

    barrier = pltpu.get_barrier_semaphore()

    def along(axis, d):
        return device(at_ctx(c, d if axis == "x" else 0, 0 if axis == "x" else d), z, k)

    for d in Z_STEPS:
        for peer in (z_peer(d), along("x", d), along("y", d)):
            pl.semaphore_signal(barrier, inc=1, device_id=peer, device_id_type=MESH)
    pl.semaphore_signal(barrier, inc=1, device_id=sibling, device_id_type=MESH)

    into_ffn = [net.local(w, a.w_ffn.at[n]) for n, w in enumerate((a.wg, a.wu))]

    lane8 = lax.broadcasted_iota(jnp.int32, (8, 128), 1)
    row8 = lax.broadcasted_iota(jnp.int32, (8, 128), 0)
    eye8 = lax.broadcasted_iota(jnp.int32, (8, 8), 0) == lax.broadcasted_iota(jnp.int32, (8, 8), 1)

    def by_head(table):
        placed = jnp.zeros((8, 128), f32)
        for r in range(2):
            row = jnp.broadcast_to(table[r : r + 1, :].astype(f32), (8, 8))
            column = jnp.sum(jnp.where(eye8, row, 0.0), axis=1, keepdims=True)
            placed += jnp.where(lane8 == 2 * f + r, column, 0.0)
        return placed

    head_rows = jnp.where(row8 == 0, a.ga[...].astype(f32), 0.0)
    head_rows = jnp.where(row8 == 1, a.gf[...].astype(f32), head_rows)
    for n in range(2):
        head_rows = jnp.where(row8 == 2 + n, a.lens[n].astype(f32), head_rows)
    a.meta[z, k, 0:8, :] = head_rows
    a.meta[z, k, 8:16, :] = by_head(a.dec[...])
    a.meta[z, k, 16:24, :] = by_head(a.mom[...])
    plan = jnp.zeros((8, 128), f32)
    for n in range(2):
        plan = jnp.where(row8 == n, a.didx[n].astype(f32), plan)
        plan = jnp.where(row8 == 2 + n, a.midx[n].astype(f32), plan)
    a.plan[z, x_at, y_at] = plan
    a.pers[k, 0] = a.pk[...]
    a.pers[k, 1] = a.pv[...]
    a.x_all[z] = a.x[...]

    pl.semaphore_wait(barrier, 10)
    for d in Z_STEPS:
        pl.semaphore_signal(plane_sem, inc=1, device_id=along("y", d), device_id_type=MESH)

    r_meta, r_meta_s, r_x = net.slots(), net.slots(), net.slots(3)
    r_plan, r_pers, r_wd, r_cot = net.slots(3), net.slots(), net.slots(), net.slots()
    def from_qkv(zz):
        start = pl.multiple_of(zz * 256, 256)
        middle = pl.multiple_of(zz * 256 + 128, 128)
        return [
            (a.wq, start, 0, 256), (a.wk, start, 256, 128), (a.wk, middle, 384, 128), (a.wv, start, 512, 256),
        ]

    w_qkv = Weight(net, a.w_all, from_qkv, c, z, k)
    w_o = Weight(net, a.wo_all, lambda zz: [(a.wo, 0, 0, 512), (a.wo, 512, 512, 512)], c, z, k)
    w_gu = Weight(
        net, a.wgu_all, lambda zz: [(a.stage.at[zz], 0, 0, 768), (a.stage.at[zz], 768, 768, 768)], c, z, k
    )
    w_qkv.step0()
    spot = a.meta.at[z, k]
    net.send([(spot, spot, z_peer(d)) for d in Z_STEPS], a.meta.at[pl.ds(0, 3), 0], r_meta)
    spot = a.plan.at[z, x_at, y_at]
    net.send([(spot, spot, along("x", d)) for d in Z_STEPS], a.plan.at[0, 0, pl.ds(0, 3)], r_plan)
    w_qkv.step1()
    net.send(
        [(a.x_all.at[z], a.x_all.at[z], z_peer(d), r_x + d - 1) for d in Z_STEPS], a.x_all.at[pl.ds(0, 3)], None
    )
    w_o.step0()

    def stage_ffn(blocks):
        for n in blocks:
            for m in range(2):
                block = a.w_ffn[m, :, 704 * n : 704 * n + 704]
                a.stage[n, :, 768 * m : 768 * m + 768] = jnp.concatenate(
                    [block, jnp.zeros((128, 64), bf16)], axis=1
                )

    net.landed(a.meta.at[pl.ds(0, 3), 0], r_meta)
    spot = a.meta.at[:, k]
    net.send([(spot, spot, sibling)], spot, r_meta_s)
    net.landed(a.plan.at[0, 0, pl.ds(0, 3)], r_plan)
    spot = a.plan.at[z, :, y_at]
    net.send([(spot, spot, along("y", d)) for d in Z_STEPS], a.plan.at[0, pl.ds(0, 3)], r_plan + 1)
    w_qkv.step2()
    net.send([(a.pers.at[k], a.pers.at[k], sibling)], a.pers.at[0], r_pers)
    wd_rows = pl.ds(pl.multiple_of(k * 352, 32), 352)
    own_wd = net.local(a.wd, a.wd_all.at[wd_rows, :])
    net.send([(a.wd, a.wd_all.at[wd_rows, :], sibling)], a.gd_r, r_wd)
    a.wd_all[704:768, :] = jnp.zeros((64, 1024), bf16)
    pl.semaphore_wait(plane_sem, 3)
    for d in Z_STEPS:
        pl.semaphore_signal(cube_sem, inc=1, device_id=z_peer(d), device_id_type=MESH)
    net.landed(a.plan.at[0, pl.ds(0, 3)], r_plan + 1)
    net.send([(a.plan.at[z], a.plan.at[z], z_peer(d)) for d in Z_STEPS], a.plan.at[pl.ds(0, 3)], r_plan + 2)
    net.landed(a.meta.at[:, k], r_meta_s)

    def gain_row(n):
        return jnp.concatenate([a.meta[i // 2, i % 2, n : n + 1, :] for i in range(8)], axis=1)

    gain_one, gain_two = gain_row(0), gain_row(1)

    def ahead(e):
        return ds(z_at(e), 256)

    def whole(ref, e):
        return ref[e].reshape(256, ref.shape[-1])

    def norm_chunk(zz):
        xf = a.x_all[zz].astype(f32)
        a.n_all[zz] = (xf * scaled(xf) * gain_one).astype(bf16)

    norm_chunk(z)
    w_qkv.step3()
    for d in (0, *Z_STEPS):
        zz = z_at(-d)
        if d:
            net.landed(a.x_all.at[0], r_x + d - 1)
            norm_chunk(zz)
        rows = sum(nn(a.n_all[zz, :, ahead(e)], whole(a.w_all, e)) for e in range(4)).astype(bf16)
        for n in range(3):
            a.qkv_s[n, ds(zz, 128), :] = rows[:, 256 * n : 256 * n + 256]

    r_qkv = net.slots()

    def pair_block(ref, cc):
        hb2, zs2, sb2 = pair_of(cc, z)
        return ref.at[:, ds(zs2 * 2 + sb2, 64), ds(hb2, 128)]

    net.own(pair_block(a.qkv_s, c), a.qkv.at[c], r_qkv)
    net.send(
        [
            (pair_block(a.qkv_s, at_ctx(c, dx, dy)), a.qkv.at[c], device(at_ctx(c, dx, dy), z, k))
            for dx, dy in CTX_STEPS
        ],
        a.qkv.at[pl.ds(0, 15)],
        r_qkv,
    )

    w_o.step1()
    for copy in into_ffn:
        copy.wait()
    stage_ffn(range(4))
    w_gu.step0()
    own_cot = net.local(a.cot, a.cot_all.at[z])
    net.send([(a.cot, a.cot_all.at[z], z_peer(d)) for d in Z_STEPS], a.cot_all.at[pl.ds(0, 3)], r_cot)
    early = len(net.due)
    for i in range(8):
        a.n_t[i] = a.n_all[:, :, 128 * i : 128 * i + 128].reshape(512, 128).T

    net.landed(a.plan.at[pl.ds(0, 3)], r_plan + 2)
    net.landed(a.pers.at[0], r_pers)
    head = 2 * z + hb
    length = a.meta[zs, k, pl.ds(2 + sb, 1), :][:, :1]
    decay, moment = (sum(a.meta[i // 2, i % 2, pl.ds(at + head, 1), :] for i in range(8)) for at in (8, 16))
    lanes = lax.broadcasted_iota(jnp.int32, (16, 128), 1).astype(f32)
    decay_at = a.plan[zs, :, :, pl.ds(sb, 1), :].reshape(16, 128)
    moment_at = a.plan[zs, :, :, pl.ds(2 + sb, 1), :].reshape(16, 128)
    decay_pick = jnp.where(decay_at == lanes, 1.0, 0.0)
    moment_pick = jnp.where(moment_at == lanes, 1.0, 0.0)
    retention = jax.nn.sigmoid(jnp.sum(decay_pick * decay, axis=1, keepdims=True))
    momentum = jax.nn.sigmoid(jnp.sum(moment_pick * moment, axis=1, keepdims=True))
    a.rate_f[...] = jnp.broadcast_to(retention, (16, 128))
    a.rate_m[...] = jnp.broadcast_to(momentum, (16, 128))
    pk, pv = a.pers[hb, 0], a.pers[hb, 1]
    places = lax.broadcasted_iota(jnp.int32, (1024, 1), 0).astype(f32)
    live = jnp.where(places < length, 1.0, 0.0)
    a.bias[...] = jnp.broadcast_to(jnp.where(places < length, 0.0, -1e30), (1024, 128))
    early_late = lax.broadcasted_iota(jnp.int32, (256, 256), 0) <= lax.broadcasted_iota(jnp.int32, (256, 256), 1)

    net.landed(a.qkv, r_qkv)

    def rows_of(n):
        return a.qkv[:, n].reshape(1024, 128)

    q, kk, v = rows_of(0), rows_of(1), rows_of(2)
    a.qa[:, 0:64] = unit_rows(q.astype(f32))[0].astype(bf16).reshape(16, 64, 128)
    a.k_l[...] = (unit_rows(kk.astype(f32))[0] * live).astype(bf16).reshape(16, 64, 128)
    for b in range(16):
        got = tn(a.k_l[b], jnp.concatenate([a.k_l[b], a.qkv[b, 2]], axis=1))
        a.qa[b, 64:192] = got[:, :128].astype(bf16)
        a.outer[b] = got[:, 128:]
    w_gu.step1()
    pl.semaphore_wait(cube_sem, 3)
    r_home, r_mq = net.slots(), net.slots()
    home_s = net.s
    net.s += 1
    home_spot = a.mt.at[ds(sb, 64), ds(head, 128)]
    quart_spot = a.mq.at[ds(zs * 2 + sb, 64), ds(hb, 128)]

    def go_home(cc):
        return remote(a.mixed.at[cc], home_spot, ssem.at[home_s], rsem.at[r_home], device(cc, zs, k))

    memory = jnp.zeros((128, 128), f32)
    velocity = jnp.zeros((128, 128), f32)
    for i in range(4):
        for b in range(4 * i, 4 * i + 4):
            low = memory.astype(bf16)
            a.m0[b] = low
            a.s0[b] = velocity.astype(bf16)
            got = nn(a.qa[b], low)
            a.reads[64 * b : 64 * b + 64, :] = got[:64]
            velocity = a.rate_m[b : b + 1, :] * velocity - RATE * (got[64:] - a.outer[b])
            memory = a.rate_f[b : b + 1, :] * memory + velocity
        span = 256 * (i + 1)
        qs = slice(256 * i, span)
        scores = nt(kk[:span], q[qs]) * SCALE + jnp.concatenate([a.bias[:span, :]] * 2, axis=1)
        last = jnp.where(early_late, scores[256 * i :], -1e30)
        scores = jnp.concatenate([scores[: 256 * i], last], axis=0) if i else last
        own_scores = nt(pk, q[qs]) * SCALE
        top = jnp.maximum(
            jnp.max(scores, axis=0, keepdims=True), jnp.max(own_scores, axis=0, keepdims=True)
        )
        e = jnp.exp(scores - top)
        own_e = jnp.exp(own_scores - top)
        total = jnp.sum(e, axis=0, keepdims=True) + jnp.sum(own_e, axis=0, keepdims=True)
        share = 1.0 / total
        p = (e * share).astype(bf16)
        own_p = (own_e * share).astype(bf16)
        a.probs[:span, qs] = p
        a.own[:, qs] = own_p
        att = tn(v[:span], p) + tn(pv, own_p)
        a.mixed[4 * i : 4 * i + 4] = (att.T + a.reads[qs, :]).astype(bf16).reshape(4, 64, 128)
        for row in (i - 1, i) if i % 2 else ():
            for dy in range(4):
                cc = 4 * row + lax.rem(y_at + dy, 4)
                if dy:
                    go_home(cc).start()
                else:
                    stays = same_plane & (x_at == row)

                    @pl.when(stays)
                    def _():
                        net.own(a.mixed.at[cc], home_spot, r_home)

                    @pl.when(jnp.logical_not(stays))
                    def _():
                        go_home(cc).start()

        if i == 1:
            w_o.step2()

    w_o.step3()
    net.landed(a.mt, r_home)
    r_nf = net.slots(3)
    xf = a.x[...].astype(f32)
    resid = xf + sum(nn(a.mt[:, ahead(e)], whole(a.wo_all, e)) for e in range(4))
    a.resid[...] = resid
    a.nf_all[z] = (resid * scaled(resid) * gain_two).astype(bf16)
    net.send(
        [(a.nf_all.at[z], a.nf_all.at[z], z_peer(d), r_nf + d - 1) for d in (2, 1, 3)],
        a.nf_all.at[pl.ds(0, 3)],
        None,
    )
    net.own(a.mixed.at[c], quart_spot, r_mq)
    net.send(
        [
            (a.mixed.at[at_ctx(c, dx, dy)], quart_spot, device(at_ctx(c, dx, dy), z, k))
            for dx, dy in CTX_STEPS
        ],
        a.mixed.at[pl.ds(0, 15)],
        r_mq,
    )
    w_gu.step2()
    own_wd.wait()
    own_cot.wait()
    w_gu.step3()
    net.landed(a.gd_r, r_wd)

    def live_chunk(zz):
        at = (lax.broadcasted_iota(jnp.int32, (64, 1), 0) + c * 64).astype(f32)
        return jnp.concatenate(
            [jnp.where(at < a.meta[zz, k, 2 + n : 3 + n, :][:, :1], 1.0, 0.0) for n in range(2)], axis=0
        )

    net.landed(a.cot_all.at[pl.ds(0, 3)], r_cot)
    for zz in range(4):
        od = (a.cot_all[zz].astype(f32) * live_chunk(zz)).astype(bf16)
        a.od_all[zz] = od
    a.dh[...] = nt(a.od_all[...].reshape(512, 1024), a.wd_all[...]).reshape(4, 128, 768)
    r_nfp, r_out = net.slots(), net.slots()
    nfp_s = net.group(a.nf_s.at[pl.ds(0, 3)])
    for group in ((0,), (2,), (1, 3)):
        places = [z_at(-d) for d in group]
        for d in group:
            if d:
                net.landed(a.nf_all.at[0], r_nf + d - 1)

        def stacked(read):
            parts = [read(zz) for zz in places]
            return jnp.concatenate(parts, axis=0) if len(parts) > 1 else parts[0]

        gu = sum(nn(stacked(lambda zz: a.nf_all[zz, :, ahead(e)]), whole(a.wgu_all, e)) for e in range(4))
        dh = stacked(lambda zz: a.dh[zz])
        g, u = gu[:, :768], gu[:, 768:]
        s = jax.nn.sigmoid(g)
        gs = g * s
        hidden = (gs * u).astype(bf16)
        d_gu = jnp.concatenate(
            [(dh * u * (s + gs * (1.0 - s))).astype(bf16), (dh * gs).astype(bf16)], axis=1
        )
        for n, zz in enumerate(places):
            a.hid_all[zz] = hidden[128 * n : 128 * n + 128]
            a.dgu_all[zz] = d_gu[128 * n : 128 * n + 128]
        for e in range(4):
            part = nt(d_gu, whole(a.wgu_all, e))
            for n, d in enumerate(group):
                if d:
                    a.nf_s[places[n], :, ahead(e)] = part[128 * n : 128 * n + 128].astype(bf16)
                else:
                    a.nf_own[:, ahead(e)] = part
        for n, d in enumerate(group):
            if d:
                net.send([(a.nf_s.at[places[n]], a.nf_r.at[d - 1], z_peer(-d))], None, r_nfp, nfp_s)

    r_gu_c, r_gd_c = net.slots(), net.slots()
    net.drain(early)

    def all_rows(ref):
        return ref[...].reshape(512, ref.shape[-1])

    def gu_tile(n, half):
        return tn(a.nf_all[:, :, ds(2 * n + half, 128)].reshape(512, 128), all_rows(a.dgu_all))

    for n in range(4):
        a.stage[n] = gu_tile(n, 1 - k).astype(bf16)
    net.send([(a.stage, a.gu_r, sibling)], a.stage, r_gu_c)
    a.gd[...] = tn(all_rows(a.hid_all), all_rows(a.od_all)).astype(bf16)
    my_rows = pl.ds(pl.multiple_of(k * 352, 32), 352)
    their_rows = pl.ds(pl.multiple_of((1 - k) * 352, 32), 352)
    net.send([(a.gd.at[their_rows, :], a.gd_r, sibling)], a.gd_r, r_gd_c)

    net.landed(a.gu_r, r_gu_c)
    for n in range(4):
        a.gu_1[n] = (gu_tile(n, k) + a.gu_r[n].astype(f32)).astype(bf16)
    net.landed(a.gd_r, r_gd_c)
    a.gd_1[...] = (a.gd[my_rows, :].astype(f32) + a.gd_r[...].astype(f32)).astype(bf16)

    d_nf = a.nf_own[...]
    net.landed(a.nf_r, r_nfp)
    for d in range(3):
        d_nf += a.nf_r[d].astype(f32)
    back, nf_gain = norm_back(a.resid[...], gain_two, d_nf)
    a.nf_gain[...] = nf_gain
    d_resid = a.od_all[z].astype(f32) + back
    a.d_resid[...] = d_resid
    a.dbr_all[z] = d_resid.astype(bf16)
    for e in range(4):
        part = nt(a.dbr_all[z], whole(a.wo_all, e)).astype(bf16)
        for n in range(4):
            a.dmix[e, n // 2, n % 2] = part[64 * (n % 2) : 64 * (n % 2) + 64, 128 * (n // 2) : 128 * (n // 2) + 128]
    r_dm, r_dbr = net.slots(), net.slots()
    dm_s = net.s
    net.s += 1
    for d in (*Z_STEPS, 0):
        for n in range(4):
            owner = (n // 2) * 8 + lax.rem(z + z_at(d), 4) * 2 + n % 2
            src = a.dmix.at[d, n // 2, n % 2]
            copy = remote(src, a.dm.at[c], ssem.at[dm_s], rsem.at[r_dm], device(owner, z_at(d), k))
            if d:
                copy.start()
            else:

                @pl.when(owner == c)
                def _():
                    net.own(src, a.dm.at[c], r_dm)

                @pl.when(owner != c)
                def _():
                    copy.start()

    ffn = [shared[n] for n in ("gate", "up", "down_a", "down_b")]
    q_w, k_w, val, w_out = (shared[n] for n in ("q", "k", "v", "out"))
    for one in ffn[:2]:
        one.step1()
    net.landed(a.dm, r_dm)
    for one in ffn[2:]:
        one.step1()
    net.send([(a.dbr_all.at[z], a.dbr_all.at[z], z_peer(d)) for d in Z_STEPS], a.dbr_all.at[pl.ds(0, 3)], r_dbr)

    dm = a.dm[...].reshape(1024, 128)
    a.dk_a[...] = jnp.zeros((1024, 128), f32)
    a.dv_a[...] = jnp.zeros((1024, 128), f32)
    for b in range(16):
        a.read_adj[b] = tn(a.qa[b, 0:64], a.dm[b])
    d_pk = jnp.zeros((16, 128), f32)
    d_pv = jnp.zeros((16, 128), f32)
    adj_m = jnp.zeros((128, 128), f32)
    adj_v = jnp.zeros((128, 128), f32)
    for i in range(4):
        for b in range(15 - 4 * i, 11 - 4 * i, -1):
            total = adj_m + adj_v
            low = total.astype(bf16)
            a.adj[b] = low
            a.gf_rows[b : b + 1, :] = jnp.sum(adj_m * a.m0[b].astype(f32), axis=0, keepdims=True)
            a.gm_rows[b : b + 1, :] = jnp.sum(total * a.s0[b].astype(f32), axis=0, keepdims=True)
            adj_m = a.rate_f[b : b + 1, :] * adj_m - RATE * nn(a.qa[b, 64:192], low) + a.read_adj[b]
            adj_v = a.rate_m[b : b + 1, :] * total
        span = 256 * (i + 1)
        qs = slice(256 * i, span)
        p = a.probs[:span, qs]
        own_p = a.own[:, qs]
        dp = nt(v[:span], dm[qs])
        own_dp = nt(pv, dm[qs])
        pf, own_pf = p.astype(f32), own_p.astype(f32)
        delta = jnp.sum(pf * dp, axis=0, keepdims=True) + jnp.sum(
            own_pf * own_dp, axis=0, keepdims=True
        )
        d_s = (pf * (dp - delta)).astype(bf16)
        own_ds = (own_pf * (own_dp - delta)).astype(bf16)
        dq = tn(kk[:span], d_s) + tn(pk, own_ds)
        a.dq_a[qs, :] = dq.T * SCALE
        a.dk_a[:span, :] += nn(d_s, q[qs]) * SCALE
        a.dv_a[:span, :] += nn(p, dm[qs])
        d_pk += nn(own_ds, q[qs]) * SCALE
        d_pv += nn(own_p, dm[qs])
    a.d_own[0:16, :] = d_pk
    a.d_own[16:32, :] = d_pv

    r_dq, r_dkv = net.slots(), net.slots()
    spots = [at_ctx(c, dx, dy) for dx, dy in CTX_STEPS] + [c]
    dq_s = net.group(a.dqkv.at[pl.ds(0, 15), 0])
    dkv_s = net.group(a.dqkv.at[pl.ds(0, 15), pl.ds(1, 2)])

    def at_home(first, count):
        return a.dq_home.at[pl.ds(first, count), ds(zs * 2 + sb, 64), ds(hb, 128)]

    def send_home(n, b, first, count, r, s):
        src, dst = a.dqkv.at[b, pl.ds(first, count)], at_home(first, count)
        if n == 15:
            net.own(src, dst, r)
        else:
            net.send([(src, dst, device(b, z, k))], None, r, s)

    for b in range(16):
        qf = a.qkv[b, 0].astype(f32)
        d_qu = nt(a.dm[b], a.m0[b])
        rows = slice(64 * b, 64 * b + 64)
        a.dqkv[b, 0] = (a.dq_a[rows, :] + unit_back(qf, unit_rows(qf)[1], d_qu)).astype(bf16)
    for n, b in enumerate(spots):
        send_home(n, b, 0, 1, r_dq, dq_s)
    for one in ffn:
        one.step2()
    for b in range(16):
        rows = slice(64 * b, 64 * b + 64)
        total, k_l = a.adj[b], a.k_l[b]
        d_outer = (-RATE * nt(total, a.m0[b])).astype(bf16)
        kf = a.qkv[b, 1].astype(f32)
        got = nn(k_l, jnp.concatenate([d_outer, total], axis=1))
        d_kl = got[:, :128] + nt(k_l, d_outer) + RATE * nt(a.qkv[b, 2], total)
        a.dqkv[b, 1] = (a.dk_a[rows, :] + unit_back(kf, unit_rows(kf)[1], d_kl * live[rows])).astype(bf16)
        a.dqkv[b, 2] = (a.dv_a[rows, :] + RATE * got[:, 128:]).astype(bf16)
    for n, b in enumerate(spots):
        send_home(n, b, 1, 2, r_dkv, dkv_s)
    d_plan = []
    for rows, rate, pick in ((a.gf_rows, a.rate_f, decay_pick), (a.gm_rows, a.rate_m, moment_pick)):
        total = jnp.sum(rows[...], axis=1, keepdims=True) * rate[...] * (1.0 - rate[...])
        d_plan.append(jnp.sum(pick * total, axis=0, keepdims=True))
    d_decay, d_moment = d_plan

    r_gq, r_gkv, r_go, r_dn, r_sm = net.slots(), net.slots(), net.slots(), net.slots(), net.slots(4)

    def qkv_tile(n, half, first, count):
        return nn(a.n_t[2 * n + half], a.dq_l[:, 256 * first : 256 * (first + count)])

    for one in ffn:
        one.step3()
    for d in Z_STEPS:
        zz = z_at(-d)
        a.out_s[zz] = nn(a.hid_all[zz], a.wd_all[...]).astype(bf16)
    net.send(
        [(a.out_s.at[z_at(-d)], a.out_r.at[d - 1], z_peer(-d)) for d in Z_STEPS], a.out_s.at[pl.ds(0, 3)], r_out
    )
    net.landed(a.dq_home.at[0], r_dq)
    a.dq_l[:, 0:256] = a.dq_home[0]
    for n in range(4):
        a.gq_s[n, :, 0:256] = qkv_tile(n, 1 - k, 0, 1).astype(bf16)
    spot = pl.ds(0, 256)
    net.send([(a.gq_s.at[:, :, spot], a.gq_r.at[:, :, spot], sibling)], a.gq_s.at[:, :, spot], r_gq)

    def out_tile(half):
        return tn(a.mq[:, ds(half, 128)], all_rows(a.dbr_all))

    net.landed(a.dbr_all.at[pl.ds(0, 3)], r_dbr)
    net.landed(a.mixed, r_mq)
    a.go_s[...] = out_tile(1 - k).astype(bf16)
    net.send([(a.go_s, a.go_r, sibling)], a.go_s, r_go)
    for one in ffn:
        one.step4()
    net.landed(a.gq_r.at[:, :, spot], r_gq)
    for n in range(4):
        a.gq_1[n, :, 0:256] = (qkv_tile(n, k, 0, 1) + a.gq_r[n, :, 0:256].astype(f32)).astype(bf16)
    q_w.step1()

    net.landed(a.dq_home.at[pl.ds(1, 2)], r_dkv)
    for n in (1, 2):
        a.dq_l[:, 256 * n : 256 * n + 256] = a.dq_home[n]
    for n in range(4):
        a.gq_s[n, :, 256:768] = qkv_tile(n, 1 - k, 1, 2).astype(bf16)
    spot = pl.ds(256, 512)
    net.send([(a.gq_s.at[:, :, spot], a.gq_r.at[:, :, spot], sibling)], a.gq_s.at[:, :, spot], r_gkv)
    for one in ffn:
        one.step5()
    dn_s = net.group(a.dn_s.at[pl.ds(0, 3)])

    def dn_part(zz):
        for e in range(4):
            a.wide[:, ahead(e)] = nt(a.dq_l[ds(zz, 128), :], whole(a.w_all, e))
        part = a.wide[...]
        rows_f = a.x_all[zz].astype(f32)
        return part, jnp.sum(part * (rows_f * scaled(rows_f)), axis=0, keepdims=True)

    gain_grad = jnp.zeros((1, 1024), f32)

    def dn_send(d):
        part, gain = dn_part(z_at(-d))
        a.dn_s[z_at(-d)] = part.astype(bf16)
        net.send([(a.dn_s.at[z_at(-d)], a.dn_r.at[d - 1], z_peer(-d))], None, r_dn, dn_s)
        return gain

    gain_grad += dn_send(2)
    gain_grad += dn_send(1)
    net.landed(a.gq_r.at[:, :, spot], r_gkv)
    for n in range(4):
        a.gq_1[n, :, 256:768] = (qkv_tile(n, k, 1, 2) + a.gq_r[n, :, 256:768].astype(f32)).astype(bf16)
    k_w.step1()
    val.step1()
    gain_grad += dn_send(3)
    part, gain = dn_part(z)
    a.nf_own[...] = part
    gain_grad += gain
    for i in range(8):
        columns = slice(128 * i, 128 * i + 128)
        a.gains[i : i + 1, :] = gain_grad[:, columns]
        a.gains[8 + i : 9 + i, :] = a.nf_gain[:, columns]
    head_at = row8 == head
    a.keep[0:32, :] = jnp.where(hb == k, a.d_own[...], 0.0)
    a.give[0:32, :] = jnp.where(hb == k, 0.0, a.d_own[...])
    for ref in (a.keep, a.give):
        ref[32:48, :] = a.gains[...]
        ref[48:56, :] = jnp.where(head_at, d_decay, 0.0)
        ref[56:64, :] = jnp.where(head_at, d_moment, 0.0)
    net.send([(a.give, a.sm_s, sibling)], a.give, r_sm)
    net.landed(a.go_r, r_go)
    a.go_1[...] = (out_tile(k) + a.go_r[...].astype(f32)).astype(bf16)
    w_out.step1()
    q_w.step2()
    net.landed(a.sm_s, r_sm)
    a.sm_x[x_at] = a.keep[...] + a.sm_s[...]
    net.send(
        [(a.sm_x.at[x_at], a.sm_x.at[x_at], along("x", d)) for d in Z_STEPS], a.sm_x.at[pl.ds(0, 3)], r_sm + 1
    )

    k_w.step2()
    val.step2()
    out_sum = a.resid[...] + nn(a.hid_all[z], a.wd_all[...])
    net.landed(a.out_r, r_out)
    for d in range(3):
        out_sum += a.out_r[d].astype(f32)
    a.out_v[...] = out_sum.astype(bf16)
    done = [net.local(a.out_v, a.output)]
    net.landed(a.sm_x.at[pl.ds(0, 3)], r_sm + 1)
    a.sm_y[y_at] = a.sm_x[0] + a.sm_x[1] + a.sm_x[2] + a.sm_x[3]
    net.send(
        [(a.sm_y.at[y_at], a.sm_y.at[y_at], along("y", d)) for d in Z_STEPS], a.sm_y.at[pl.ds(0, 3)], r_sm + 2
    )
    for one in (q_w, k_w, val):
        one.step3()
    w_out.step2()
    net.landed(a.sm_y.at[pl.ds(0, 3)], r_sm + 2)
    plane = a.sm_y[0] + a.sm_y[1] + a.sm_y[2] + a.sm_y[3]
    a.small[0:32, :] = plane[0:32]
    a.sm_z[z] = plane[32:64]
    net.send([(a.sm_z.at[z], a.sm_z.at[z], z_peer(d)) for d in Z_STEPS], a.sm_z.at[pl.ds(0, 3)], r_sm + 3)
    for one in (q_w, k_w, val):
        one.step4()
    w_out.step3()
    w_out.step4()
    d_n = a.nf_own[...]
    net.landed(a.dn_r, r_dn)
    for d in range(3):
        d_n += a.dn_r[d].astype(f32)
    back, _ = norm_back(a.x[...].astype(f32), gain_one, d_n)
    a.d_resid[...] = a.d_resid[...] + back
    done.append(net.local(a.d_resid, a.input_grad))
    for one in (q_w, k_w, val, w_out):
        one.step5()
    net.landed(a.sm_z.at[pl.ds(0, 3)], r_sm + 3)
    a.small[32:64, :] = a.sm_z[0] + a.sm_z[1] + a.sm_z[2] + a.sm_z[3]
    for one in (*ffn, w_out, q_w, k_w, val):
        one.step6()
    for copy in done:
        copy.wait()
    net.drain()
    assert (net.s, net.r, net.l) == SEMS, (net.s, net.r, net.l)

    for slot, ref in ((home_s, a.mixed), (dm_s, a.dm)):

        @pl.when(same_plane)
        def _():
            size = ref.at[pl.ds(0, 15)]
            remote(size, size, ssem.at[slot], rsem.at[0], here).wait_send()

        @pl.when(jnp.logical_not(same_plane))
        def _():
            remote(ref, ref, ssem.at[slot], rsem.at[0], here).wait_send()


def finish_kernel(*refs):
    ins, outs = refs[:10], refs[10:25]
    buf_in, buf_out, sem_in, sem_out = refs[25:35], refs[35:48], refs[48], refs[49]
    c, z, k = coords()
    f = 2 * z + k
    loads = [pltpu.make_async_copy(ins[n], buf_in[n], sem_in.at[n]) for n in range(10)]
    for copy in (*loads[2:], *loads[:2]):
        copy.start()
    gate, up, q, kk, v, down, w_out, small = buf_in[2:]
    gain1, gq, gk, gv, go, pk, pv, gain2, gg, gu, gd, dec, mom = buf_out
    sent = []

    def store(*indices):
        for n in indices:
            copy = pltpu.make_async_copy(buf_out[n], outs[2 + n], sem_out.at[2 + n])
            copy.start()
            sent.append(copy)

    for at, (src, dst, n) in enumerate(((gate, gg, 8), (up, gu, 9))):
        loads[2 + at].wait()
        for m in range(4):
            dst[:, 704 * m : 704 * m + 704] = src[m, :, 0:704].astype(f32)
        store(n)
    for at, (src, dst, n) in enumerate(((q, gq, 1), (kk, gk, 2), (v, gv, 3))):
        loads[4 + at].wait()
        for m in range(4):
            dst[:, 256 * m : 256 * m + 256] = src[m].astype(f32)
        store(n)
    for at, (src, dst, n) in enumerate(((down, gd, 10), (w_out, go, 4))):
        loads[7 + at].wait()
        dst[...] = src[...].astype(f32)
        store(n)
    loads[9].wait()
    pk[...] = small[0:16, :]
    pv[...] = small[16:32, :]
    gain1[...] = small[pl.ds(32 + f, 1), :]
    gain2[...] = small[pl.ds(40 + f, 1), :]
    eye = lax.broadcasted_iota(jnp.int32, (8, 8), 0) == lax.broadcasted_iota(jnp.int32, (8, 8), 1)
    lane = lax.broadcasted_iota(jnp.int32, (8, 128), 1)
    for ref, at in ((dec, 48), (mom, 56)):
        for r in range(2):
            column = jnp.sum(jnp.where(lane == 2 * f + r, small[at : at + 8, :], 0.0), axis=1, keepdims=True)
            ref[r : r + 1, :] = jnp.sum(jnp.where(eye, column, 0.0), axis=0, keepdims=True)
    store(0, 5, 6, 7, 11, 12)
    for n in range(2):
        loads[n].wait()
        copy = pltpu.make_async_copy(buf_in[n], outs[n], sem_out.at[n])
        copy.start()
        sent.append(copy)
    for copy in sent:
        copy.wait()


def shards(
    inputs, gain_attn, w_query, w_key, w_value, w_out, persist_key, persist_value, gain_ffn,
    w_gate, w_up, w_down, decay_table, momentum_table, lengths, decay_index, momentum_index,
    cotangent,
):
    operands = dict(
        x=inputs.reshape(128, 1024), cot=cotangent.reshape(128, 1024),
        wq=w_query, wk=w_key, wv=w_value, wo=w_out, wg=w_gate, wu=w_up, wd=w_down,
        pk=persist_key, pv=persist_value, ga=gain_attn.reshape(1, 128), gf=gain_ffn.reshape(1, 128),
        dec=decay_table, mom=momentum_table, lens=lengths, didx=decay_index.reshape(2), midx=momentum_index.reshape(2),
    )
    far = {"cot", "wq", "wk", "wv", "wo", "wd", "wg", "wu"}
    scalars = {"lens", "didx", "midx"}

    def space(name):
        return pl.ANY if name in far else pltpu.SMEM if name in scalars else pltpu.VMEM

    near = {"small"}
    scratch = [pltpu.VMEM(shape, dtype) for shape, dtype in SCRATCH.values()]
    for zdim, block, piece in SHARED.values():
        scratch += shared_shapes(zdim, block, piece)
    scratch += [pltpu.SemaphoreType.DMA((n,)) for n in SEMS]
    scratch += [pltpu.SemaphoreType.REGULAR, pltpu.SemaphoreType.REGULAR]
    results = pl.pallas_call(
        layer_kernel,
        out_shape=[jax.ShapeDtypeStruct(s, t) for s, t in OUTPUTS.values()],
        in_specs=[pl.BlockSpec(memory_space=space(n)) for n in INPUTS],
        out_specs=[pl.BlockSpec(memory_space=pltpu.VMEM if n in near else pl.ANY) for n in OUTPUTS],
        scratch_shapes=scratch,
        compiler_params=pltpu.CompilerParams(
            collective_id=1, has_side_effects=True, vmem_limit_bytes=VMEM_LIMIT
        ),
        name="layer",
    )(*[operands[n] for n in INPUTS])
    shapes = [
        (1, 128), (128, 1024), (128, 1024), (128, 1024), (128, 1024), (16, 128), (16, 128), (1, 128),
        (128, 2816), (128, 2816), (352, 1024), (2, 8), (2, 8),
    ]
    far_away = pl.BlockSpec(memory_space=pl.ANY)
    output, input_grad, *grads = pl.pallas_call(
        finish_kernel,
        out_shape=[jax.ShapeDtypeStruct(*OUTPUTS[n]) for n in ("output", "input_grad")]
        + [jax.ShapeDtypeStruct(s, f32) for s in shapes],
        in_specs=[far_away] * 10,
        out_specs=[far_away] * 15,
        scratch_shapes=[pltpu.VMEM(*v) for v in OUTPUTS.values()]
        + [pltpu.VMEM(s, f32) for s in shapes]
        + [pltpu.SemaphoreType.DMA((10,)), pltpu.SemaphoreType.DMA((15,))],
        compiler_params=pltpu.CompilerParams(vmem_limit_bytes=VMEM_LIMIT),
        name="finish",
    )(*results)
    gain1, gq, gk, gv, go, pk, pv, gain2, gg, gu, gd, dec, mom = grads
    return (
        output.reshape(2, 64, 1024), input_grad.reshape(2, 64, 1024), gain1.reshape(128),
        gq, gk, gv, go, pk, pv, gain2.reshape(128), gg, gu, gd, dec, mom,
    )


def solution(mesh):
    rows, cols = P("fsdp", None), P(None, "fsdp")
    tokens = P("fsdp", "ctx", None)
    in_specs = (
        tokens, P("fsdp"), rows, rows, rows, rows, cols, cols, P("fsdp"), rows, rows, rows, rows, rows,
        P("fsdp"), P("fsdp", "ctx"), P("fsdp", "ctx"), tokens,
    )
    out_specs = (
        tokens, tokens, P("fsdp"), rows, rows, rows, rows, cols, cols, P("fsdp"), rows, rows, rows, rows, rows,
    )
    return jax.shard_map(shards, mesh=mesh, in_specs=in_specs, out_specs=out_specs, check_vma=False)
```
